32 devices in a mesh: dp: 16 (over z, y, x), seq: 2 (over core).
Axes of the slice: x: 2, y: 2, z: 4, core: 2. Of those that a mesh axis runs over, the one named last changes fastest.
Arguments:
- dec_input: bfloat16 [48, 128, 768], P('dp'), may hold values from -6 to 6
- enc_states: bfloat16 [48, 656, 768], P('dp', 'seq'), may hold values from -6 to 6
- dec_lengths: int32 [48], P('dp'), may hold values from 32 to 128, as said below
- enc_lengths: int32 [48], P('dp'), may hold values from 358 to 656, as said below
- rel_buckets: int32 [48, 128, 128], P('dp'), may hold values from 0 to 31
- out_grad: bfloat16 [48, 128, 768], P('dp'), may hold values from -6 to 6
- gain_self: float32 [768], replicated, may hold values from 0.5 to 1.5
- gain_cross: float32 [768], replicated, may hold values from 0.5 to 1.5
- gain_ffn: float32 [768], replicated, may hold values from 0.5 to 1.5
- rel_table: float32 [32, 12], P(None, 'seq'), may hold values from -4 to 4
- self_query: bfloat16 [768, 768], P(None, 'seq'), may hold values from -0.21875 to 0.21875
- self_key: bfloat16 [768, 768], P(None, 'seq'), may hold values from -0.21875 to 0.21875
- self_value: bfloat16 [768, 768], P(None, 'seq'), may hold values from -0.21875 to 0.21875
- self_out: bfloat16 [768, 768], P('seq'), may hold values from -1 to 1
- cross_query: bfloat16 [768, 768], P(None, 'seq'), may hold values from -0.21875 to 0.21875
- cross_key: bfloat16 [768, 768], P(None, 'seq'), may hold values from -0.21875 to 0.21875
- cross_value: bfloat16 [768, 768], P(None, 'seq'), may hold values from -0.21875 to 0.21875
- cross_out: bfloat16 [768, 768], P('seq'), may hold values from -4 to 4
- ffn_in: bfloat16 [768, 3072], P(None, 'seq'), may hold values from -0.21875 to 0.21875
- ffn_out: bfloat16 [3072, 768], P('seq'), may hold values from -0.109375 to 0.109375
Outputs:
- layer_out: bfloat16 [48, 128, 768], P('dp')
- input_grad: float32 [48, 128, 768], P('dp')
- enc_grad: bfloat16 [48, 656, 768], P('dp', 'seq')
- gain_self_grad: float32 [768], replicated
- gain_cross_grad: float32 [768], replicated
- gain_ffn_grad: float32 [768], replicated
- table_grad: float32 [32, 12], P(None, 'seq')
- self_query_grad: float32 [768, 768], P(None, 'seq')
- self_key_grad: float32 [768, 768], P(None, 'seq')
- self_value_grad: float32 [768, 768], P(None, 'seq')
- self_out_grad: float32 [768, 768], P('seq')
- cross_query_grad: float32 [768, 768], P(None, 'seq')
- cross_key_grad: float32 [768, 768], P(None, 'seq')
- cross_value_grad: float32 [768, 768], P(None, 'seq')
- cross_out_grad: float32 [768, 768], P('seq')
- ffn_in_grad: float32 [768, 3072], P(None, 'seq')
- ffn_out_grad: float32 [3072, 768], P('seq')
The draws below stay inside these ranges and needn't reach their ends.
Inputs may be any that keep to these rules, and one draw needn't show every extreme that they name: `dec_lengths`: some document has all 128 decoder tokens and some exactly 32. `enc_lengths`: each length is 656 (high resolution) or 656 * 59 // 108 (low resolution); each aligned block of 3 documents holds both.
All inputs are finite; a program needn't handle non-finite values.
Results may differ from the reference program's by a relative error of at most 0.02.
The reference program's roundings to bfloat16 on the way count: a program that leaves them out, or rounds other values in their place, can miss the bound.
Values may be sent and summed in bfloat16 or wider, within the bound.
No kernel may reach another device: no remote copies, remote signals or barrier semaphores. Data moves between devices by JAX's collectives and lax.ppermute only.
A program may use at most 192 MiB of HBM per device.

```python
import jax
import jax.numpy as jnp
from jax import lax

D = 768
H = 12
DH = 64
FF = 3072
NB = 32
DEC = 128
B_DEV = 3
B = 48
ENC = 656


def draw_dec_lengths(key, part):
    key = jax.random.fold_in(key, 11)
    draw_one, draw_two = jax.random.split(key)
    lengths = jax.random.randint(draw_one, (B,), DEC // 4, DEC + 1)
    ordering = jax.random.permutation(draw_two, B)
    lengths = lengths.at[ordering[0]].set(DEC)
    lengths = lengths.at[ordering[1]].set(DEC // 4)
    return lengths.astype(jnp.int32)


def draw_enc_lengths(key, part):
    key = jax.random.fold_in(key, 23)
    draw_one, draw_two = jax.random.split(key)
    blocks = B // B_DEV
    levels = jax.random.randint(draw_one, (blocks, B_DEV), 0, 2)
    picked = jax.random.randint(draw_two, (blocks, 1), 0, B_DEV)
    columns = jnp.arange(B_DEV, dtype=jnp.int32)[None, :]
    levels = jnp.where(columns == picked, 1, levels)
    levels = jnp.where(columns == (picked + 1) % B_DEV, 0, levels)
    short_len = ENC * 59 // 108
    return jnp.where(levels == 1, ENC, short_len).reshape(B).astype(jnp.int32)


def plant(values, own_key, smallest, largest):
    longest = values.shape.index(max(values.shape))
    spots = []
    for shift in (0, 1):
        where = [jax.random.randint(jax.random.fold_in(own_key, axis), (), 0, length) for axis, length in enumerate(values.shape)]
        where[longest] = (where[longest] + shift) % values.shape[longest]
        spots.append(tuple(where))
    return values.at[spots[0]].set(smallest).at[spots[1]].set(largest)


def block_levels(key, extent, shards, least, high):
    def one(position, shards_of):
        steps = jax.random.uniform(jax.random.fold_in(jax.random.fold_in(key, 6), position), (shards_of,), jnp.float32, least / len(shards), high / len(shards))
        return jnp.repeat(jnp.exp(steps), extent[position] // shards_of).reshape((-1,) + (1,) * (len(extent) - position - 1))

    level = one(*shards[0])
    for cut in shards[1:]:
        level = level * one(*cut)
    return level


def gaussian(stream_key, shape, spread, reach, cuts=(), kind=jnp.bfloat16):
    result = jax.random.normal(stream_key, shape, jnp.float32) * spread
    if len(cuts) > 0:
        result = block_levels(stream_key, shape, cuts, -0.22, 0.18) * result
    return jnp.clip(result, min=-reach, max=reach).astype(kind)


def setup_inputs(seed: int = 0) -> dict:
    splits = jax.random.split(jax.random.key(seed), 21)
    dec_input = gaussian(splits[0], (B, DEC, D), 1.0, 6.0, ((0, 16),))
    enc_states = gaussian(splits[1], (B, ENC, D), 1.0, 6.0, ((0, 16), (1, 2)))
    dec_lengths = draw_dec_lengths(jax.random.fold_in(splits[20], 71), 0)
    enc_lengths = draw_enc_lengths(jax.random.fold_in(splits[20], 71), 0)
    rel_buckets = plant(jax.random.randint(splits[4], (B, DEC, DEC), 0, NB), jax.random.fold_in(splits[4], 1), 0, NB - 1).astype(jnp.int32)
    out_grad = gaussian(splits[5], (B, DEC, D), 1.0, 6.0, ((0, 16),))
    gain_self = jnp.clip(1.0 + 0.1 * jax.random.normal(splits[6], (D,), jnp.float32), 0.5, 1.5)
    gain_cross = jnp.clip(1.0 + 0.1 * jax.random.normal(splits[7], (D,), jnp.float32), 0.5, 1.5)
    gain_ffn = jnp.clip(1.0 + 0.1 * jax.random.normal(splits[8], (D,), jnp.float32), 0.5, 1.5)
    rel_table = gaussian(splits[9], (NB, H), 1.0, 4.0, ((1, 2),), jnp.float32)
    self_query = gaussian(splits[10], (D, D), D ** -0.5, 0.21875, ((1, 2),))
    self_key = gaussian(splits[11], (D, D), D ** -0.5, 0.21875, ((1, 2),))
    self_value = gaussian(splits[12], (D, D), D ** -0.5, 0.21875, ((1, 2),))
    self_out = gaussian(splits[13], (D, D), (D // 24) ** -0.5, 1.0, ((0, 2),))
    cross_query = gaussian(splits[14], (D, D), D ** -0.5, 0.21875, ((1, 2),))
    cross_key = gaussian(splits[15], (D, D), D ** -0.5, 0.21875, ((1, 2),))
    cross_value = gaussian(splits[16], (D, D), D ** -0.5, 0.21875, ((1, 2),))
    cross_out = gaussian(splits[17], (D, D), (max(D // 384, 2)) ** -0.5, 4.0, ((0, 2),))
    ffn_in = gaussian(splits[18], (D, FF), D ** -0.5, 0.21875, ((1, 2),))
    ffn_out = gaussian(splits[19], (FF, D), FF ** -0.5, 0.109375, ((0, 2),))
    return {"dec_input": dec_input, "enc_states": enc_states, "dec_lengths": dec_lengths, "enc_lengths": enc_lengths, "rel_buckets": rel_buckets, "out_grad": out_grad, "gain_self": gain_self, "gain_cross": gain_cross, "gain_ffn": gain_ffn, "rel_table": rel_table, "self_query": self_query, "self_key": self_key, "self_value": self_value, "self_out": self_out, "cross_query": cross_query, "cross_key": cross_key, "cross_value": cross_value, "cross_out": cross_out, "ffn_in": ffn_in, "ffn_out": ffn_out}


EPSILON = 1e-06
MASKED = -1e+30
HIGHEST = lax.Precision.HIGHEST

@jax.custom_vjp
def low(v):
    return lax.optimization_barrier(v.astype(jnp.bfloat16)).astype(jnp.float32)

@jax.custom_vjp
def low_back(v):
    return v

def low_keep(v):
    return (low(v), None)

def low_pass(kept, grad):
    return (grad,)

def back_keep(v):
    return (v, None)

def back_low(kept, grad):
    return (low(grad),)
low.defvjp(low_keep, low_pass)
low_back.defvjp(back_keep, back_low)

def rms_norm(values, scale_gain):
    return values * lax.rsqrt(lax.optimization_barrier(jnp.mean(values * values, axis=-1, keepdims=True)) + EPSILON) * scale_gain

def product(left_side, right_side):
    return jnp.matmul(left_side, right_side, precision=HIGHEST)

def heads_of(tensor):
    return tensor.reshape(tensor.shape[0], H, DH)

def attend(scores, allowed, values):
    scores = jnp.where(allowed[None], low_back(scores), MASKED)
    row_max = lax.optimization_barrier(jnp.max(scores, axis=-1, keepdims=True))
    exp_scores = jnp.exp(scores - row_max)
    attn_probs = exp_scores / lax.optimization_barrier(jnp.sum(exp_scores, axis=-1, keepdims=True))
    context = jnp.einsum('hij,jhd->ihd', low(attn_probs), values, precision=HIGHEST)
    return low_back(low(context)).reshape(context.shape[0], -1)

def decoder_layer(params, inputs, encoded, dec_len, enc_len, buckets):
    gain_self, gain_cross, gain_ffn, rel_table, self_query, self_key, self_value, self_out, cross_query, cross_key, cross_value, cross_out, ffn_in, ffn_out = params
    score_scale = DH ** (-0.5)
    normed = low(rms_norm(inputs, gain_self))
    queries = heads_of(low_back(low(product(normed, self_query))))
    key_heads = heads_of(low_back(low(product(normed, self_key))))
    values = heads_of(low_back(low(product(normed, self_value))))
    onehot = (buckets[:, :, None] == jnp.arange(NB, dtype=jnp.int32)[None, None, :]).astype(jnp.float32)
    rel_bias = jnp.einsum('ijn,nh->hij', onehot, rel_table, precision=HIGHEST)
    scores = jnp.einsum('ihd,jhd->hij', queries, key_heads, precision=HIGHEST) * score_scale + rel_bias
    positions = jnp.arange(DEC, dtype=jnp.int32)
    allowed = (positions[None, :] <= positions[:, None]) & (positions[None, :] < dec_len)
    after_self = inputs + low_back(product(attend(scores, allowed, values), self_out))
    normed = low(rms_norm(after_self, gain_cross))
    queries = heads_of(low_back(low(product(normed, cross_query))))
    key_heads = heads_of(low_back(low(product(encoded, cross_key))))
    values = heads_of(low_back(low(product(encoded, cross_value))))
    scores = jnp.einsum('ihd,jhd->hij', queries, key_heads, precision=HIGHEST) * score_scale
    key_pos = jnp.arange(ENC, dtype=jnp.int32)
    allowed = jnp.broadcast_to(key_pos[None, :] < enc_len, (DEC, ENC))
    after_cross = after_self + low_back(product(attend(scores, allowed, values), cross_out))
    normed = low(rms_norm(after_cross, gain_ffn))
    hidden = low_back(product(normed, ffn_in))
    activated = low(jax.nn.gelu(hidden))
    return after_cross + low_back(product(activated, ffn_out))

def reference(dec_input, enc_states, dec_lengths, enc_lengths, rel_buckets, out_grad, gain_self, gain_cross, gain_ffn, rel_table, self_query, self_key, self_value, self_out, cross_query, cross_key, cross_value, cross_out, ffn_in, ffn_out):
    params = tuple((weight_array.astype(jnp.float32) for weight_array in (gain_self, gain_cross, gain_ffn, rel_table, self_query, self_key, self_value, self_out, cross_query, cross_key, cross_value, cross_out, ffn_in, ffn_out)))

    def per_document(running, document):
        dec_row, enc_row, dec_len, enc_len, bucket_row, grad_row = document

        def forward(weights, inputs, encoded):
            return decoder_layer(weights, inputs, encoded, dec_len, enc_len, bucket_row)
        output, pullback = jax.vjp(forward, params, dec_row.astype(jnp.float32), enc_row.astype(jnp.float32))
        param_grads, inputs_grad, encoded_grad = pullback(grad_row.astype(jnp.float32))
        running = jax.tree.map(lambda left_side, right_side: left_side + right_side, running, param_grads)
        return (running, (output.astype(jnp.bfloat16), inputs_grad, encoded_grad.astype(jnp.bfloat16)))
    zero_grads = tuple((jnp.zeros(weight_array.shape, jnp.float32) for weight_array in params))
    totals, (layer_out, input_grad, enc_grad) = lax.scan(per_document, zero_grads, (dec_input, enc_states, dec_lengths, enc_lengths, rel_buckets, out_grad))
    return (layer_out, input_grad, enc_grad, totals[0], totals[1], totals[2], totals[3], totals[4], totals[5], totals[6], totals[7], totals[8], totals[9], totals[10], totals[11], totals[12], totals[13])
```

```python
import functools

import jax
import jax.numpy as jnp
from jax import lax
from jax.experimental import pallas as pl
from jax.experimental.pallas import tpu as pltpu
from jax.sharding import PartitionSpec as P

DH = 64
NB = 32
PAIR = 2 * DH
EPSILON = 1e-06
MASKED = -1e30
F32 = jnp.float32
BF16 = jnp.bfloat16
MIB = 1024 * 1024


def dot(a, b):
    return lax.dot_general(a, b, (((1,), (0,)), ((), ())), preferred_element_type=F32)


def dot_nt(a, b):
    return lax.dot_general(a, b, (((1,), (1,)), ((), ())), preferred_element_type=F32)


def dot_tn(a, b):
    return lax.dot_general(a, b, (((0,), (0,)), ((), ())), preferred_element_type=F32)


VMEM = pl.BlockSpec(memory_space=pltpu.VMEM)
SMEM = pl.BlockSpec(memory_space=pltpu.SMEM)
ANY = pl.BlockSpec(memory_space=pl.ANY)


def kernel(body, name, outs, ins, after=(), smem=0, out_specs=None, in_specs=None, scratch=()):
    n_in, n_after = len(ins), len(after)

    def wrapped(*refs):
        body(*refs[:n_in], *refs[n_in + n_after :])

    in_specs = list(in_specs) if in_specs is not None else [SMEM] * smem + [VMEM] * (n_in - smem)
    return pl.pallas_call(
        wrapped,
        name=name,
        out_shape=[jax.ShapeDtypeStruct(s, t) for s, t in outs],
        in_specs=in_specs + [ANY] * n_after,
        out_specs=list(out_specs) if out_specs is not None else [VMEM] * len(outs),
        scratch_shapes=list(scratch),
        compiler_params=pltpu.CompilerParams(vmem_limit_bytes=56 * MIB),
        cost_estimate=pl.CostEstimate(flops=0, bytes_accessed=0, transcendentals=0),
    )(*ins, *after)


def inverse_rms(values):
    return lax.rsqrt(jnp.mean(values * values, axis=-1, keepdims=True) + EPSILON)


def rms_backward(values, gain, grad):
    inverse = inverse_rms(values)
    scaled = grad * gain
    inner = jnp.mean(scaled * values, axis=-1, keepdims=True)
    grad_in = inverse * scaled - values * (inverse * inverse * inverse * inner)
    return grad_in, jnp.sum(grad * values * inverse, axis=0, keepdims=True)


def lane_masks():
    lanes = lax.broadcasted_iota(jnp.int32, (1, PAIR), 1)
    low = (lanes < DH).astype(F32)
    return low.astype(BF16), (1.0 - low).astype(BF16)


def stack_pair(pair, scale=1.0):
    low, high = lane_masks()
    s = jnp.asarray(scale, BF16)
    return jnp.concatenate([pair * (low * s), pair * (high * s)], axis=0)


def join_pair(stacked):
    half = stacked.shape[0] // 2
    lanes = lax.broadcasted_iota(jnp.int32, (half, PAIR), 1)
    return jnp.where(lanes < DH, stacked[:half], stacked[half:])


def soft(scores):
    top = functools.reduce(jnp.maximum, [jnp.max(s, axis=-1, keepdims=True) for s in scores])
    exps = [jnp.exp(s - top) for s in scores]
    total = functools.reduce(jnp.add, [jnp.sum(e, axis=-1, keepdims=True) for e in exps])
    inv = 1.0 / total
    return [e * inv for e in exps]


def attend(q2, keys, values, biases, masks):
    probs = soft(
        [
            jnp.where(m, dot_nt(q2, k) if b is None else dot_nt(q2, k) + b, MASKED)
            for k, b, m in zip(keys, biases, masks)
        ]
    )
    return functools.reduce(jnp.add, [dot(p.astype(BF16), v) for p, v in zip(probs, values)])


def attend_back(q2, do2, keys, values, biases, masks):
    probs = soft(
        [
            jnp.where(m, dot_nt(q2, k) if b is None else dot_nt(q2, k) + b, MASKED)
            for k, b, m in zip(keys, biases, masks)
        ]
    )
    dv = [dot_tn(p.astype(BF16), do2).astype(BF16) for p in probs]
    dp = [dot_nt(do2, v) for v in values]
    row = functools.reduce(
        jnp.add, [jnp.sum(p * g, axis=-1, keepdims=True) for p, g in zip(probs, dp)]
    )
    ds = [(p * (g - row)).astype(BF16) for p, g in zip(probs, dp)]
    dq = functools.reduce(jnp.add, [dot(s, k) for s, k in zip(ds, keys)])
    dk = [dot_tn(s, q2).astype(BF16) for s in ds]
    return dq, ds, dk, dv


def self_mask(length, size):
    rows = lax.broadcasted_iota(jnp.int32, (size, size), 0)
    cols = lax.broadcasted_iota(jnp.int32, (size, size), 1)
    one = (cols <= rows) & (cols < length)
    return jnp.concatenate([one, one], axis=0)


def pair_bias(table, buckets, pair):
    size = buckets.shape[0]
    rows = []
    for head in (2 * pair, 2 * pair + 1):
        line = jnp.broadcast_to(table[head : head + 1, :], (size, table.shape[1]))
        rows.append(jnp.take_along_axis(line, buckets, axis=1, mode="promise_in_bounds"))
    return jnp.concatenate(rows, axis=0)


def self_forward(lens, x, gain, wq, wk, wv, buckets, table, h_o, q_o, k_o, v_o, o_o):
    docs, size = buckets.shape[0], buckets.shape[1]
    xf = x[...].astype(F32)
    h = (xf * inverse_rms(xf) * gain[...]).astype(BF16)
    h_o[...] = h
    q_o[...] = dot(h, wq[...]).astype(BF16)
    k_o[...] = dot(h, wk[...]).astype(BF16)
    v_o[...] = dot(h, wv[...]).astype(BF16)
    tab = table[...]
    for d in range(docs):
        rows = slice(d * size, (d + 1) * size)
        mask = self_mask(lens[d], size)
        index = buckets[d]
        for p in range(wq.shape[1] // PAIR):
            cols = slice(p * PAIR, (p + 1) * PAIR)
            q2 = stack_pair(q_o[rows, cols], DH**-0.5)
            bias = pair_bias(tab, index, p)
            out = attend(q2, [k_o[rows, cols]], [v_o[rows, cols]], [bias], [mask])
            o_o[rows, cols] = join_pair(out).astype(BF16)


def project_kv(e, wk, wv, kv_o):
    n = wk.shape[1]
    for d in range(e.shape[0]):
        tokens = e[d]
        kv_o[d, :, :n] = dot(tokens, wk[...]).astype(BF16)
        kv_o[d, :, n:] = dot(tokens, wv[...]).astype(BF16)


def cross_masks(length, core, size, half):
    out = []
    for part in (core, 1 - core):
        pos = lax.broadcasted_iota(jnp.int32, (2 * size, half), 1) + part * half
        out.append(pos < length)
    return out


def cross_forward(meta, lens, x, o_own, o_oth, wo_own, wo_oth, gain, wq, kv_own, kv_oth, x1_o, h_o, q_o, o_o):
    docs, half, n = kv_own.shape[0], kv_own.shape[1], wq.shape[1]
    size = x.shape[0] // docs
    x1 = x[...].astype(F32) + (dot(o_own[...], wo_own[...]) + dot(o_oth[...], wo_oth[...]))
    x1_o[...] = x1
    h = (x1 * inverse_rms(x1) * gain[...]).astype(BF16)
    h_o[...] = h
    q_o[...] = dot(h, wq[...]).astype(BF16)
    for d in range(docs):
        rows = slice(d * size, (d + 1) * size)
        masks = cross_masks(lens[d], meta[2], size, half)
        for p in range(n // PAIR):
            cols = slice(p * PAIR, (p + 1) * PAIR)
            vals = slice(n + p * PAIR, n + (p + 1) * PAIR)
            q2 = stack_pair(q_o[rows, cols], DH**-0.5)
            out = attend(
                q2,
                [kv_own[d, :, cols], kv_oth[d, :, cols]],
                [kv_own[d, :, vals], kv_oth[d, :, vals]],
                [None, None],
                masks,
            )
            o_o[rows, cols] = join_pair(out).astype(BF16)


GELU_C = 0.7978845608028654
GELU_A = 0.044715


def ffn_grads(meta, x1, o_own, o_oth, wo_own, wo_oth, gain, win, wout, dy, x2_o, h_o, z_o, du_o, ak, as_, bk, bs):
    quad, zq = meta[0], meta[1]
    x2 = x1[...] + (dot(o_own[...], wo_own[...]) + dot(o_oth[...], wo_oth[...]))
    x2_o[...] = x2
    h = (x2 * inverse_rms(x2) * gain[...]).astype(BF16)
    h_o[...] = h
    h_t = h.T
    dyv = dy[...]
    block = win.shape[1] // 4
    for s in range(4):
        off = pl.multiple_of((quad ^ s) * block, 128)
        u = dot(h, win[:, pl.ds(off, block)])
        inner = GELU_C * (u + GELU_A * (u * u * u))
        t = jnp.tanh(inner)
        z = (0.5 * u * (1.0 + t)).astype(BF16)
        dz = dot_nt(dyv, wout[pl.ds(off, block), :])
        slope = 0.5 * (1.0 + t) + 0.5 * u * (1.0 - t * t) * (GELU_C * (1.0 + 3.0 * GELU_A * (u * u)))
        du = (dz * slope).astype(BF16)
        z_o[s] = z
        du_o[s] = du
        out_grad = dot_tn(z, dyv).astype(BF16)
        in_grad = dot(h_t, du).astype(BF16)
        a_ref, a_at = (ak, s // 2) if s % 2 == 0 else (as_, s // 2)
        b_ref, b_at = (bk, s % 2) if s < 2 else (bs, s % 2)
        ra, rb = out_grad.shape[0] // 4, in_grad.shape[0] // 4
        for az in range(4):
            a_ref[a_at, zq ^ az] = out_grad[az * ra : (az + 1) * ra]
            b_ref[b_at, zq ^ az] = in_grad[az * rb : (az + 1) * rb]


def ffn_rest(meta, z, du, win, wout, part_o):
    quad = meta[0]
    block = win.shape[1] // 4
    rows = z.shape[1]
    branch = grad = 0.0
    for s in range(4):
        off = pl.multiple_of((quad ^ s) * block, 128)
        branch = branch + dot(z[s], wout[pl.ds(off, block), :])
        grad = grad + dot_nt(du[s], win[:, pl.ds(off, block)])
    part_o[:rows] = branch.astype(BF16)
    part_o[rows:] = grad.astype(BF16)


def cross_backward(meta, lens, x2, p_own, p_oth, gain, dy, wo, q, kv_own, kv_oth, y_o, gain_o, dx2_o, dc_o, dq_o, dkv_own, dkv_oth):
    docs, half, n = kv_own.shape[0], kv_own.shape[1], q.shape[1]
    rows_all = x2.shape[0]
    size = rows_all // docs
    both = p_own[...].astype(F32) + p_oth[...].astype(F32)
    x2v = x2[...]
    y_o[...] = (x2v + both[:rows_all]).astype(BF16)
    dv, gain_grad = rms_backward(x2v, gain[...], both[rows_all:])
    gain_o[...] = gain_grad
    dx2 = dy[...].astype(F32) + dv
    dx2_o[...] = dx2
    dc = dx2.astype(BF16)
    dc_o[...] = dc
    do = dot_nt(dc, wo[...]).astype(BF16)
    for d in range(docs):
        rows = slice(d * size, (d + 1) * size)
        masks = cross_masks(lens[d], meta[2], size, half)
        for p in range(n // PAIR):
            cols = slice(p * PAIR, (p + 1) * PAIR)
            vals = slice(n + p * PAIR, n + (p + 1) * PAIR)
            q2 = stack_pair(q[rows, cols], DH**-0.5)
            do2 = stack_pair(do[rows, cols])
            dq, _, dk, dv = attend_back(
                q2,
                do2,
                [kv_own[d, :, cols], kv_oth[d, :, cols]],
                [kv_own[d, :, vals], kv_oth[d, :, vals]],
                [None, None],
                masks,
            )
            dq_o[rows, cols] = (join_pair(dq) * DH**-0.5).astype(BF16)
            dkv_own[d, :, cols], dkv_oth[d, :, cols] = dk
            dkv_own[d, :, vals], dkv_oth[d, :, vals] = dv


def store_blocks(tensors, quad, zq, sa, sb):
    for t, (a, b) in enumerate(tensors):
        r = a.shape[0] // 4
        for az in range(4):
            sa[t, zq ^ az] = a[az * r : (az + 1) * r].astype(BF16)
            sb[t, zq ^ az] = b[az * r : (az + 1) * r].astype(BF16)


def send_blocks(quad, sa, sb, ak, as_, bk, bs, sem):
    copies = []
    for s in range(4):
        a_ref, a_at = (ak, s // 2) if s % 2 == 0 else (as_, s // 2)
        b_ref, b_at = (bk, s % 2) if s < 2 else (bs, s % 2)
        copies.append(pltpu.make_async_copy(sa.at[quad ^ s], a_ref.at[a_at], sem.at[0, s]))
        copies.append(pltpu.make_async_copy(sb.at[quad ^ s], b_ref.at[b_at], sem.at[1, s]))
    for c in copies:
        c.start()
    for c in copies:
        c.wait()


def cross_grads(meta, h, dq, e_own, e_oth, dkv_own, dkv_oth, dc, o, ak, as_, bk, bs, sa, sb, sem):
    n = dq.shape[1]
    quad, zq = meta[0], meta[1]
    kv = 0.0
    for d in range(e_own.shape[0]):
        kv = kv + dot_tn(e_own[d], dkv_own[d]) + dot_tn(e_oth[d], dkv_oth[d])
    gq = dot_tn(h[...], dq[...])
    go = dot_tn(o[...], dc[...])
    m = gq.shape[0] // 2
    store_blocks(
        [
            (gq[:m], gq[m:]),
            (kv[:m, :n], kv[m:, :n]),
            (kv[:m, n:], kv[m:, n:]),
            (go[:, :m], go[:, m:]),
        ],
        quad,
        zq,
        sa,
        sb,
    )
    send_blocks(quad, sa, sb, ak, as_, bk, bs, sem)


def self_backward(lens, x1, dx2, dq_own, dq_oth, wq_own, wq_oth, gain, wo, q, k, v, buckets, table, gain_o, dx1_o, da_o, dqkv_o, tab_o):
    docs, size = buckets.shape[0], buckets.shape[1]
    n = q.shape[1]
    dh = dot_nt(dq_own[...], wq_own[...]) + dot_nt(dq_oth[...], wq_oth[...])
    dv, gain_grad = rms_backward(x1[...], gain[...], dh)
    gain_o[...] = gain_grad
    dx1 = dx2[...] + dv
    dx1_o[...] = dx1
    da = dx1.astype(BF16)
    da_o[...] = da
    do = dot_nt(da, wo[...]).astype(BF16)
    tab = table[...]
    lanes = lax.broadcasted_iota(jnp.int32, (8, 128), 1)
    subs = lax.broadcasted_iota(jnp.int32, (8, 128), 0)
    tab_grad = jnp.zeros((8, 128), F32)
    for p in range(n // PAIR):
        cols = slice(p * PAIR, (p + 1) * PAIR)
        sums = [jnp.zeros((2 * 8, size), F32) for _ in range(NB)]
        for d in range(docs):
            rows = slice(d * size, (d + 1) * size)
            mask = self_mask(lens[d], size)
            index = buckets[d]
            q2 = stack_pair(q[rows, cols], DH**-0.5)
            do2 = stack_pair(do[rows, cols])
            bias = pair_bias(tab, index, p)
            dq, ds, dk, dvv = attend_back(
                q2, do2, [k[rows, cols]], [v[rows, cols]], [bias], [mask]
            )
            dqkv_o[rows, cols] = (join_pair(dq) * DH**-0.5).astype(BF16)
            dqkv_o[rows, n + p * PAIR : n + (p + 1) * PAIR] = dk[0]
            dqkv_o[rows, 2 * n + p * PAIR : 2 * n + (p + 1) * PAIR] = dvv[0]
            dsf = ds[0].astype(F32)
            index2 = jnp.concatenate([index, index], axis=0)
            for b in range(NB):
                hit = jnp.where(index2 == b, dsf, 0.0)
                sums[b] = sums[b] + jnp.sum(
                    hit.reshape(2, size // 8, 8, size), axis=1
                ).reshape(16, size)
        for b in range(NB):
            for j in range(2):
                total = jnp.sum(sums[b][8 * j : 8 * j + 8])
                tab_grad = jnp.where((subs == 2 * p + j) & (lanes == b), total, tab_grad)
    tab_o[...] = tab_grad


def self_input(dqkv, wq, wk, wv, part_o):
    n = wq.shape[1]
    part_o[...] = (
        dot_nt(dqkv[:, :n], wq[...])
        + dot_nt(dqkv[:, n : 2 * n], wk[...])
        + dot_nt(dqkv[:, 2 * n :], wv[...])
    ).astype(BF16)


def self_grads(meta, h, dqkv, da, o, ak, as_, bk, bs, sa, sb, sem):
    quad, zq = meta[0], meta[1]
    n = o.shape[1]
    g = dot_tn(h[...], dqkv[...])
    go = dot_tn(o[...], da[...])
    m = g.shape[0] // 2
    store_blocks(
        [(g[:m, t * n : (t + 1) * n], g[m:, t * n : (t + 1) * n]) for t in range(3)]
        + [(go[:, :m], go[:, m:])],
        quad,
        zq,
        sa,
        sb,
    )
    send_blocks(quad, sa, sb, ak, as_, bk, bs, sem)


def finish_input(x, p_own, p_oth, gain, dx1, gain_o, dx_o):
    dv, gain_grad = rms_backward(
        x[...].astype(F32), gain[...], p_own[...].astype(F32) + p_oth[...].astype(F32)
    )
    gain_o[...] = gain_grad
    dx_o[...] = dx1[...] + dv


def finish_enc(dkv_own, dkv_got, wk, wv, wk_oth, wv_oth, out):
    n = wk.shape[1]
    for d in range(dkv_own.shape[0]):
        out[d] = (
            dot_nt(dkv_own[d, :, :n], wk[...])
            + dot_nt(dkv_own[d, :, n:], wv[...])
            + (dot_nt(dkv_got[d, :, :n], wk_oth[...]) + dot_nt(dkv_got[d, :, n:], wv_oth[...]))
        ).astype(BF16)


def plus(a, b):
    return (a.astype(F32) + b.astype(F32)).astype(BF16)


def add_one(ak, ar, bk, br, ak_o, as_o, bk_o, bs_o):
    ak_o[...] = plus(ak[0], ar[0])
    as_o[...] = plus(ak[1], ar[1])
    bk_o[...] = plus(bk[0], br[0])
    bs_o[...] = plus(bk[1], br[1])


def add_two(ak, ar, bk, br, z0, z1, z2, z3):
    for s, out in enumerate((z0, z1, z2, z3)):
        a = plus(ak[s], ar[s])
        b = plus(bk[s], br[s])
        c = b.shape[1]
        ra = a.shape[0]
        for j in range(a.shape[1] // c):
            out[j * ra : (j + 1) * ra] = a[:, j * c : (j + 1) * c]
        out[ra * (a.shape[1] // c) :] = b


def add_three(z0, r1, r2, r3, out):
    out[...] = (
        z0[...].astype(F32) + r1[...].astype(F32) + r2[...].astype(F32) + r3[...].astype(F32)
    ).astype(BF16)


def split_shard(meta, f0, f1, f2, f3, a_o, b_o):
    zq = meta[1]
    ra, wide = a_o.shape[1], a_o.shape[2]
    c = f0.shape[1]
    for s, f in enumerate((f0, f1, f2, f3)):
        for j in range(wide // c):
            a_o[zq ^ s, :, j * c : (j + 1) * c] = f[j * ra : (j + 1) * ra]
        b_o[zq ^ s] = f[ra * (wide // c) :]


def write_ffn(meta, a0, a1, a2, a3, b0, b1, b2, b3, out_o, in_o):
    quad = meta[0]
    block = b0.shape[1]
    for s, (a, b) in enumerate(((a0, b0), (a1, b1), (a2, b2), (a3, b3))):
        out_o[quad ^ s] = a[...].astype(F32)
        in_o[:, pl.ds(pl.multiple_of((quad ^ s) * block, 128), block)] = b[...].astype(F32)


def write_attention(meta, a0, a1, a2, a3, b0, b1, b2, b3, q_o, k_o, v_o, o_o, sa, sb):
    quad = meta[0]
    for s, (a, b) in enumerate(((a0, b0), (a1, b1), (a2, b2), (a3, b3))):
        sa[quad ^ s] = a[...]
        sb[quad ^ s] = b[...]
    m = sa.shape[1]
    for t, out in enumerate((q_o, k_o, v_o)):
        out[:m] = sa[t].astype(F32)
        out[m:] = sb[t].astype(F32)
    o_o[:, :m] = sa[3].astype(F32)
    o_o[:, m:] = sb[3].astype(F32)


class Sum:
    def __init__(self, name, dp, meta, ak, as_, bk, bs):
        self.name, self.dp, self.meta = name, dp, meta
        self.ak, self.as_, self.bk, self.bs = ak, as_, bk, bs

    def move(self, a, mask):
        return lax.ppermute(a, "dp", [(i, i ^ mask) for i in range(self.dp)])

    def call(self, body, what, outs, ins, after, **kw):
        return kernel(body, f"{self.name}_{what}", outs, ins, after, **kw)

    def step1(self):
        self.ar = self.move(self.as_, 1)
        self.br = self.move(self.bs, 2)

    def step2(self, after=()):
        sa, sb = self.ak.shape[1:], self.bk.shape[1:]
        self.ak, self.as_, self.bk, self.bs = self.call(
            add_one,
            "add_one",
            [(sa, BF16), (sa, BF16), (sb, BF16), (sb, BF16)],
            [self.ak, self.ar, self.bk, self.br],
            after,
        )
        self.ar = self.move(self.as_, 2)
        self.br = self.move(self.bs, 1)
        return self.ak

    def step3(self, after=()):
        c = self.bk.shape[2]
        rows = self.ak.shape[1] * (self.ak.shape[2] // c) + self.bk.shape[1]
        self.z = self.call(
            add_two,
            "add_two",
            [((rows, c), BF16)] * 4,
            [self.ak, self.ar, self.bk, self.br],
            after,
        )
        self.zr = [self.move(self.z[s], 4 * s) for s in (1, 2, 3)]
        return self.z[0]

    def step4(self, after=()):
        shard = self.call(
            add_three,
            "add_three",
            [(self.z[0].shape, BF16)],
            [self.z[0], *self.zr],
            after,
        )[0]
        step = 16
        while step < self.dp:
            shard = plus(shard, self.move(shard, step))
            step *= 2
        self.f = [shard] + [self.move(shard, 4 * s) for s in (1, 2, 3)]
        return shard

    def step5(self, after=()):
        a, b = self.call(
            split_shard,
            "split_shard",
            [(self.ak.shape, BF16), (self.bk.shape, BF16)],
            [self.meta, *self.f],
            after,
            smem=1,
        )
        a = a.reshape(-1, a.shape[2])
        b = b.reshape(-1, b.shape[2])
        self.a = [a, self.move(a, 1), self.move(a, 2), None]
        self.b = [b, self.move(b, 1), self.move(b, 2), None]
        return a

    def step6(self):
        self.a[3] = self.move(self.a[2], 1)
        self.b[3] = self.move(self.b[1], 2)

    def blocks(self):
        return [self.meta, *self.a, *self.b]


def shards(
    dec_input,
    enc_states,
    dec_lengths,
    enc_lengths,
    rel_buckets,
    out_grad,
    gain_self,
    gain_cross,
    gain_ffn,
    rel_table,
    self_query,
    self_key,
    self_value,
    self_out,
    cross_query,
    cross_key,
    cross_value,
    cross_out,
    ffn_in,
    ffn_out,
    *,
    dp,
):
    docs, size, width = dec_input.shape
    half = enc_states.shape[1]
    rows = docs * size
    n = self_query.shape[1]
    hidden = ffn_in.shape[1]
    index = lax.axis_index("dp")
    meta = jnp.stack([index & 3, (index >> 2) & 3, lax.axis_index("seq")]).astype(jnp.int32)

    def swap(a):
        return lax.ppermute(a, "seq", [(0, 1), (1, 0)])

    x = dec_input.reshape(rows, width)
    dy = out_grad.reshape(rows, width)
    g1, g2, g3 = (g.reshape(1, width) for g in (gain_self, gain_cross, gain_ffn))
    table = jnp.pad(rel_table.T, ((0, 8 - rel_table.shape[1]), (0, 128 - NB)))

    enc_oth = swap(enc_states)
    self_out_oth, cross_out_oth, cross_query_oth = swap(self_out), swap(cross_out), swap(cross_query)
    cross_key_oth, cross_value_oth = swap(cross_key), swap(cross_value)

    tok = (rows, width)
    head = (rows, n)
    h1, q1, k1, v1, o1 = kernel(
        self_forward,
        "self_forward",
        [(tok, BF16)] + [(head, BF16)] * 4,
        [dec_lengths, x, g1, self_query, self_key, self_value, rel_buckets, table],
        smem=1,
    )
    o1_oth = swap(o1)
    kv_shape = (docs, half, 2 * n)
    kv_own = kernel(project_kv, "project_own", [(kv_shape, BF16)], [enc_states, cross_key, cross_value], [o1])[0]
    kv_oth = kernel(project_kv, "project_oth", [(kv_shape, BF16)], [enc_oth, cross_key, cross_value], [kv_own])[0]
    x1, h2, q2, o2 = kernel(
        cross_forward,
        "cross_forward",
        [(tok, F32), (tok, BF16), (head, BF16), (head, BF16)],
        [meta, enc_lengths, x, o1, o1_oth, self_out, self_out_oth, g2, cross_query, kv_own, kv_oth],
        smem=2,
    )
    o2_oth = swap(o2)
    block = hidden // 4
    a_shape, b_shape = (2, 4, block // 4, width), (2, 4, width // 4, block)
    x2, h3, z, du, ak, as_, bk, bs = kernel(
        ffn_grads,
        "ffn_grads",
        [(tok, F32), (tok, BF16), ((4, rows, block), BF16), ((4, rows, block), BF16)]
        + [(a_shape, BF16)] * 2
        + [(b_shape, BF16)] * 2,
        [meta, x1, o2, o2_oth, cross_out, cross_out_oth, g3, ffn_in, ffn_out, dy],
        smem=1,
    )
    ffn = Sum("ffn", dp, meta, ak, as_, bk, bs)
    ffn.step1()
    part = kernel(ffn_rest, "ffn_rest", [((2 * rows, width), BF16)], [meta, z, du, ffn_in, ffn_out], smem=1)[0]
    part_oth = swap(part)
    y, gain3, dx2, dc, dq2, dkv_own, dkv_oth = kernel(
        cross_backward,
        "cross_backward",
        [(tok, BF16), ((1, width), F32), (tok, F32), (tok, BF16), (head, BF16)] + [(kv_shape, BF16)] * 2,
        [meta, enc_lengths, x2, part, part_oth, g3, dy, cross_out, q2, kv_own, kv_oth],
        smem=2,
    )
    dq2_oth = swap(dq2)
    dkv_got = swap(dkv_oth)
    blocks = (2, 4, n // 4, n)
    group_out = [(blocks, BF16)] * 4
    group_scratch = [pltpu.VMEM((4, 4, n // 4, n), BF16)] * 2 + [pltpu.SemaphoreType.DMA((2, 4))]
    sums = kernel(
        cross_grads,
        "cross_grads",
        group_out,
        [meta, h2, dq2, enc_states, enc_oth, dkv_own, dkv_oth, dc, o2],
        smem=1,
        out_specs=[ANY] * 4,
        scratch=group_scratch,
    )
    cross = Sum("cross", dp, meta, *sums)
    last = ffn.step2([sums[0]])
    cross.step1()
    gain2, dx1, da, dqkv, tab_grad = kernel(
        self_backward,
        "self_backward",
        [((1, width), F32), (tok, F32), (tok, BF16), ((rows, 3 * n), BF16), ((8, 128), F32)],
        [dec_lengths, x1, dx2, dq2, dq2_oth, cross_query, cross_query_oth, g2, self_out, q1, k1, v1, rel_buckets, table],
        [last],
        smem=1,
    )
    sums = kernel(
        self_grads,
        "self_grads",
        group_out,
        [meta, h1, dqkv, da, o1],
        smem=1,
        out_specs=[ANY] * 4,
        scratch=group_scratch,
    )
    own = Sum("self", dp, meta, *sums)
    part1 = kernel(self_input, "self_input", [(tok, BF16)], [dqkv, self_query, self_key, self_value], [sums[0]])[0]
    part1_oth = swap(part1)
    last = ffn.step3([part1])
    last = cross.step2([last])
    own.step1()
    gain1, dx = kernel(
        finish_input, "finish_input", [((1, width), F32), (tok, F32)], [x, part1, part1_oth, g1, dx1], [last]
    )
    small = jnp.concatenate([gain1, gain2, gain3], axis=1).reshape(-1, 128)
    small = lax.all_gather(jnp.concatenate([small, tab_grad], axis=0), "dp")
    enc_grad = kernel(
        finish_enc,
        "finish_enc",
        [((docs, half, width), BF16)],
        [dkv_own, dkv_got, cross_key, cross_value, cross_key_oth, cross_value_oth],
        [dx],
    )[0]
    last = ffn.step4([enc_grad])
    last = cross.step3([last])
    last = own.step2([last])
    last = ffn.step5([last])
    last = cross.step4([last])
    last = own.step3([last])
    ffn.step6()
    last = cross.step5([last])
    last = own.step4([last])
    cross.step6()
    last = own.step5([last])
    own.step6()
    out_grad_sum, in_grad_sum = kernel(
        write_ffn,
        "write_ffn",
        [((4, block, width), F32), (ffn_in.shape, F32)],
        ffn.blocks(),
        [last],
        smem=1,
    )
    full = [((width, n), F32)] * 3 + [((n, width), F32)]
    write_scratch = [pltpu.VMEM((4, n, n), BF16)] * 2
    cross_sums = kernel(
        write_attention, "write_cross", full, cross.blocks(), [in_grad_sum], smem=1, scratch=write_scratch
    )
    self_sums = kernel(
        write_attention, "write_self", full, own.blocks(), [cross_sums[0]], smem=1, scratch=write_scratch
    )
    total = jnp.sum(small, axis=0)
    gains = total[: 3 * width // 128].reshape(3, width)
    tab_sum = total[3 * width // 128 :][: n // DH, :NB].T
    return (
        y.reshape(dec_input.shape),
        dx.reshape(dec_input.shape),
        enc_grad,
        gains[0],
        gains[1],
        gains[2],
        tab_sum,
        *self_sums,
        *cross_sums,
        in_grad_sum,
        out_grad_sum.reshape(ffn_out.shape),
    )


def solution(mesh):
    col, row, doc = P(None, "seq"), P("seq", None), P("dp", None, None)
    in_specs = (
        (doc, P("dp", "seq", None), P("dp"), P("dp"), doc, doc)
        + (P(),) * 3
        + (col,) * 4
        + (row,)
        + (col,) * 3
        + (row, col, row)
    )
    out_specs = (
        (doc, doc, P("dp", "seq", None))
        + (P(),) * 3
        + (col,) * 4
        + (row,)
        + (col,) * 3
        + (row, col, row)
    )
    return jax.shard_map(
        functools.partial(shards, dp=mesh.shape["dp"]),
        mesh=mesh,
        in_specs=in_specs,
        out_specs=out_specs,
        check_vma=False,
    )
```

```python
import functools

import jax
import jax.numpy as jnp
from jax import lax
from jax.experimental import pallas as pl
from jax.experimental.pallas import tpu as pltpu
from jax.sharding import PartitionSpec as P

DH = 64
NB = 32
PAIR = 2 * DH
SCALE = DH**-0.5
EPSILON = 1e-06
MASKED = -1e30
F32 = jnp.float32
BF16 = jnp.bfloat16
MIB = 1024 * 1024
SUM_LIMIT = 16


def dot(a, b):
    return lax.dot_general(a, b, (((1,), (0,)), ((), ())), preferred_element_type=F32)


def dot_nt(a, b):
    return lax.dot_general(a, b, (((1,), (1,)), ((), ())), preferred_element_type=F32)


def dot_tn(a, b):
    return lax.dot_general(a, b, (((0,), (0,)), ((), ())), preferred_element_type=F32)


VMEM = pl.BlockSpec(memory_space=pltpu.VMEM)
SMEM = pl.BlockSpec(memory_space=pltpu.SMEM)
ANY = pl.BlockSpec(memory_space=pl.ANY)


def kernel(body, name, outs, ins, after=(), smem=0, in_specs=None, out_specs=None, scratch=(), grid=None, limit=30, aliases=None, us=0.5):
    n_in, n_after = len(ins), len(after)

    def wrapped(*refs):
        body(*refs[:n_in], *refs[n_in + n_after :])

    in_specs = list(in_specs) if in_specs is not None else [VMEM] * (n_in - smem)
    out_specs = list(out_specs) if out_specs is not None else [VMEM] * len(outs)
    params = pltpu.CompilerParams(vmem_limit_bytes=limit * MIB)
    cost = pl.CostEstimate(flops=int(us * 10e9), bytes_accessed=0, transcendentals=0)
    shapes = [jax.ShapeDtypeStruct(s, t) for s, t in outs]
    if grid is None:
        call = pl.pallas_call(
            wrapped,
            name=name,
            out_shape=shapes,
            in_specs=[SMEM] * smem + in_specs + [ANY] * n_after,
            out_specs=out_specs,
            scratch_shapes=list(scratch),
            compiler_params=params,
            cost_estimate=cost,
            input_output_aliases=aliases or {},
        )
    else:
        call = pl.pallas_call(
            wrapped,
            name=name,
            out_shape=shapes,
            grid_spec=pltpu.PrefetchScalarGridSpec(
                num_scalar_prefetch=smem,
                grid=grid,
                in_specs=in_specs + [ANY] * n_after,
                out_specs=out_specs,
                scratch_shapes=list(scratch),
            ),
            compiler_params=params,
            cost_estimate=cost,
            input_output_aliases=aliases or {},
        )
    return call(*ins, *after)


def pin(*arrays):
    return [pltpu.with_memory_space_constraint(a, pltpu.HBM) for a in arrays]


def whole(shape):
    return pl.BlockSpec(shape, lambda *_: (0,) * len(shape))


def step_block(shape, axis=0):
    return pl.BlockSpec(shape, lambda i, *_: tuple(i if a == axis else 0 for a in range(len(shape))))


def inverse_rms(values):
    return lax.rsqrt(jnp.mean(values * values, axis=-1, keepdims=True) + EPSILON)


def row_of(gain):
    return gain[...].reshape(1, gain.shape[0])


def rms_backward(values, gain, grad):
    inverse = inverse_rms(values)
    scaled = grad * gain
    inner = jnp.mean(scaled * values, axis=-1, keepdims=True)
    grad_in = inverse * scaled - values * (inverse * inverse * inverse * inner)
    return grad_in, jnp.sum(grad * values * inverse, axis=0, keepdims=True)


def stack_pair(pair, scale=1.0):
    lanes = lax.broadcasted_iota(jnp.int32, (1, PAIR), 1)
    low = jnp.where(lanes < DH, scale, 0.0).astype(BF16)
    high = jnp.where(lanes < DH, 0.0, scale).astype(BF16)
    return jnp.concatenate([pair * low, pair * high], axis=0)


def join_pair(turned):
    n = turned.shape[1] // 2
    return jnp.concatenate([turned[:DH, :n], turned[DH:, n:]], axis=0).T


def fold(op, parts):
    return functools.reduce(op, parts)


def attend(q2, keys, values, biases):
    scores = [dot_nt(k, q2) + b for k, b in zip(keys, biases)]
    top = fold(jnp.maximum, [jnp.max(s, axis=0, keepdims=True) for s in scores])
    exps = [jnp.exp(s - top) for s in scores]
    total = fold(jnp.add, [jnp.sum(e, axis=0, keepdims=True) for e in exps])
    inv = 1.0 / total
    out = fold(jnp.add, [dot_tn(v, (e * inv).astype(BF16)) for e, v in zip(exps, values)])
    return out, top + jnp.log(total)


def attend_back(q2, do2, lse, keys, values, biases):
    probs = [jnp.exp(dot_nt(k, q2) + b - lse) for k, b in zip(keys, biases)]
    dv = [dot(p.astype(BF16), do2).astype(BF16) for p in probs]
    dp = [dot_nt(v, do2) for v in values]
    row = fold(jnp.add, [jnp.sum(p * g, axis=0, keepdims=True) for p, g in zip(probs, dp)])
    ds = [(p * (g - row)).astype(BF16) for p, g in zip(probs, dp)]
    dq = fold(jnp.add, [dot_tn(k, s) for s, k in zip(ds, keys)])
    dk = [dot(s, q2).astype(BF16) for s in ds]
    return dq, ds, dk, dv


def twice(a):
    return jnp.concatenate([a, a], axis=1)


def self_hidden(length, size):
    keys = lax.broadcasted_iota(jnp.int32, (size, size), 0)
    queries = lax.broadcasted_iota(jnp.int32, (size, size), 1)
    return jnp.where((keys <= queries) & (keys < length), 0.0, MASKED)


def cross_hidden(length, core, size, half):
    out = []
    for part in (core, 1 - core):
        pos = lax.broadcasted_iota(jnp.int32, (half, size), 0) + part * half
        out.append(twice(jnp.where(pos < length, 0.0, MASKED)))
    return out


def table_lines(table):
    lanes = lax.broadcasted_iota(jnp.int32, (1, 128), 1)
    lines = []
    for head in range(table.shape[0]):
        line = jnp.zeros((1, 128), F32)
        for b in range(NB):
            line = jnp.where(lanes == b, table[head, b], line)
        lines.append(line)
    return lines


def pair_bias(lines, index, pair, hidden):
    cols = []
    for head in (2 * pair, 2 * pair + 1):
        line = jnp.broadcast_to(lines[head], index.shape)
        cols.append(jnp.take_along_axis(line, index, axis=1, mode="promise_in_bounds") + hidden)
    return jnp.concatenate(cols, axis=1)


def self_forward(lens, table, x, gain, wq, wk, wv, buckets, h_o, q_o, k_o, v_o, o_o, lse_o):
    docs, size = buckets.shape[0], buckets.shape[1]
    xf = x[...].astype(F32)
    h = (xf * inverse_rms(xf) * row_of(gain)).astype(BF16)
    h_o[...] = h
    q_o[...] = dot(h, wq[...]).astype(BF16)
    k_o[...] = dot(h, wk[...]).astype(BF16)
    v_o[...] = dot(h, wv[...]).astype(BF16)
    lines = table_lines(table)
    pairs = wq.shape[1] // PAIR
    for d in range(docs):
        rows = slice(d * size, (d + 1) * size)
        hidden = self_hidden(lens[d], size)
        index = buckets[d].T
        for p in range(pairs):
            cols = slice(p * PAIR, (p + 1) * PAIR)
            q2 = stack_pair(q_o[rows, cols], SCALE)
            bias = pair_bias(lines, index, p, hidden)
            out, lse = attend(q2, [k_o[rows, cols]], [v_o[rows, cols]], [bias])
            o_o[rows, cols] = join_pair(out).astype(BF16)
            at = d * pairs + p
            lse_o[at : at + 1, :] = lse


def project_kv(e, wk, wv, kv_o):
    n = wk.shape[1]
    kv_o[0, :, :n] = dot(e[0], wk[...]).astype(BF16)
    kv_o[0, :, n:] = dot(e[0], wv[...]).astype(BF16)


def cross_forward(meta, lens, x, o_own, o_oth, wo_own, wo_oth, gain, wq, kv_own, kv_oth, x1_o, h_o, q_o, o_o, lse_o):
    half, n = kv_own.shape[1], wq.shape[1]
    size = o_o.shape[0]
    doc = pl.program_id(0)

    @pl.when(doc == 0)
    def _():
        x1 = x[...].astype(F32) + (dot(o_own[...], wo_own[...]) + dot(o_oth[...], wo_oth[...]))
        x1_o[...] = x1
        h = (x1 * inverse_rms(x1) * row_of(gain)).astype(BF16)
        h_o[...] = h
        q_o[...] = dot(h, wq[...]).astype(BF16)

    hidden = cross_hidden(lens[doc], meta[2], size, half)
    q = q_o[pl.ds(pl.multiple_of(doc * size, size), size), :]
    for p in range(n // PAIR):
        cols = slice(p * PAIR, (p + 1) * PAIR)
        vals = slice(n + p * PAIR, n + (p + 1) * PAIR)
        out, lse = attend(
            stack_pair(q[:, cols], SCALE),
            [kv_own[0, :, cols], kv_oth[0, :, cols]],
            [kv_own[0, :, vals], kv_oth[0, :, vals]],
            hidden,
        )
        o_o[:, cols] = join_pair(out).astype(BF16)
        lse_o[0, p : p + 1, :] = lse


GELU_C = 0.7978845608028654
GELU_A = 0.044715


def grid_slot(i):
    return jnp.where(i < 2, 2 * i + 1, 2 * (i - 2))


def ffn_act_grad(meta, dy, wout, dz_o):
    dz_o[0] = dot_nt(dy[...], wout[...])


def ffn_forward(meta, x1, o_own, o_oth, wo_own, wo_oth, gain, win, dz, x2_o, z_send, z_keep, du_send, du_keep, part_o, h_s, total):
    i = pl.program_id(0)

    @pl.when(i == 0)
    def _():
        x2 = x1[...] + (dot(o_own[...], wo_own[...]) + dot(o_oth[...], wo_oth[...]))
        x2_o[...] = x2
        h = (x2 * inverse_rms(x2) * row_of(gain)).astype(BF16)
        h_s[...] = h
        half = h.shape[1] // 2
        du_send[2] = h[:, :half]
        du_send[3] = h[:, half:]

    u = dot(h_s[...], win[...])
    u2 = u * u
    t = jnp.tanh(GELU_C * (u + GELU_A * (u * u2)))
    g = 0.5 * (1.0 + t)
    slope = g + (0.5 * GELU_C) * u * (1.0 - t * t) * (1.0 + 3.0 * GELU_A * u2)
    z = (u * g).astype(BF16)
    du = (dz[0] * slope).astype(BF16)
    z_slot = meta[0] ^ grid_slot(i) ^ meta[3]

    @pl.when((z_slot & 1) == 1)
    def _():
        z_send[z_slot >> 1] = z

    @pl.when((z_slot & 1) == 0)
    def _():
        z_keep[z_slot >> 1] = z

    @pl.when(i < 2)
    def _():
        du_send[i] = du

    @pl.when(i >= 2)
    def _():
        du_keep[i - 2] = du

    grad = dot_nt(du, win[...])

    @pl.when(i == 0)
    def _():
        total[...] = grad

    @pl.when((i > 0) & (i < 3))
    def _():
        total[...] += grad

    @pl.when(i == 3)
    def _():
        part_o[...] = (total[...] + grad).astype(BF16)


def ffn_out_grads(meta, keep, got, dy, dy_got, keep_o, send_o):
    half = dy.shape[1] // 2
    for j, out in enumerate((keep_o, send_o)):
        w = (dot_tn(keep[j], dy[...]) + dot_tn(got[j], dy_got[...])).astype(BF16)
        r = w.shape[0] // 4
        for az in range(4):
            for k in range(2):
                out[meta[1] ^ az, k * r : (k + 1) * r] = w[az * r : (az + 1) * r, k * half : (k + 1) * half]


def ffn_in_grads(meta, keep, send, got, keep_o, send_o):
    for j, out in enumerate((keep_o, send_o)):
        for k in range(2):
            w = (dot_tn(send[2 + k], keep[j]) + dot_tn(got[2 + k], got[j])).astype(BF16)
            r = w.shape[0] // 2
            for az in range(2):
                out[meta[1] ^ (2 * k + az)] = w[az * r : (az + 1) * r]


def ffn_branch(meta, send, keep, wout, part_o, total):
    i = pl.program_id(0)
    branch = dot(jnp.where(i < 2, send[0], keep[0]), wout[...])

    @pl.when(i == 0)
    def _():
        total[...] = branch

    @pl.when((i > 0) & (i < 3))
    def _():
        total[...] += branch

    @pl.when(i == 3)
    def _():
        part_o[...] = (total[...] + branch).astype(BF16)


def finish_output(x2, p_own, p_oth, y_o):
    y_o[...] = (x2[...] + (p_own[...].astype(F32) + p_oth[...].astype(F32))).astype(BF16)


def cross_backward(meta, lens, x2, p_own, p_oth, gain, dy, wo, q, lse, kv_own, kv_oth, gain_o, dx2_o, dc_o, dq_o, dkv_own, dkv_oth, do_s):
    half, n = kv_own.shape[1], q.shape[1]
    size = q.shape[0]
    doc = pl.program_id(0)

    @pl.when(doc == 0)
    def _():
        dv, gain_grad = rms_backward(x2[...], row_of(gain), p_own[...].astype(F32) + p_oth[...].astype(F32))
        gain_o[...] = gain_grad
        dx2 = dy[...].astype(F32) + dv
        dx2_o[...] = dx2
        dc = dx2.astype(BF16)
        dc_o[...] = dc
        do_s[...] = dot_nt(dc, wo[...]).astype(BF16)

    hidden = cross_hidden(lens[doc], meta[2], size, half)
    do = do_s[pl.ds(pl.multiple_of(doc * size, size), size), :]
    for p in range(n // PAIR):
        cols = slice(p * PAIR, (p + 1) * PAIR)
        vals = slice(n + p * PAIR, n + (p + 1) * PAIR)
        dq, _, dk, dv = attend_back(
            stack_pair(q[:, cols], SCALE),
            stack_pair(do[:, cols]),
            lse[0, p : p + 1, :],
            [kv_own[0, :, cols], kv_oth[0, :, cols]],
            [kv_own[0, :, vals], kv_oth[0, :, vals]],
            hidden,
        )
        dq_o[:, cols] = (join_pair(dq) * SCALE).astype(BF16)
        dkv_own[0, :, cols], dkv_oth[0, :, cols] = dk
        dkv_own[0, :, vals], dkv_oth[0, :, vals] = dv


def store_tensors(tensors, zq, scratch):
    for t, quarters in enumerate(tensors):
        for az, quarter in enumerate(quarters):
            scratch[t, zq ^ az] = quarter.astype(BF16)


def tall(a):
    r = a.shape[0] // 4
    return [a[z * r : (z + 1) * r] for z in range(4)]


def wide(a):
    r, c = a.shape[0] // 2, a.shape[1] // 2
    return [a[(z % 2) * r : (z % 2 + 1) * r, (z // 2) * c : (z // 2 + 1) * c] for z in range(4)]


def send_blocks(quad, scratch, keep, send, sem):
    copies = []
    for s in range(4):
        ref = keep if s % 2 == 0 else send
        copies.append(pltpu.make_async_copy(scratch.at[quad ^ s], ref.at[s // 2], sem.at[s]))
    for c in copies:
        c.start()
    for c in copies:
        c.wait()


def cross_grads(meta, h, dq, e_own, e_oth, dkv_own, dkv_oth, dc, o, keep, send, scratch, sem):
    n = dq.shape[1]
    kv = dot_tn(e_own[...], dkv_own[...]) + dot_tn(e_oth[...], dkv_oth[...])
    gq = dot_tn(h[...], dq[...])
    go = dot_tn(o[...], dc[...])
    store_tensors([tall(gq), tall(kv[:, :n]), tall(kv[:, n:]), wide(go)], meta[1], scratch)
    send_blocks(meta[0], scratch, keep, send, sem)


def self_backward(lens, table, x1, dx2, dq_own, dq_oth, wq_own, wq_oth, gain, wo, q, k, v, lse, buckets, gain_o, dx1_o, da_o, dqkv_o, ds_o):
    docs, size = buckets.shape[0], buckets.shape[1]
    n = q.shape[1]
    dh = dot_nt(dq_own[...], wq_own[...]) + dot_nt(dq_oth[...], wq_oth[...])
    dv, gain_grad = rms_backward(x1[...], row_of(gain), dh)
    gain_o[...] = gain_grad
    dx1 = dx2[...] + dv
    dx1_o[...] = dx1
    da = dx1.astype(BF16)
    da_o[...] = da
    do = dot_nt(da, wo[...]).astype(BF16)
    lines = table_lines(table)
    pairs = n // PAIR
    for d in range(docs):
        rows = slice(d * size, (d + 1) * size)
        hidden = self_hidden(lens[d], size)
        index = buckets[d].T
        for p in range(pairs):
            cols = slice(p * PAIR, (p + 1) * PAIR)
            at = d * pairs + p
            dq, ds, dk, dvv = attend_back(
                stack_pair(q[rows, cols], SCALE),
                stack_pair(do[rows, cols]),
                lse[at : at + 1, :],
                [k[rows, cols]],
                [v[rows, cols]],
                [pair_bias(lines, index, p, hidden)],
            )
            dqkv_o[rows, cols] = (join_pair(dq) * SCALE).astype(BF16)
            dqkv_o[rows, n + p * PAIR : n + (p + 1) * PAIR] = dk[0]
            dqkv_o[rows, 2 * n + p * PAIR : 2 * n + (p + 1) * PAIR] = dvv[0]
            ds_o[p, d] = ds[0]


def self_input(dqkv, wq, wk, wv, part_o):
    n = wq.shape[1]
    part_o[...] = (
        dot_nt(dqkv[:, :n], wq[...])
        + dot_nt(dqkv[:, n : 2 * n], wk[...])
        + dot_nt(dqkv[:, 2 * n :], wv[...])
    ).astype(BF16)


def self_grads(meta, h, dqkv, da, o, keep, send, scratch, sem):
    n = o.shape[1]
    g = dot_tn(h[...], dqkv[...])
    go = dot_tn(o[...], da[...])
    store_tensors([tall(g[:, t * n : (t + 1) * n]) for t in range(3)] + [wide(go)], meta[1], scratch)
    send_blocks(meta[0], scratch, keep, send, sem)


def finish_input(x, p_own, p_oth, gain, dx1, gain_o, dx_o):
    dv, gain_grad = rms_backward(
        x[...].astype(F32), row_of(gain), p_own[...].astype(F32) + p_oth[...].astype(F32)
    )
    gain_o[...] = gain_grad
    dx_o[...] = dx1[...] + dv


def small_grads(buckets, ds, gain1, gain2, gain3, out):
    docs, size = buckets.shape[0], buckets.shape[1]
    pairs = ds.shape[0]
    half = out.shape[1]
    lanes = lax.broadcasted_iota(jnp.int32, (8, 128), 1)
    subs = lax.broadcasted_iota(jnp.int32, (8, 128), 0)
    out[...] = jnp.zeros(out.shape, F32)
    for j, gain in enumerate((gain1, gain2, gain3)):
        for k in range(2):
            out[2 * j + k : 2 * j + k + 1, :] = gain[:, k * half : (k + 1) * half]
    table = jnp.zeros((8, 128), F32)
    index = [twice(buckets[d].T) for d in range(docs)]
    for p in range(pairs):
        for b in range(NB):
            line = fold(
                jnp.add,
                [
                    jnp.sum(jnp.where(index[d] == b, ds[p, d].astype(F32), 0.0), axis=0, keepdims=True)
                    for d in range(docs)
                ],
            )
            for j in range(2):
                total = jnp.sum(line[:, j * size : (j + 1) * size], axis=1, keepdims=True)
                table = jnp.where((subs == 2 * p + j) & (lanes == b), total, table)
    out[8:16, :128] = table


def enc_part(dkv, wk, wv, out):
    n = wk.shape[1]
    out[0] = (dot_nt(dkv[0, :, :n], wk[...]) + dot_nt(dkv[0, :, n:], wv[...])).astype(BF16)


def finish_enc(dkv, wk, wv, got, out):
    n = wk.shape[1]
    own = dot_nt(dkv[0, :, :n], wk[...]) + dot_nt(dkv[0, :, n:], wv[...])
    out[0] = (own + got[0].astype(F32)).astype(BF16)


def add_quads(keep, got, keep_o, send_o):
    keep_o[...] = keep[0] + got[0]
    send_o[...] = keep[1] + got[1]


EXTRA = 16


def add_quads(keep, got, keep_o, send_o):
    keep_o[...] = keep[0] + got[0]
    send_o[...] = keep[1] + got[1]


def add_pieces(keep, got, keep_o, send_o):
    for j in range(2):
        keep_o[j] = keep[2 * j] + got[2 * j]
        send_o[j] = keep[2 * j + 1] + got[2 * j + 1]


def add_pair(keep, got, keep_o, send_o):
    keep_o[...] = keep[0] + got[0]
    send_o[...] = keep[1] + got[1]


def add_shard(keep, got, out):
    out[...] = keep[...] + got[...]


def put_two(a, b, out):
    out[0] = a[...]
    out[1] = b[...]


def join_pieces(meta, own, got, out):
    r = own.shape[1]
    for j in range(2):
        out[pl.ds(pl.multiple_of((meta[1] ^ (2 * j)) * r, r), r), :] = own[j]
        out[pl.ds(pl.multiple_of((meta[1] ^ (2 * j + 1)) * r, r), r), :] = got[j]


def put_blocks(a, b, out):
    r = a.shape[0]
    out[:r] = a[...]
    out[r:] = b[...]


def plus_small(own, got):
    return (own[...].astype(BF16).astype(F32) + got.astype(F32)).astype(BF16)


def self_quads(keep, got, small, keep_o, send_o):
    keep_o[...] = keep[0] + got[0]
    r = keep.shape[2]
    for z in range(4):
        send_o[z * r : (z + 1) * r] = keep[1, z] + got[1, z]
    send_o[4 * r :] = small[...].astype(BF16)


def self_pieces(keep, got, small, keep_o, send_o, small_o):
    r = keep.shape[1]
    total = plus_small(small, got[4 * r :])
    small_o[...] = total
    for j in range(2):
        keep_o[j] = keep[2 * j] + got[2 * j * r : (2 * j + 1) * r]
        send_o[j * r : (j + 1) * r] = keep[2 * j + 1] + got[(2 * j + 1) * r : (2 * j + 2) * r]
    send_o[2 * r :] = total


def self_pair(keep, got, small, keep_o, send_o, small_o):
    r = keep.shape[1]
    total = plus_small(small, got[2 * r :])
    small_o[...] = total
    keep_o[...] = keep[0] + got[:r]
    send_o[:r] = keep[1] + got[r : 2 * r]
    send_o[r:] = total


def self_shard(keep, got, small, out, small_o):
    r = keep.shape[0]
    out[...] = keep[...] + got[:r]
    small_o[...] = plus_small(small, got[r:])


def self_blocks(a, b, small, out):
    r = a.shape[0]
    out[:r] = a[...]
    out[r : 2 * r] = b[...]
    out[2 * r :] = small[...]


def write_small(own, got, gain1_o, gain2_o, gain3_o, table_o):
    total = own[...].astype(F32) + got[got.shape[0] - EXTRA :, :].astype(F32)
    for j, gain in enumerate((gain1_o, gain2_o, gain3_o)):
        gain[...] = jnp.concatenate([total[2 * j : 2 * j + 1], total[2 * j + 1 : 2 * j + 2]], axis=1).reshape(gain.shape)
    heads, buckets = table_o.shape
    table_o[...] = total[8 : 8 + heads, :buckets]


def write_ffn_out(slots, meta, both, *refs):
    out, done, scratch, sem = refs[-4:]
    done[...] = jnp.zeros(done.shape, F32)
    r, c = scratch.shape[1] // 4, scratch.shape[2] // 2
    copies = []
    for i, s in enumerate(slots):
        for z in range(4):
            for j in range(2):
                at = (8 * i + 2 * z + j) * r
                scratch[i, z * r : (z + 1) * r, j * c : (j + 1) * c] = both[at : at + r].astype(F32)
        copies.append(pltpu.make_async_copy(scratch.at[i], out.at[meta[0] ^ s], sem.at[i]))
        copies[-1].start()
    for copy in copies:
        copy.wait()


def write_ffn_in(slots, meta, both, *refs):
    out, done, scratch, sem = refs[-4:]
    done[...] = jnp.zeros(done.shape, F32)
    r, c = scratch.shape[1:]
    copies = []
    for i, s in enumerate(slots):
        scratch[i] = both[i * r : (i + 1) * r].astype(F32)
        cols = pl.ds(pl.multiple_of((meta[0] ^ s) * c, 128), c)
        copies.append(pltpu.make_async_copy(scratch.at[i], out.at[:, cols], sem.at[i]))
        copies[-1].start()
    for copy in copies:
        copy.wait()


def write_attention(slots, meta, both, *refs):
    q_o, k_o, v_o, o_o, done, scratch, sem = refs[-7:]
    done[...] = jnp.zeros(done.shape, F32)
    rows, c = scratch.shape[1:]
    m = rows // 2

    def copies_of(i, t):
        if t < 3:
            return [pltpu.make_async_copy(scratch.at[i], (q_o, k_o, v_o)[t], sem.at[i, 0])]
        return [
            pltpu.make_async_copy(
                scratch.at[i, pl.ds(j * m, m)], o_o.at[:, pl.ds(j * c, c)], sem.at[i, j]
            )
            for j in range(2)
        ]

    for i, s in enumerate(slots):
        scratch[i] = both[i * rows : (i + 1) * rows].astype(F32)
        for t in range(4):

            @pl.when((meta[0] ^ s) == t)
            def _(i=i, t=t):
                for copy in copies_of(i, t):
                    copy.start()

    for i, s in enumerate(slots):
        for t in range(4):

            @pl.when((meta[0] ^ s) == t)
            def _(i=i, t=t):
                for copy in copies_of(i, t):
                    copy.wait()


class Sum:
    def __init__(self, name, dp, masks, meta, keep=None, send=None):
        self.name, self.dp, self.masks, self.meta = name, dp, masks, meta
        self.keep, self.send, self.small = keep, send, None

    def move(self, a, mask, what):
        pairs = [(2 * i + c, 2 * (i ^ mask[c]) + c) for i in range(self.dp) for c in range(2)]
        with jax.named_scope(f"{self.name}_{what}"):
            return lax.ppermute(a, ("top", "mid", "xy", "seq"), pairs)

    def exchange(self, a, k, what):
        self.got = self.move(a, self.masks[k], what)

    def call(self, body, outs, ins, after, **kw):
        name = f"{self.name}_{body.__name__}" if hasattr(body, "__name__") else f"{self.name}_write"
        return kernel(body, name, outs, ins, after, **{"limit": SUM_LIMIT, **kw})

    def step_a(self):
        self.exchange(self.send, 0, "sum_a")

    def step_b(self, after=(), small=None):
        z, r, c = self.keep.shape[1:]
        ins, self.small = [self.keep, self.got], small
        if small is None:
            self.keep, send = self.call(add_quads, [((z, r, c), BF16)] * 2, ins, after)
        else:
            self.keep, send = self.call(
                self_quads, [((z, r, c), BF16), ((z * r + EXTRA, c), BF16)], [*ins, small], after
            )
        self.exchange(send, 1, "sum_b")
        return self.keep

    def step_c(self, after=()):
        z, r, c = self.keep.shape
        ins, half = [self.keep, self.got], ((2, r, c), BF16)
        if self.small is None:
            self.keep, send = self.call(add_pieces, [half] * 2, ins, after)
        else:
            self.keep, send, self.small = self.call(
                self_pieces,
                [half, ((2 * r + EXTRA, c), BF16), (self.small.shape, BF16)],
                [*ins, self.small],
                after,
            )
        self.exchange(send, 2, "sum_c")
        return self.keep

    def step_d(self, after=()):
        z, r, c = self.keep.shape
        ins, one = [self.keep, self.got], ((r, c), BF16)
        if self.small is None:
            self.keep, send = self.call(add_pair, [one] * 2, ins, after)
        else:
            self.keep, send, self.small = self.call(
                self_pair,
                [one, ((r + EXTRA, c), BF16), (self.small.shape, BF16)],
                [*ins, self.small],
                after,
            )
        self.exchange(send, 3, "sum_d")
        return self.keep

    def step_e(self, after=()):
        ins, one = [self.keep, self.got], (self.keep.shape, BF16)
        if self.small is None:
            self.shard = self.call(add_shard, [one], ins, after)[0]
        else:
            self.shard, self.small = self.call(
                self_shard, [one, (self.small.shape, BF16)], [*ins, self.small], after
            )
        step = 16
        while step < self.dp:
            rest = (step, step)
            self.shard = self.shard + self.move(self.shard, rest, "sum_rest")
            if self.small is not None:
                self.small = self.small + self.move(self.small, rest, "sum_rest")
            step *= 2
        self.exchange(self.shard, 3, "gather_d")
        return self.shard

    def step_f(self, after=()):
        shape = (2,) + self.shard.shape
        self.two = self.call(put_two, [(shape, BF16)], [self.shard, self.got], after)[0]
        self.exchange(self.two, 2, "gather_c")
        return self.two

    def step_g(self, after=()):
        r, c = self.shard.shape
        self.block = self.call(
            join_pieces, [((4 * r, c), BF16)], [self.meta, self.two, self.got], after, smem=1
        )[0]
        self.exchange(self.block, 1, "gather_b")
        return self.block

    def step_h(self, after=()):
        r, c = self.block.shape
        ins = [self.block, self.got]
        if self.small is None:
            self.near = self.call(put_blocks, [((2 * r, c), BF16)], ins, after)[0]
        else:
            self.near = self.call(self_blocks, [((2 * r + EXTRA, c), BF16)], [*ins, self.small], after)[0]
        self.exchange(self.near, 0, "gather_a")
        return self.near

    def write(self, slots, both, into, after):
        body, outs, scratch = self.target
        into = list(into)
        *self.out, done = self.call(
            functools.partial(body, slots),
            [(o, F32) for o in outs] + [((8, 128), F32)],
            [self.meta, both, *into],
            after,
            smem=1,
            in_specs=[VMEM] + [ANY] * len(into),
            out_specs=[ANY] * len(outs) + [VMEM],
            scratch=scratch,
            aliases={2 + i: i for i in range(len(into))},
            limit=30,
            us=2,
        )
        return done

    def write1(self, after=()):
        return self.write((0, 2), self.near, (), after)

    def write2(self, after=()):
        return self.write((1, 3), self.got, self.out, after)


def shards(
    dec_input,
    enc_states,
    dec_lengths,
    enc_lengths,
    rel_buckets,
    out_grad,
    gain_self,
    gain_cross,
    gain_ffn,
    rel_table,
    self_query,
    self_key,
    self_value,
    self_out,
    cross_query,
    cross_key,
    cross_value,
    cross_out,
    ffn_in,
    ffn_out,
    *,
    dp,
):
    docs, size, width = dec_input.shape
    half = enc_states.shape[1]
    rows = docs * size
    n = self_query.shape[1]
    hidden = ffn_in.shape[1]
    block = hidden // 4
    pairs = n // PAIR
    index, core = lax.axis_index(("top", "mid", "xy")), lax.axis_index("seq")
    bits = [(index >> k) & 1 for k in range(4)]
    one, two = jnp.where(core == 0, bits[0], bits[1]), jnp.where(core == 0, bits[1], bits[0])
    near, far, up, top = (1, 2), (2, 1), (4, 4), (8, 8)
    quad, quad_out = one + 2 * two, bits[2] + 2 * one
    meta = jnp.stack([quad, bits[2] + 2 * bits[3], core, quad_out, two + 2 * bits[3]]).astype(jnp.int32)
    meta_out = meta[3:]

    def swap(a):
        return lax.ppermute(a, "seq", [(0, 1), (1, 0)])

    x = dec_input.reshape(rows, width)
    dy = out_grad.reshape(rows, width)
    fo = Sum("ffn_out", dp, (up, near, far, top), meta_out)
    fi = Sum("ffn_in", dp, (near, far, up, top), meta)
    dy_got = fo.move(dy, up, "tokens")
    enc_oth = swap(enc_states)
    self_out_oth, cross_out_oth, cross_query_oth = swap(self_out), swap(cross_out), swap(cross_query)

    tok = (rows, width)
    head = (rows, n)
    h1, q1, k1, v1, o1, lse1 = kernel(
        self_forward,
        "self_forward",
        [(tok, BF16)] + [(head, BF16)] * 4 + [((docs * pairs, 2 * size), F32)],
        [dec_lengths, rel_table.T, *pin(x), gain_self, *pin(self_query, self_key, self_value, rel_buckets)],
        smem=2,
        us=2.7,
    )
    o1_oth = swap(o1)
    kv_shape = (docs, half, 2 * n)
    kv_block = step_block((1, half, 2 * n))
    enc_block = step_block((1, half, width))
    w_block = whole((width, n))
    project = dict(grid=(docs,), in_specs=[enc_block, w_block, w_block], out_specs=[kv_block])
    kv_own = kernel(project_kv, "project_own", [(kv_shape, BF16)], [enc_states, cross_key, cross_value], [o1], us=2, **project)[0]
    kv_oth = kernel(project_kv, "project_oth", [(kv_shape, BF16)], [enc_oth, cross_key, cross_value], [kv_own], us=2, **project)[0]
    wide_tok, wide_head, wo_block = whole(tok), whole(head), whole((n, width))
    gain_block = whole((width,))
    lse_shape = (docs, pairs, 2 * size)
    lse_block = step_block((1, pairs, 2 * size))
    head_block = step_block((size, n))
    x1, h2, q2, o2, lse2 = kernel(
        cross_forward,
        "cross_forward",
        [(tok, F32), (tok, BF16), (head, BF16), (head, BF16), (lse_shape, F32)],
        [meta, enc_lengths, x, o1, o1_oth, self_out, self_out_oth, gain_cross, cross_query, kv_own, kv_oth],
        smem=2,
        grid=(docs,),
        in_specs=[wide_tok, wide_head, wide_head, wo_block, wo_block, gain_block, w_block, kv_block, kv_block],
        out_specs=[wide_tok, wide_tok, wide_head, head_block, lse_block],
        us=8,
    )
    o2_oth = swap(o2)
    group = (2, 4, width // 4, n)
    act = (4, rows, block)
    act_block = pl.BlockSpec((1, rows, block), lambda i, m: (grid_slot(i), 0, 0))
    win_block = pl.BlockSpec((width, block), lambda i, m: (0, m[0] ^ grid_slot(i)))
    wout_block = pl.BlockSpec((block, width), lambda i, m: (m[0] ^ grid_slot(i), 0))
    dz = kernel(
        ffn_act_grad,
        "ffn_act_grad",
        [(act, F32)],
        [meta, dy, ffn_out],
        [o2],
        smem=1,
        grid=(4,),
        in_specs=[wide_tok, wout_block],
        out_specs=[act_block],
        us=2.5,
    )[0]
    pair_act, sent = (2, rows, block), (4, rows, block)
    x2, z_send, z_keep, du_send, du_keep, part = kernel(
        ffn_forward,
        "ffn_forward",
        [(tok, F32), (pair_act, BF16), (pair_act, BF16), (sent, BF16), (pair_act, BF16), (tok, BF16)],
        [meta, x1, o2, o2_oth, cross_out, cross_out_oth, gain_ffn, ffn_in, dz],
        [dy_got],
        smem=1,
        grid=(4,),
        in_specs=[wide_tok, wide_head, wide_head, wo_block, wo_block, gain_block, win_block, act_block],
        out_specs=[wide_tok, whole(pair_act), whole(pair_act), whole(sent), whole(pair_act), wide_tok],
        scratch=[pltpu.VMEM(tok, BF16), pltpu.VMEM(tok, F32)],
        us=8,
    )
    z_got = fo.move(z_send, up, "sum_a")
    du_got = fi.move(du_send, near, "sum_a")
    part_oth = swap(part)
    gain3, dx2, dc, dq2, dkv_own, dkv_oth = kernel(
        cross_backward,
        "cross_backward",
        [((1, width), F32), (tok, F32), (tok, BF16), (head, BF16)] + [(kv_shape, BF16)] * 2,
        [meta, enc_lengths, x2, part, part_oth, gain_ffn, dy, cross_out, q2, lse2, kv_own, kv_oth],
        smem=2,
        grid=(docs,),
        in_specs=[wide_tok, wide_tok, wide_tok, gain_block, wide_tok, wo_block]
        + [head_block, lse_block, kv_block, kv_block],
        out_specs=[whole((1, width)), wide_tok, wide_tok, head_block, kv_block, kv_block],
        scratch=[pltpu.VMEM(head, BF16)],
        us=10,
    )
    dq2_oth = swap(dq2)
    piece = group[1:]
    fo.keep, send = kernel(
        ffn_out_grads, "ffn_out_grads", [(piece, BF16)] * 2, [meta_out, z_keep, z_got, dy, dy_got], [dq2], smem=1, us=3
    )
    fo.exchange(send, 1, "sum_b")
    fi.keep, send = kernel(
        ffn_in_grads, "ffn_in_grads", [(piece, BF16)] * 2, [meta, du_keep, du_send, du_got], [fo.keep], smem=1, us=3
    )
    fi.exchange(send, 1, "sum_b")
    group_scratch = [pltpu.VMEM((4,) + group[1:], BF16), pltpu.SemaphoreType.DMA((4,))]
    enc_rows = (docs * half, width)
    keep, send = kernel(
        cross_grads,
        "cross_grads",
        [(group, BF16)] * 2,
        [meta, h2, dq2, enc_states.reshape(enc_rows), enc_oth.reshape(enc_rows)]
        + [dkv_own.reshape(enc_rows), dkv_oth.reshape(enc_rows), dc, o2],
        [fi.keep],
        smem=1,
        out_specs=[ANY] * 2,
        scratch=group_scratch,
        us=5,
    )
    cross = Sum("cross", dp, (near, far, up, top), meta, keep, send)
    cross.step_a()
    last = fo.step_c([keep])
    last = fi.step_c([last])
    gain2, dx1, da, dqkv, ds1 = kernel(
        self_backward,
        "self_backward",
        [((1, width), F32), (tok, F32), (tok, BF16), ((rows, 3 * n), BF16), ((pairs, docs, size, 2 * size), BF16)],
        [dec_lengths, rel_table.T, x1, dx2, dq2, dq2_oth, cross_query, cross_query_oth, gain_cross, self_out]
        + [q1, k1, v1, lse1, rel_buckets],
        [last],
        smem=2,
        us=5,
    )
    last = ds1
    keep, send = kernel(
        self_grads,
        "self_grads",
        [(group, BF16)] * 2,
        [meta, h1, dqkv, da, o1],
        [last],
        smem=1,
        out_specs=[ANY] * 2,
        scratch=group_scratch,
        us=2.7,
    )
    own = Sum("self", dp, (near, far, up, top), meta, keep, send)
    own.step_a()
    sems = pltpu.SemaphoreType.DMA
    fo.target = (write_ffn_out, [(4, block, width)], [pltpu.VMEM((2, block, width), F32), sems((2,))])
    fi.target = (write_ffn_in, [ffn_in.shape], [pltpu.VMEM((2, width, block), F32), sems((2,))])
    cross.target = own.target = (
        write_attention,
        [(width, n)] * 3 + [(n, width)],
        [pltpu.VMEM((2, width, n), F32), sems((2, 2))],
    )
    last = fo.step_d([keep])
    last = fi.step_d([last])
    last = cross.step_b([last])
    part1 = kernel(
        self_input, "self_input", [(tok, BF16)], [dqkv, self_query, self_key, self_value], [last], us=1
    )[0]
    part1_oth = swap(part1)
    last = fo.step_e([part1])
    last = fi.step_e([last])
    gain1, dx = kernel(
        finish_input,
        "finish_input",
        [((1, width), F32), (tok, F32)],
        [x, part1, part1_oth, gain_self, dx1],
        [last],
        us=2,
    )
    last = dx
    small = kernel(
        small_grads,
        "small_grads",
        [((EXTRA, width // 2), F32)],
        [rel_buckets, ds1, gain1, gain2, gain3],
        [last],
        us=4,
    )[0]
    last = cross.step_c([small])
    last = fo.step_f([last])
    last = fi.step_f([last])
    last = own.step_b([last], small)
    enc_sent = kernel(
        enc_part,
        "enc_part",
        [((docs, half, width), BF16)],
        [dkv_oth, cross_key, cross_value],
        [last],
        grid=(docs,),
        in_specs=[kv_block, w_block, w_block],
        out_specs=[enc_block],
        us=3,
    )[0]
    enc_got = swap(enc_sent)
    last = cross.step_d([enc_sent])
    last = fo.step_g([last])
    last = fi.step_g([last])
    last = own.step_c([last, enc_got])
    last = cross.step_e([last])
    last = fi.step_h([last])
    last = own.step_d([last])
    last = cross.step_f([last])
    last = own.step_e([last])
    last = cross.step_g([last])
    last = own.step_f([last])
    last = fi.write1([last])
    last = cross.step_h([last])
    last = own.step_g([last])
    last = fo.step_h([last])
    enc_grad = kernel(
        finish_enc,
        "finish_enc",
        [((docs, half, width), BF16)],
        [dkv_own, cross_key, cross_value, enc_got],
        [last],
        grid=(docs,),
        in_specs=[kv_block, w_block, w_block, enc_block],
        out_specs=[enc_block],
        us=3,
    )[0]
    last = fi.write2([enc_grad])
    last = own.step_h([last])
    branch = kernel(
        ffn_branch,
        "ffn_branch",
        [(tok, BF16)],
        [meta_out, z_send, z_keep, ffn_out],
        [last],
        smem=1,
        grid=(4,),
        in_specs=[
            pl.BlockSpec((1, rows, block), lambda i, m: (jnp.minimum(i, 1), 0, 0)),
            pl.BlockSpec((1, rows, block), lambda i, m: (jnp.maximum(i - 2, 0), 0, 0)),
            wout_block,
        ],
        out_specs=[wide_tok],
        scratch=[pltpu.VMEM(tok, F32)],
        us=2.5,
    )[0]
    branch_oth = swap(branch)
    last = cross.write1([branch])
    last = fo.write1([last, branch_oth])
    y = kernel(finish_output, "finish_output", [(tok, BF16)], [x2, branch, branch_oth], [last], us=1)[0]
    last = cross.write2([y])
    last = own.write1([last])
    last = fo.write2([last])
    totals = kernel(
        write_small,
        "write_small",
        [((width,), F32)] * 3 + [((n // DH, NB), F32)],
        [own.small, own.got],
        [last],
        limit=16,
    )
    own.write2([totals[-1]])
    return (
        y.reshape(dec_input.shape),
        dx.reshape(dec_input.shape),
        enc_grad,
        totals[0],
        totals[1],
        totals[2],
        totals[3].T,
        *own.out,
        *cross.out,
        fi.out[0],
        fo.out[0].reshape(ffn_out.shape),
    )


def solution(mesh):
    dp = mesh.shape["dp"]
    split = jax.sharding.Mesh(mesh.devices.reshape(dp // 8, 2, 4, 2), ("top", "mid", "xy", "seq"))
    rows = ("top", "mid", "xy")
    col, row, doc = P(None, "seq"), P("seq", None), P(rows, None, None)
    in_specs = (
        (doc, P(rows, "seq", None), P(rows), P(rows), doc, doc)
        + (P(),) * 3
        + (col,) * 4
        + (row,)
        + (col,) * 3
        + (row, col, row)
    )
    out_specs = (
        (doc, doc, P(rows, "seq", None))
        + (P(),) * 3
        + (col,) * 4
        + (row,)
        + (col,) * 3
        + (row, col, row)
    )
    return jax.shard_map(
        functools.partial(shards, dp=dp),
        mesh=split,
        in_specs=in_specs,
        out_specs=out_specs,
        check_vma=False,
    )
```

```python
import functools

import jax
import jax.numpy as jnp
from jax import lax
from jax.experimental import pallas as pl
from jax.experimental.pallas import tpu as pltpu
from jax.sharding import PartitionSpec as P

DH = 64
NB = 32
PAIR = 2 * DH
SCALE = DH**-0.5
EPSILON = 1e-06
MASKED = -1e30
F32 = jnp.float32
BF16 = jnp.bfloat16
MIB = 1024 * 1024
SUM_LIMIT = 16


def dot(a, b):
    return lax.dot_general(a, b, (((1,), (0,)), ((), ())), preferred_element_type=F32)


def dot_nt(a, b):
    return lax.dot_general(a, b, (((1,), (1,)), ((), ())), preferred_element_type=F32)


def dot_tn(a, b):
    return lax.dot_general(a, b, (((0,), (0,)), ((), ())), preferred_element_type=F32)


VMEM = pl.BlockSpec(memory_space=pltpu.VMEM)
SMEM = pl.BlockSpec(memory_space=pltpu.SMEM)
ANY = pl.BlockSpec(memory_space=pl.ANY)


def kernel(body, name, outs, ins, after=(), smem=0, in_specs=None, out_specs=None, scratch=(), grid=None, limit=30, aliases=None, us=0.5, fetch=()):
    n_in, n_out, n_after, n_fetch = len(ins), len(outs), len(after), len(fetch)

    def wrapped(*refs):
        at = n_in + n_after
        sources, at = refs[at : at + n_fetch], at + n_fetch
        results, at = refs[at : at + n_out], at + n_out
        targets, at = refs[at : at + n_fetch], at + n_fetch
        rest, sems = (refs[at:-1], refs[-1]) if n_fetch else (refs[at:], None)
        copies = [pltpu.make_async_copy(src, to, sems.at[i]) for i, (src, to) in enumerate(zip(sources, targets))]

        def begin():
            for copy in copies:
                copy.start()

        def end():
            for copy in copies:
                copy.wait()

        if copies and grid is not None:
            pl.when(pl.program_id(0) == 0)(begin)
        else:
            begin()
        body(*refs[:n_in], *results, *rest)
        if copies and grid is not None:
            pl.when(pl.program_id(0) == grid[0] - 1)(end)
        else:
            end()

    in_specs = list(in_specs) if in_specs is not None else [VMEM] * (n_in - smem)
    out_specs = list(out_specs) if out_specs is not None else [VMEM] * len(outs)
    in_specs += [ANY] * (n_after + n_fetch)
    out_specs += [ANY] * n_fetch
    scratch = list(scratch) + ([pltpu.SemaphoreType.DMA((n_fetch,))] if n_fetch else [])
    params = pltpu.CompilerParams(vmem_limit_bytes=limit * MIB)
    cost = pl.CostEstimate(flops=int(us * 10e9), bytes_accessed=0, transcendentals=0)
    shapes = [pltpu.HBM(o[0], o[1]) if len(o) > 2 else jax.ShapeDtypeStruct(*o) for o in outs]
    shapes += [pltpu.VMEM(a.shape, a.dtype) for a in fetch]
    if grid is None:
        how = dict(in_specs=[SMEM] * smem + in_specs, out_specs=out_specs, scratch_shapes=scratch)
    else:
        how = dict(
            grid_spec=pltpu.PrefetchScalarGridSpec(
                num_scalar_prefetch=smem, grid=grid, in_specs=in_specs, out_specs=out_specs, scratch_shapes=scratch
            )
        )
    call = pl.pallas_call(
        wrapped,
        name=name,
        out_shape=shapes,
        compiler_params=params,
        cost_estimate=cost,
        input_output_aliases=aliases or {},
        **how,
    )
    return call(*ins, *after, *pin(*fetch))


def pin(*arrays):
    return [pltpu.with_memory_space_constraint(a, pltpu.HBM) for a in arrays]


def whole(shape):
    return pl.BlockSpec(shape, lambda *_: (0,) * len(shape))


def step_block(shape):
    return pl.BlockSpec(shape, lambda i, *_: (i,) + (0,) * (len(shape) - 1))


def inverse_rms(values):
    return lax.rsqrt(jnp.mean(values * values, axis=-1, keepdims=True) + EPSILON)


def row_of(gain):
    return gain[...].reshape(1, gain.shape[0])


def rms_backward(values, gain, grad):
    inverse = inverse_rms(values)
    scaled = grad * gain
    inner = jnp.mean(scaled * values, axis=-1, keepdims=True)
    grad_in = inverse * scaled - values * (inverse * inverse * inverse * inner)
    return grad_in, jnp.sum(grad * values * inverse, axis=0, keepdims=True)


def stack_pair(pair, scale=1.0):
    lanes = lax.broadcasted_iota(jnp.int32, (1, PAIR), 1)
    low = jnp.where(lanes < DH, scale, 0.0).astype(BF16)
    high = jnp.where(lanes < DH, 0.0, scale).astype(BF16)
    return jnp.concatenate([pair * low, pair * high], axis=0)


def join_pair(turned):
    n = turned.shape[1] // 2
    return jnp.concatenate([turned[:DH, :n], turned[DH:, n:]], axis=0).T


def fold(op, parts):
    return functools.reduce(op, parts)


def attend(q2, keys, values, biases):
    scores = [dot_nt(k, q2) + b for k, b in zip(keys, biases)]
    top = fold(jnp.maximum, [jnp.max(s, axis=0, keepdims=True) for s in scores])
    exps = [jnp.exp(s - top) for s in scores]
    total = fold(jnp.add, [jnp.sum(e, axis=0, keepdims=True) for e in exps])
    inv = 1.0 / total
    out = fold(jnp.add, [dot_tn(v, (e * inv).astype(BF16)) for e, v in zip(exps, values)])
    return out, top + jnp.log(total)


def attend_back(q2, do2, lse, keys, values, biases):
    probs = [jnp.exp(dot_nt(k, q2) + b - lse) for k, b in zip(keys, biases)]
    dv = [dot(p.astype(BF16), do2).astype(BF16) for p in probs]
    dp = [dot_nt(v, do2) for v in values]
    row = fold(jnp.add, [jnp.sum(p * g, axis=0, keepdims=True) for p, g in zip(probs, dp)])
    ds = [(p * (g - row)).astype(BF16) for p, g in zip(probs, dp)]
    dq = fold(jnp.add, [dot_tn(k, s) for s, k in zip(ds, keys)])
    dk = [dot(s, q2).astype(BF16) for s in ds]
    return dq, ds, dk, dv


def twice(a):
    return jnp.concatenate([a, a], axis=1)


def self_hidden(length, size):
    keys = lax.broadcasted_iota(jnp.int32, (size, size), 0)
    queries = lax.broadcasted_iota(jnp.int32, (size, size), 1)
    return jnp.where((keys <= queries) & (keys < length), 0.0, MASKED)


def cross_hidden(length, core, size, half):
    out = []
    for part in (core, 1 - core):
        pos = lax.broadcasted_iota(jnp.int32, (half, size), 0) + part * half
        out.append(twice(jnp.where(pos < length, 0.0, MASKED)))
    return out


def table_lines(table):
    lanes = lax.broadcasted_iota(jnp.int32, (1, 128), 1)
    lines = []
    for head in range(table.shape[0]):
        line = jnp.zeros((1, 128), F32)
        for b in range(NB):
            line = jnp.where(lanes == b, table[head, b], line)
        lines.append(line)
    return lines


def pair_bias(lines, index, pair, hidden):
    cols = []
    for head in (2 * pair, 2 * pair + 1):
        line = jnp.broadcast_to(lines[head], index.shape)
        cols.append(jnp.take_along_axis(line, index, axis=1, mode="promise_in_bounds") + hidden)
    return jnp.concatenate(cols, axis=1)


def self_forward(lens, table, x, gain, wq, wk, wv, wo, buckets, h_o, q_o, k_o, v_o, o_o, lse_o, part_o):
    docs, size = buckets.shape[0], buckets.shape[1]
    xf = x[...].astype(F32)
    h = (xf * inverse_rms(xf) * row_of(gain)).astype(BF16)
    h_o[...] = h
    q_o[...] = dot(h, wq[...]).astype(BF16)
    k_o[...] = dot(h, wk[...]).astype(BF16)
    v_o[...] = dot(h, wv[...]).astype(BF16)
    lines = table_lines(table)
    pairs = wq.shape[1] // PAIR
    for d in range(docs):
        rows = slice(d * size, (d + 1) * size)
        hidden = self_hidden(lens[d], size)
        index = buckets[d].T
        for p in range(pairs):
            cols = slice(p * PAIR, (p + 1) * PAIR)
            q2 = stack_pair(q_o[rows, cols], SCALE)
            bias = pair_bias(lines, index, p, hidden)
            out, lse = attend(q2, [k_o[rows, cols]], [v_o[rows, cols]], [bias])
            o_o[rows, cols] = join_pair(out).astype(BF16)
            at = d * pairs + p
            lse_o[at : at + 1, :] = lse
    part_o[...] = dot(o_o[...], wo[...]).astype(BF16)


def plus_parts(own, oth):
    return own[...].astype(F32) + oth[...].astype(F32)


def project_kv(e, wk, wv, kv_o):
    n = wk.shape[1]
    kv_o[0, :, :n] = dot(e[0], wk[...]).astype(BF16)
    kv_o[0, :, n:] = dot(e[0], wv[...]).astype(BF16)


def cross_forward(meta, lens, x, p_own, p_oth, gain, wq, wo, kv_own, kv_oth, x1_o, h_o, q_o, o_o, lse_o, part_o):
    docs, half, n = kv_own.shape[0], kv_own.shape[1], wq.shape[1]
    size = x.shape[0] // docs
    x1 = x[...].astype(F32) + plus_parts(p_own, p_oth)
    x1_o[...] = x1
    h = (x1 * inverse_rms(x1) * row_of(gain)).astype(BF16)
    h_o[...] = h
    q = dot(h, wq[...]).astype(BF16)
    q_o[...] = q
    for d in range(docs):
        rows = slice(d * size, (d + 1) * size)
        hidden = cross_hidden(lens[d], meta[2], size, half)
        out = []
        for p in range(n // PAIR):
            cols = slice(p * PAIR, (p + 1) * PAIR)
            vals = slice(n + p * PAIR, n + (p + 1) * PAIR)
            turned, lse = attend(
                stack_pair(q[rows, cols], SCALE),
                [kv_own[d, :, cols], kv_oth[d, :, cols]],
                [kv_own[d, :, vals], kv_oth[d, :, vals]],
                hidden,
            )
            out.append(join_pair(turned).astype(BF16))
            lse_o[d, p : p + 1, :] = lse
        o = jnp.concatenate(out, axis=1)
        o_o[rows, :] = o
        part_o[rows, :] = dot(o, wo[...]).astype(BF16)


GELU_C = 0.7978845608028654
GELU_A = 0.044715


def grid_slot(i):
    return jnp.where(i < 2, 2 * i + 1, 2 * (i - 2))


def ffn_act_grad(meta, dy, wout, dz_o):
    dz_o[0] = dot_nt(dy[...], wout[...])


def ffn_forward(meta, x1, p_own, p_oth, gain, win, dz, x2_o, z_send, z_keep, du_send, du_keep, part_o):
    x2 = x1[...] + plus_parts(p_own, p_oth)
    x2_o[...] = x2
    h = (x2 * inverse_rms(x2) * row_of(gain)).astype(BF16)
    half = h.shape[1] // 2
    du_send[2] = h[:, :half]
    du_send[3] = h[:, half:]
    block = win.shape[1] // 4
    total = 0.0
    for s in (1, 3, 0, 2):
        w = win[:, pl.ds(pl.multiple_of((meta[0] ^ s) * block, 128), block)]
        u = dot(h, w)
        u2 = u * u
        t = jnp.tanh(GELU_C * (u + GELU_A * (u * u2)))
        g = 0.5 * (1.0 + t)
        slope = g + (0.5 * GELU_C) * u * (1.0 - t * t) * (1.0 + 3.0 * GELU_A * u2)
        z = (u * g).astype(BF16)
        du = (dz[s] * slope).astype(BF16)
        z_slot = meta[0] ^ s ^ meta[3]

        @pl.when((z_slot & 1) == 1)
        def _(z=z, z_slot=z_slot):
            z_send[z_slot >> 1] = z

        @pl.when((z_slot & 1) == 0)
        def _(z=z, z_slot=z_slot):
            z_keep[z_slot >> 1] = z

        (du_send if s % 2 else du_keep)[s // 2] = du
        total = total + dot_nt(du, w)
    part_o[...] = total.astype(BF16)


def ffn_out_grads(meta, keep, got, dy, dy_got, keep_o, send_o):
    half = dy.shape[1] // 2
    for j, out in enumerate((keep_o, send_o)):
        w = (dot_tn(keep[j], dy[...]) + dot_tn(got[j], dy_got[...])).astype(BF16)
        r = w.shape[0] // 4
        for az in range(4):
            for k in range(2):
                out[meta[1] ^ az, k * r : (k + 1) * r] = w[az * r : (az + 1) * r, k * half : (k + 1) * half]


def ffn_in_grads(meta, keep, send, got, keep_o, send_o):
    for j, out in enumerate((keep_o, send_o)):
        for k in range(2):
            w = (dot_tn(send[2 + k], keep[j]) + dot_tn(got[2 + k], got[j])).astype(BF16)
            r = w.shape[0] // 2
            for az in range(2):
                out[meta[1] ^ (2 * k + az)] = w[az * r : (az + 1) * r]


def ffn_branch(meta, send, keep, wout, part_o, total):
    i = pl.program_id(0)
    branch = dot(jnp.where(i < 2, send[0], keep[0]), wout[...])

    @pl.when(i == 0)
    def _():
        total[...] = branch

    @pl.when((i > 0) & (i < 3))
    def _():
        total[...] += branch

    @pl.when(i == 3)
    def _():
        part_o[...] = (total[...] + branch).astype(BF16)


def finish_output(x2, p_own, p_oth, y_o):
    y_o[...] = (x2[...] + (p_own[...].astype(F32) + p_oth[...].astype(F32))).astype(BF16)


def cross_backward(meta, lens, x2, p_own, p_oth, gain, dy, wo, wq, q, lse, kv_own, kv_oth, gain_o, dx2_o, dc_o, dq_o, part_o, dkv_own, dkv_oth):
    docs, half, n = kv_own.shape[0], kv_own.shape[1], q.shape[1]
    size = x2.shape[0] // docs
    dv, gain_grad = rms_backward(x2[...], row_of(gain), plus_parts(p_own, p_oth))
    gain_o[...] = gain_grad
    dx2 = dy[...].astype(F32) + dv
    dx2_o[...] = dx2
    dc = dx2.astype(BF16)
    dc_o[...] = dc
    do = dot_nt(dc, wo[...]).astype(BF16)
    for d in range(docs):
        rows = slice(d * size, (d + 1) * size)
        hidden = cross_hidden(lens[d], meta[2], size, half)
        out = []
        for p in range(n // PAIR):
            cols = slice(p * PAIR, (p + 1) * PAIR)
            vals = slice(n + p * PAIR, n + (p + 1) * PAIR)
            dq, _, dk, dv = attend_back(
                stack_pair(q[rows, cols], SCALE),
                stack_pair(do[rows, cols]),
                lse[d, p : p + 1, :],
                [kv_own[d, :, cols], kv_oth[d, :, cols]],
                [kv_own[d, :, vals], kv_oth[d, :, vals]],
                hidden,
            )
            out.append((join_pair(dq) * SCALE).astype(BF16))
            dkv_own[d, :, cols], dkv_oth[d, :, cols] = dk
            dkv_own[d, :, vals], dkv_oth[d, :, vals] = dv
        dq = jnp.concatenate(out, axis=1)
        dq_o[rows, :] = dq
        part_o[rows, :] = dot_nt(dq, wq[...]).astype(BF16)


def store_tensors(tensors, zq, scratch):
    for t, quarters in enumerate(tensors):
        for az, quarter in enumerate(quarters):
            scratch[t, zq ^ az] = quarter.astype(BF16)


def tall(a):
    r = a.shape[0] // 4
    return [a[z * r : (z + 1) * r] for z in range(4)]


def wide(a):
    r, c = a.shape[0] // 2, a.shape[1] // 2
    return [a[(z % 2) * r : (z % 2 + 1) * r, (z // 2) * c : (z // 2 + 1) * c] for z in range(4)]


def send_blocks(quad, scratch, keep, send, sem):
    copies = []
    for s in range(4):
        ref = keep if s % 2 == 0 else send
        copies.append(pltpu.make_async_copy(scratch.at[quad ^ s], ref.at[s // 2], sem.at[s]))
    for c in copies:
        c.start()
    for c in copies:
        c.wait()


def cross_grads(meta, h, dq, e_own, e_oth, dkv_own, dkv_oth, dc, o, keep, send, scratch, sem):
    n = dq.shape[1]
    kv = dot_tn(e_own[...], dkv_own[...]) + dot_tn(e_oth[...], dkv_oth[...])
    gq = dot_tn(h[...], dq[...])
    go = dot_tn(o[...], dc[...])
    store_tensors([tall(gq), tall(kv[:, :n]), tall(kv[:, n:]), wide(go)], meta[1], scratch)
    send_blocks(meta[0], scratch, keep, send, sem)


def self_backward(lens, table, x1, dx2, p_own, p_oth, gain, wo, q, k, v, lse, buckets, gain_o, dx1_o, da_o, dqkv_o, ds_o):
    docs, size = buckets.shape[0], buckets.shape[1]
    n = q.shape[1]
    dv, gain_grad = rms_backward(x1[...], row_of(gain), plus_parts(p_own, p_oth))
    gain_o[...] = gain_grad
    dx1 = dx2[...] + dv
    dx1_o[...] = dx1
    da = dx1.astype(BF16)
    da_o[...] = da
    do = dot_nt(da, wo[...]).astype(BF16)
    lines = table_lines(table)
    pairs = n // PAIR
    for d in range(docs):
        rows = slice(d * size, (d + 1) * size)
        hidden = self_hidden(lens[d], size)
        index = buckets[d].T
        for p in range(pairs):
            cols = slice(p * PAIR, (p + 1) * PAIR)
            at = d * pairs + p
            dq, ds, dk, dvv = attend_back(
                stack_pair(q[rows, cols], SCALE),
                stack_pair(do[rows, cols]),
                lse[at : at + 1, :],
                [k[rows, cols]],
                [v[rows, cols]],
                [pair_bias(lines, index, p, hidden)],
            )
            dqkv_o[rows, cols] = (join_pair(dq) * SCALE).astype(BF16)
            dqkv_o[rows, n + p * PAIR : n + (p + 1) * PAIR] = dk[0]
            dqkv_o[rows, 2 * n + p * PAIR : 2 * n + (p + 1) * PAIR] = dvv[0]
            ds_o[p, d] = ds[0]


def self_input(dqkv, wq, wk, wv, part_o):
    n = wq.shape[1]
    part_o[...] = (
        dot_nt(dqkv[:, :n], wq[...])
        + dot_nt(dqkv[:, n : 2 * n], wk[...])
        + dot_nt(dqkv[:, 2 * n :], wv[...])
    ).astype(BF16)


def self_grads(meta, h, dqkv, da, o, keep, send, scratch, sem):
    n = o.shape[1]
    g = dot_tn(h[...], dqkv[...])
    go = dot_tn(o[...], da[...])
    store_tensors([tall(g[:, t * n : (t + 1) * n]) for t in range(3)] + [wide(go)], meta[1], scratch)
    send_blocks(meta[0], scratch, keep, send, sem)


def finish_input(x, p_own, p_oth, gain, dx1, gain_o, dx_o):
    dv, gain_grad = rms_backward(
        x[...].astype(F32), row_of(gain), p_own[...].astype(F32) + p_oth[...].astype(F32)
    )
    gain_o[...] = gain_grad
    dx_o[...] = dx1[...] + dv


def small_grads(buckets, ds, gain1, gain2, gain3, out):
    docs, size = buckets.shape[0], buckets.shape[1]
    pairs = ds.shape[0]
    half = out.shape[1]
    lanes = lax.broadcasted_iota(jnp.int32, (8, 128), 1)
    subs = lax.broadcasted_iota(jnp.int32, (8, 128), 0)
    out[...] = jnp.zeros(out.shape, F32)
    for j, gain in enumerate((gain1, gain2, gain3)):
        for k in range(2):
            out[2 * j + k : 2 * j + k + 1, :] = gain[:, k * half : (k + 1) * half]
    table = jnp.zeros((8, 128), F32)
    index = [twice(buckets[d].T) for d in range(docs)]
    for p in range(pairs):
        for b in range(NB):
            line = fold(
                jnp.add,
                [
                    jnp.sum(jnp.where(index[d] == b, ds[p, d].astype(F32), 0.0), axis=0, keepdims=True)
                    for d in range(docs)
                ],
            )
            for j in range(2):
                total = jnp.sum(line[:, j * size : (j + 1) * size], axis=1, keepdims=True)
                table = jnp.where((subs == 2 * p + j) & (lanes == b), total, table)
    out[8:16, :128] = table


def enc_part(dkv, wk, wv, out):
    n = wk.shape[1]
    out[0] = (dot_nt(dkv[0, :, :n], wk[...]) + dot_nt(dkv[0, :, n:], wv[...])).astype(BF16)


def finish_enc(dkv, wk, wv, got, out):
    n = wk.shape[1]
    own = dot_nt(dkv[0, :, :n], wk[...]) + dot_nt(dkv[0, :, n:], wv[...])
    out[0] = (own + got[0].astype(F32)).astype(BF16)


def add_quads(keep, got, keep_o, send_o):
    keep_o[...] = keep[0] + got[0]
    send_o[...] = keep[1] + got[1]


EXTRA = 16


def add_quads(keep, got, keep_o, send_o):
    keep_o[...] = keep[0] + got[0]
    send_o[...] = keep[1] + got[1]


def add_pieces(keep, got, keep_o, send_o):
    for j in range(2):
        keep_o[j] = keep[2 * j] + got[2 * j]
        send_o[j] = keep[2 * j + 1] + got[2 * j + 1]


def add_pair(keep, got, keep_o, send_o):
    keep_o[...] = keep[0] + got[0]
    send_o[...] = keep[1] + got[1]


def add_shard(keep, got, out):
    out[...] = keep[...] + got[...]


def put_two(a, b, out):
    out[0] = a[...]
    out[1] = b[...]


def join_pieces(meta, own, got, out):
    r = own.shape[1]
    for j in range(2):
        out[pl.ds(pl.multiple_of((meta[1] ^ (2 * j)) * r, r), r), :] = own[j]
        out[pl.ds(pl.multiple_of((meta[1] ^ (2 * j + 1)) * r, r), r), :] = got[j]


def put_blocks(a, b, out):
    r = a.shape[0]
    out[:r] = a[...]
    out[r:] = b[...]


def plus_small(own, got):
    return (own[...].astype(BF16).astype(F32) + got.astype(F32)).astype(BF16)


def self_pieces(keep, got, small, keep_o, send_o):
    r = keep.shape[1]
    for j in range(2):
        keep_o[j] = keep[2 * j] + got[2 * j]
        send_o[j * r : (j + 1) * r] = keep[2 * j + 1] + got[2 * j + 1]
    send_o[2 * r :] = small[...].astype(BF16)


def self_pair(keep, got, small, keep_o, send_o, small_o):
    r = keep.shape[1]
    total = plus_small(small, got[2 * r :])
    small_o[...] = total
    keep_o[...] = keep[0] + got[:r]
    send_o[:r] = keep[1] + got[r : 2 * r]
    send_o[r:] = total


def self_shard(keep, got, small, out, small_o):
    r = keep.shape[0]
    out[...] = keep[...] + got[:r]
    small_o[...] = plus_small(small, got[r:])


def self_join(meta, own, got, small, out):
    join_pieces(meta, own, got, out)
    out[4 * own.shape[1] :] = small[...]


def self_blocks(a, b, small, out):
    r = a.shape[0] - EXTRA
    out[:r] = a[:r]
    out[r : 2 * r] = b[:r]
    out[2 * r :] = plus_small(small, b[r:])


def write_small(own, got, gain1_o, gain2_o, gain3_o, table_o):
    at = got.shape[0] - EXTRA
    total = own[at:, :].astype(F32) + got[at:, :].astype(F32)
    for j, gain in enumerate((gain1_o, gain2_o, gain3_o)):
        gain[...] = jnp.concatenate([total[2 * j : 2 * j + 1], total[2 * j + 1 : 2 * j + 2]], axis=1).reshape(gain.shape)
    heads, buckets = table_o.shape
    table_o[...] = total[8 : 8 + heads, :buckets]


def write_ffn_out(slots, meta, both, *refs):
    out, done, scratch, sem = refs[-4:]
    done[...] = jnp.zeros(done.shape, F32)
    r, c = scratch.shape[1] // 4, scratch.shape[2] // 2
    copies = []
    for i, s in enumerate(slots):
        for z in range(4):
            for j in range(2):
                at = (8 * i + 2 * z + j) * r
                scratch[i, z * r : (z + 1) * r, j * c : (j + 1) * c] = both[at : at + r].astype(F32)
        copies.append(pltpu.make_async_copy(scratch.at[i], out.at[meta[0] ^ s], sem.at[i]))
        copies[-1].start()
    for copy in copies:
        copy.wait()


def write_ffn_in(slots, meta, both, *refs):
    out, done, scratch, sem = refs[-4:]
    done[...] = jnp.zeros(done.shape, F32)
    r, c = scratch.shape[1:]
    copies = []
    for i, s in enumerate(slots):
        scratch[i] = both[i * r : (i + 1) * r].astype(F32)
        cols = pl.ds(pl.multiple_of((meta[0] ^ s) * c, 128), c)
        copies.append(pltpu.make_async_copy(scratch.at[i], out.at[:, cols], sem.at[i]))
        copies[-1].start()
    for copy in copies:
        copy.wait()


def write_attention(slots, meta, both, *refs):
    q_o, k_o, v_o, o_o, done, scratch, sem = refs[-7:]
    done[...] = jnp.zeros(done.shape, F32)
    rows, c = scratch.shape[1:]
    m = rows // 2

    def copies_of(i, t):
        if t < 3:
            return [pltpu.make_async_copy(scratch.at[i], (q_o, k_o, v_o)[t], sem.at[i, 0])]
        return [
            pltpu.make_async_copy(
                scratch.at[i, pl.ds(j * m, m)], o_o.at[:, pl.ds(j * c, c)], sem.at[i, j]
            )
            for j in range(2)
        ]

    for i, s in enumerate(slots):
        scratch[i] = both[i * rows : (i + 1) * rows].astype(F32)
        for t in range(4):

            @pl.when((meta[0] ^ s) == t)
            def _(i=i, t=t):
                for copy in copies_of(i, t):
                    copy.start()

    for i, s in enumerate(slots):
        for t in range(4):

            @pl.when((meta[0] ^ s) == t)
            def _(i=i, t=t):
                for copy in copies_of(i, t):
                    copy.wait()


class Sum:
    def __init__(self, name, dp, masks, meta, keep=None, send=None):
        self.name, self.dp, self.masks, self.meta = name, dp, masks, meta
        self.keep, self.send, self.small = keep, send, None

    def move(self, a, mask, what):
        pairs = [(2 * i + c, 2 * (i ^ mask[c]) + c) for i in range(self.dp) for c in range(2)]
        with jax.named_scope(f"{self.name}_{what}"):
            return lax.ppermute(a, ("top", "mid", "xy", "seq"), pairs)

    def exchange(self, a, k, what):
        self.got = self.move(a, self.masks[k], what)

    def call(self, body, outs, ins, after, **kw):
        name = f"{self.name}_{body.__name__}" if hasattr(body, "__name__") else f"{self.name}_write"
        return kernel(body, name, outs, ins, [after], **{"limit": SUM_LIMIT, **kw})

    def step_a(self):
        self.exchange(self.send, 0, "sum_a")

    def step_b(self, after):
        z, r, c = self.keep.shape[1:]
        self.keep, send = self.call(add_quads, [((z, r, c), BF16)] * 2, [self.keep, self.got], after)
        self.exchange(send, 1, "sum_b")
        return self.keep

    def step_c(self, after, small=None):
        z, r, c = self.keep.shape
        ins, half = [self.keep, self.got], ((2, r, c), BF16)
        self.small = small
        if small is None:
            self.keep, send = self.call(add_pieces, [half] * 2, ins, after)
        else:
            self.keep, send = self.call(self_pieces, [half, ((2 * r + EXTRA, c), BF16)], [*ins, small], after)
        self.exchange(send, 2, "sum_c")
        return self.keep

    def step_d(self, after):
        z, r, c = self.keep.shape
        ins, one = [self.keep, self.got], ((r, c), BF16)
        if self.small is None:
            self.keep, send = self.call(add_pair, [one] * 2, ins, after)
        else:
            self.keep, send, self.small = self.call(
                self_pair,
                [one, ((r + EXTRA, c), BF16), (self.small.shape, BF16)],
                [*ins, self.small],
                after,
            )
        self.exchange(send, 3, "sum_d")
        return self.keep

    def step_e(self, after):
        ins, one = [self.keep, self.got], (self.keep.shape, BF16)
        if self.small is None:
            self.shard = self.call(add_shard, [one], ins, after)[0]
        else:
            self.shard, self.small = self.call(
                self_shard, [one, (self.small.shape, BF16)], [*ins, self.small], after
            )
        step = 16
        while step < self.dp:
            rest = (step, step)
            self.shard = self.shard + self.move(self.shard, rest, "sum_rest")
            if self.small is not None:
                self.small = self.small + self.move(self.small, rest, "sum_rest")
            step *= 2
        self.exchange(self.shard, 3, "gather_d")
        return self.shard

    def step_f(self, after):
        shape = (2,) + self.shard.shape
        self.two = self.call(put_two, [(shape, BF16)], [self.shard, self.got], after)[0]
        self.exchange(self.two, 2, "gather_c")
        return self.two

    def step_g(self, after):
        r, c = self.shard.shape
        ins = [self.meta, self.two, self.got]
        if self.small is None:
            self.block = self.call(join_pieces, [((4 * r, c), BF16)], ins, after, smem=1)[0]
        else:
            self.block = self.call(self_join, [((4 * r + EXTRA, c), BF16)], [*ins, self.small], after, smem=1)[0]
        self.exchange(self.block, 1, "gather_b")
        return self.block

    def step_h(self, after):
        r, c = self.block.shape
        ins = [self.block, self.got]
        if self.small is None:
            self.near = self.call(put_blocks, [((2 * r, c), BF16)], ins, after)[0]
        else:
            self.near = self.call(self_blocks, [((2 * r - EXTRA, c), BF16)], [*ins, self.small], after)[0]
        self.exchange(self.near, 0, "gather_a")
        return self.near

    def write(self, slots, both, into, after):
        body, outs, scratch = self.target
        into = list(into)
        *self.out, done = self.call(
            functools.partial(body, slots),
            [(o, F32) for o in outs] + [((8, 128), F32)],
            [self.meta, both, *into],
            after,
            smem=1,
            in_specs=[VMEM] + [ANY] * len(into),
            out_specs=[ANY] * len(outs) + [VMEM],
            scratch=scratch,
            aliases={2 + i: i for i in range(len(into))},
            limit=30,
            us=0.1,
        )
        return done

    def write1(self, after):
        return self.write((0, 2), self.near, (), after)

    def write2(self, after):
        return self.write((1, 3), self.got, self.out, after)


def shards(
    dec_input,
    enc_states,
    dec_lengths,
    enc_lengths,
    rel_buckets,
    out_grad,
    gain_self,
    gain_cross,
    gain_ffn,
    rel_table,
    self_query,
    self_key,
    self_value,
    self_out,
    cross_query,
    cross_key,
    cross_value,
    cross_out,
    ffn_in,
    ffn_out,
    *,
    dp,
):
    docs, size, width = dec_input.shape
    half = enc_states.shape[1]
    rows = docs * size
    n = self_query.shape[1]
    hidden = ffn_in.shape[1]
    block = hidden // 4
    pairs = n // PAIR
    index, core = lax.axis_index(("top", "mid", "xy")), lax.axis_index("seq")
    bits = [(index >> k) & 1 for k in range(4)]
    one, two = jnp.where(core == 0, bits[0], bits[1]), jnp.where(core == 0, bits[1], bits[0])
    near, far, up, top = (1, 2), (2, 1), (4, 4), (8, 8)
    quad, quad_out = one + 2 * two, bits[2] + 2 * one
    meta = jnp.stack([quad, bits[2] + 2 * bits[3], core, quad_out, two + 2 * bits[3]]).astype(jnp.int32)
    meta_out = meta[3:]

    def swap(a):
        return lax.ppermute(a, "seq", [(0, 1), (1, 0)])

    dec_lengths, enc_lengths, table = pin(dec_lengths, enc_lengths, rel_table.T)
    gain_self, gain_cross, gain_ffn = pin(gain_self, gain_cross, gain_ffn)
    buckets = pin(rel_buckets)[0]
    x = dec_input.reshape(rows, width)
    dy = out_grad.reshape(rows, width)
    fo = Sum("ffn_out", dp, (up, near, far, top), meta_out)
    fi = Sum("ffn_in", dp, (near, far, up, top), meta)
    dy_got = fo.move(dy, up, "tokens")
    enc_oth = swap(enc_states)

    tok = (rows, width)
    head = (rows, n)
    kept = "kept"
    h1, q1, k1, v1, o1, lse1, self_part = kernel(
        self_forward,
        "self_forward",
        [(tok, BF16, kept)] + [(head, BF16, kept)] * 4 + [((docs * pairs, 2 * size), F32), (tok, BF16)],
        [dec_lengths, table, *pin(x), gain_self, *pin(self_query, self_key, self_value, self_out), buckets],
        smem=2,
        us=2.7,
    )
    self_part_oth = swap(self_part)
    kv_shape = (docs, half, 2 * n)
    kv_block = step_block((1, half, 2 * n))
    enc_block = step_block((1, half, width))
    w_block = whole((width, n))
    project = dict(grid=(docs,), in_specs=[enc_block, w_block, w_block], out_specs=[kv_block], us=2)
    kv_own, query_near, out_near = kernel(
        project_kv,
        "project_own",
        [(kv_shape, BF16)],
        pin(enc_states, cross_key, cross_value),
        [self_part],
        fetch=[cross_query, cross_out],
        **project,
    )
    kv_oth, ffn_out_near, dy_near = kernel(
        project_kv,
        "project_oth",
        [(kv_shape, BF16)],
        [enc_oth, *pin(cross_key, cross_value)],
        [kv_own],
        fetch=[ffn_out, dy],
        **project,
    )
    wide_tok, wide_head, wo_block = whole(tok), whole(head), whole((n, width))
    gain_block = whole((width,))
    lse_shape = (docs, pairs, 2 * size)
    lse_block = step_block((1, pairs, 2 * size))
    head_block = step_block((size, n))
    tok_block = step_block((size, width))
    x1, h2, q2, o2, lse2, cross_part, ffn_in_near = kernel(
        cross_forward,
        "cross_forward",
        [(tok, F32), (tok, BF16, kept), (head, BF16, kept), (head, BF16, kept), (lse_shape, F32), (tok, BF16)],
        [meta, enc_lengths, *pin(x), self_part, self_part_oth, gain_cross, query_near, out_near, kv_own, kv_oth],
        smem=2,
        fetch=[ffn_in],
        us=8,
    )
    cross_part_oth = swap(cross_part)
    group = (2, 4, width // 4, n)
    act = (4, rows, block)
    act_block = pl.BlockSpec((1, rows, block), lambda i, m: (grid_slot(i), 0, 0))
    win_block = pl.BlockSpec((width, block), lambda i, m: (0, m[0] ^ grid_slot(i)))
    wout_block = pl.BlockSpec((block, width), lambda i, m: (m[0] ^ grid_slot(i), 0))
    dz = kernel(
        ffn_act_grad,
        "ffn_act_grad",
        [(act, F32)],
        [meta, dy_near, ffn_out_near],
        [cross_part],
        smem=1,
        grid=(4,),
        in_specs=[wide_tok, wout_block],
        out_specs=[act_block],
        us=2.5,
    )[0]
    pair_act, sent = (2, rows, block), (4, rows, block)
    x2, z_send, z_keep, du_send, du_keep, part = kernel(
        ffn_forward,
        "ffn_forward",
        [(tok, F32), (pair_act, BF16), (pair_act, BF16), (sent, BF16), (pair_act, BF16), (tok, BF16)],
        [meta, x1, cross_part, cross_part_oth, gain_ffn, ffn_in_near, dz],
        [dy_got],
        smem=1,
        us=8,
    )
    z_got = fo.move(z_send, up, "sum_a")
    du_got = fi.move(du_send, near, "sum_a")
    part_oth = swap(part)
    gain3, dx2, dc, dq2, query_part, dkv_own, dkv_oth = kernel(
        cross_backward,
        "cross_backward",
        [((1, width), F32), (tok, F32), (tok, BF16), (head, BF16), (tok, BF16)] + [(kv_shape, BF16)] * 2,
        [meta, enc_lengths, x2, part, part_oth, gain_ffn, dy, cross_out, cross_query, q2, lse2, kv_own, kv_oth],
        smem=2,
        us=10,
    )
    query_part_oth = swap(query_part)
    piece = group[1:]
    group_scratch = [pltpu.VMEM((4,) + group[1:], BF16), pltpu.SemaphoreType.DMA((4,))]
    enc_rows = (docs * half, width)
    cross = Sum("cross", dp, (near, far, up, top), meta)
    own = Sum("self", dp, (near, far, up, top), meta)

    def run_out_grads(last):
        fo.keep, send = kernel(
            ffn_out_grads, "ffn_out_grads", [(piece, BF16)] * 2, [meta_out, z_keep, z_got, dy, dy_got], [last], smem=1, us=3
        )
        fo.exchange(send, 1, "sum_b")
        return fo.keep

    def run_in_grads(last):
        fi.keep, send = kernel(
            ffn_in_grads, "ffn_in_grads", [(piece, BF16)] * 2, [meta, du_keep, du_send, du_got], [last], smem=1, us=3
        )
        fi.exchange(send, 1, "sum_b")
        return fi.keep

    def run_cross_grads(last):
        cross.keep, cross.send = kernel(
            cross_grads,
            "cross_grads",
            [(group, BF16)] * 2,
            [meta, h2, dq2, enc_states.reshape(enc_rows), enc_oth.reshape(enc_rows)]
            + [dkv_own.reshape(enc_rows), dkv_oth.reshape(enc_rows), dc, o2],
            [last],
            smem=1,
            out_specs=[ANY] * 2,
            scratch=group_scratch,
            us=5,
        )
        cross.step_a()
        return cross.keep

    sems = pltpu.SemaphoreType.DMA
    fo.target = (write_ffn_out, [(4, block, width)], [pltpu.VMEM((2, block, width), F32), sems((2,))])
    fi.target = (write_ffn_in, [ffn_in.shape], [pltpu.VMEM((2, width, block), F32), sems((2,))])
    cross.target = own.target = (
        write_attention,
        [(width, n)] * 3 + [(n, width)],
        [pltpu.VMEM((2, width, n), F32), sems((2, 2))],
    )

    def run_self_backward(last):
        nonlocal gain2, dx1, da, dqkv, ds1
        gain2, dx1, da, dqkv, ds1 = kernel(
            self_backward,
            "self_backward",
            [((1, width), F32), (tok, F32), (tok, BF16), ((rows, 3 * n), BF16), ((pairs, docs, size, 2 * size), BF16)],
            [dec_lengths, table, x1, dx2, query_part, query_part_oth, gain_cross, self_out]
            + [q1, k1, v1, lse1, buckets],
            [last],
            smem=2,
            us=5,
        )
        return ds1

    def run_self_grads(last):
        own.keep, own.send = kernel(
            self_grads,
            "self_grads",
            [(group, BF16)] * 2,
            [meta, h1, dqkv, da, o1],
            [last],
            smem=1,
            out_specs=[ANY] * 2,
            scratch=group_scratch,
            us=2.7,
        )
        own.step_a()
        return own.keep

    def run_self_input(last):
        nonlocal part1, part1_oth
        part1 = kernel(
            self_input, "self_input", [(tok, BF16)], [dqkv, self_query, self_key, self_value], [last], us=0.1
        )[0]
        part1_oth = swap(part1)
        return part1

    def run_enc_part(last):
        nonlocal enc_sent, enc_got
        enc_sent = kernel(
            enc_part,
            "enc_part",
            [((docs, half, width), BF16)],
            [dkv_oth, cross_key, cross_value],
            [last],
            grid=(docs,),
            in_specs=[kv_block, w_block, w_block],
            out_specs=[enc_block],
            us=0.1,
        )[0]
        enc_got = swap(enc_sent)
        return enc_sent

    def run_finish_input(last):
        nonlocal gain1, dx
        gain1, dx = kernel(
            finish_input,
            "finish_input",
            [((1, width), F32), (tok, F32)],
            [x, part1, part1_oth, gain_self, dx1],
            [last],
            us=0.1,
        )
        return dx

    def run_small(last):
        nonlocal small
        small = kernel(
            small_grads,
            "small_grads",
            [((EXTRA, width // 2), F32)],
            [buckets, ds1, gain1, gain2, gain3],
            [last],
            us=0.1,
        )[0]
        return small

    def run_finish_enc(last):
        nonlocal enc_grad
        enc_grad = kernel(
            finish_enc,
            "finish_enc",
            [((docs, half, width), BF16)],
            [dkv_own, cross_key, cross_value, enc_got],
            [last],
            grid=(docs,),
            in_specs=[kv_block, w_block, w_block, enc_block],
            out_specs=[enc_block],
            us=0.1,
        )[0]
        return enc_grad

    def run_branch(last):
        nonlocal branch, branch_oth
        branch = kernel(
            ffn_branch,
            "ffn_branch",
            [(tok, BF16)],
            [meta_out, z_send, z_keep, ffn_out],
            [last],
            smem=1,
            grid=(4,),
            in_specs=[
                pl.BlockSpec((1, rows, block), lambda i, m: (jnp.minimum(i, 1), 0, 0)),
                pl.BlockSpec((1, rows, block), lambda i, m: (jnp.maximum(i - 2, 0), 0, 0)),
                wout_block,
            ],
            out_specs=[wide_tok],
            scratch=[pltpu.VMEM(tok, F32)],
            us=0.1,
        )[0]
        branch_oth = swap(branch)
        return branch

    def run_finish_output(last):
        nonlocal y
        y = kernel(finish_output, "finish_output", [(tok, BF16)], [x2, branch, branch_oth], [last], us=0.1)[0]
        return y

    gain2 = dx1 = da = dqkv = ds1 = part1 = part1_oth = enc_sent = enc_got = None
    gain1 = dx = small = enc_grad = branch = branch_oth = y = None
    steps = (
        (run_enc_part, run_in_grads, run_cross_grads, run_out_grads, fi.step_c, run_self_backward)
        + (run_finish_enc, fi.step_d, fo.step_c, cross.step_b, fi.step_e, run_self_grads, fo.step_d)
        + (run_self_input, cross.step_c, fi.step_f, run_finish_input, run_small, own.step_b, fo.step_e)
        + (cross.step_d, fi.step_g, lambda last: own.step_c(last, small), fo.step_f, cross.step_e)
        + (fi.step_h, fi.write1, own.step_d, cross.step_f, fo.step_g, own.step_e, cross.step_g, own.step_f)
        + (run_branch, fi.write2, cross.step_h, own.step_g, fo.step_h, run_finish_output, own.step_h)
        + (fo.write1, own.write1, cross.write1, cross.write2, fo.write2)
    )
    last = dq2
    for step in steps:
        last = step(last)
    totals = kernel(
        write_small,
        "write_small",
        [((width,), F32)] * 3 + [((n // DH, NB), F32)],
        [own.near, own.got],
        [last],
        limit=16,
    )
    own.write2(totals[-1])
    return (
        y.reshape(dec_input.shape),
        dx.reshape(dec_input.shape),
        enc_grad,
        totals[0],
        totals[1],
        totals[2],
        totals[3].T,
        *own.out,
        *cross.out,
        fi.out[0],
        fo.out[0].reshape(ffn_out.shape),
    )


def solution(mesh):
    dp = mesh.shape["dp"]
    split = jax.sharding.Mesh(mesh.devices.reshape(dp // 8, 2, 4, 2), ("top", "mid", "xy", "seq"))
    rows = ("top", "mid", "xy")
    col, row, doc = P(None, "seq"), P("seq", None), P(rows, None, None)
    in_specs = (
        (doc, P(rows, "seq", None), P(rows), P(rows), doc, doc)
        + (P(),) * 3
        + (col,) * 4
        + (row,)
        + (col,) * 3
        + (row, col, row)
    )
    out_specs = (
        (doc, doc, P(rows, "seq", None))
        + (P(),) * 3
        + (col,) * 4
        + (row,)
        + (col,) * 3
        + (row, col, row)
    )
    return jax.shard_map(
        functools.partial(shards, dp=dp),
        mesh=split,
        in_specs=in_specs,
        out_specs=out_specs,
        check_vma=False,
    )
```

```python
import functools

import jax
import jax.numpy as jnp
from jax import lax
from jax.experimental import pallas as pl
from jax.experimental.pallas import tpu as pltpu
from jax.sharding import PartitionSpec as P

DH = 64
NB = 32
PAIR = 2 * DH
SCALE = DH**-0.5
EPSILON = 1e-06
MASKED = -1e30
F32 = jnp.float32
BF16 = jnp.bfloat16
MIB = 1024 * 1024
SUM_LIMIT = 16


def dot(a, b):
    return lax.dot_general(a, b, (((1,), (0,)), ((), ())), preferred_element_type=F32)


def dot_nt(a, b):
    return lax.dot_general(a, b, (((1,), (1,)), ((), ())), preferred_element_type=F32)


def dot_tn(a, b):
    return lax.dot_general(a, b, (((0,), (0,)), ((), ())), preferred_element_type=F32)


VMEM = pl.BlockSpec(memory_space=pltpu.VMEM)
SMEM = pl.BlockSpec(memory_space=pltpu.SMEM)
ANY = pl.BlockSpec(memory_space=pl.ANY)


def kernel(body, name, outs, ins, after=(), smem=0, in_specs=None, out_specs=None, scratch=(), grid=None, limit=30, aliases=None, us=0.5, fetch=()):
    n_in, n_out, n_after, n_fetch = len(ins), len(outs), len(after), len(fetch)

    def wrapped(*refs):
        at = n_in + n_after
        sources, at = refs[at : at + n_fetch], at + n_fetch
        results, at = refs[at : at + n_out], at + n_out
        targets, at = refs[at : at + n_fetch], at + n_fetch
        rest, sems = (refs[at:-1], refs[-1]) if n_fetch else (refs[at:], None)
        copies = [pltpu.make_async_copy(src, to, sems.at[i]) for i, (src, to) in enumerate(zip(sources, targets))]

        def begin():
            for copy in copies:
                copy.start()

        def end():
            for copy in copies:
                copy.wait()

        if copies and grid is not None:
            pl.when(pl.program_id(0) == 0)(begin)
        else:
            begin()
        body(*refs[:n_in], *results, *rest)
        if copies and grid is not None:
            pl.when(pl.program_id(0) == grid[0] - 1)(end)
        else:
            end()

    in_specs = list(in_specs) if in_specs is not None else [VMEM] * (n_in - smem)
    out_specs = list(out_specs) if out_specs is not None else [VMEM] * len(outs)
    in_specs += [ANY] * (n_after + n_fetch)
    out_specs += [ANY] * n_fetch
    scratch = list(scratch) + ([pltpu.SemaphoreType.DMA((n_fetch,))] if n_fetch else [])
    params = pltpu.CompilerParams(vmem_limit_bytes=limit * MIB)
    cost = pl.CostEstimate(flops=int(us * 10e9), bytes_accessed=0, transcendentals=0)
    shapes = [pltpu.HBM(o[0], o[1]) if len(o) > 2 else jax.ShapeDtypeStruct(*o) for o in outs]
    shapes += [pltpu.VMEM(a.shape, a.dtype) for a in fetch]
    if grid is None:
        how = dict(in_specs=[SMEM] * smem + in_specs, out_specs=out_specs, scratch_shapes=scratch)
    else:
        how = dict(
            grid_spec=pltpu.PrefetchScalarGridSpec(
                num_scalar_prefetch=smem, grid=grid, in_specs=in_specs, out_specs=out_specs, scratch_shapes=scratch
            )
        )
    call = pl.pallas_call(
        wrapped,
        name=name,
        out_shape=shapes,
        compiler_params=params,
        cost_estimate=cost,
        input_output_aliases=aliases or {},
        **how,
    )
    return call(*ins, *after, *pin(*fetch))


def pin(*arrays):
    return [pltpu.with_memory_space_constraint(a, pltpu.HBM) for a in arrays]


def whole(shape):
    return pl.BlockSpec(shape, lambda *_: (0,) * len(shape))


def step_block(shape):
    return pl.BlockSpec(shape, lambda i, *_: (i,) + (0,) * (len(shape) - 1))


def inverse_rms(values):
    return lax.rsqrt(jnp.mean(values * values, axis=-1, keepdims=True) + EPSILON)


def row_of(gain):
    return gain[...].reshape(1, gain.shape[0])


def rms_backward(values, gain, grad):
    inverse = inverse_rms(values)
    scaled = grad * gain
    inner = jnp.mean(scaled * values, axis=-1, keepdims=True)
    grad_in = inverse * scaled - values * (inverse * inverse * inverse * inner)
    return grad_in, jnp.sum(grad * values * inverse, axis=0, keepdims=True)


def stack_pair(pair, scale=1.0):
    lanes = lax.broadcasted_iota(jnp.int32, (1, PAIR), 1)
    low = jnp.where(lanes < DH, scale, 0.0).astype(BF16)
    high = jnp.where(lanes < DH, 0.0, scale).astype(BF16)
    return jnp.concatenate([pair * low, pair * high], axis=0)


def join_pair(turned):
    n = turned.shape[1] // 2
    return jnp.concatenate([turned[:DH, :n], turned[DH:, n:]], axis=0).T


def fold(op, parts):
    return functools.reduce(op, parts)


def attend(q2, keys, values, biases):
    scores = [dot_nt(k, q2) + b for k, b in zip(keys, biases)]
    top = fold(jnp.maximum, [jnp.max(s, axis=0, keepdims=True) for s in scores])
    exps = [jnp.exp(s - top) for s in scores]
    total = fold(jnp.add, [jnp.sum(e, axis=0, keepdims=True) for e in exps])
    inv = 1.0 / total
    out = fold(jnp.add, [dot_tn(v, (e * inv).astype(BF16)) for e, v in zip(exps, values)])
    return out, top + jnp.log(total)


def attend_back(q2, do2, lse, keys, values, biases):
    probs = [jnp.exp(dot_nt(k, q2) + b - lse) for k, b in zip(keys, biases)]
    dv = [dot(p.astype(BF16), do2).astype(BF16) for p in probs]
    dp = [dot_nt(v, do2) for v in values]
    row = fold(jnp.add, [jnp.sum(p * g, axis=0, keepdims=True) for p, g in zip(probs, dp)])
    ds = [(p * (g - row)).astype(BF16) for p, g in zip(probs, dp)]
    dq = fold(jnp.add, [dot_tn(k, s) for s, k in zip(ds, keys)])
    dk = [dot(s, q2).astype(BF16) for s in ds]
    return dq, ds, dk, dv


def twice(a):
    return jnp.concatenate([a, a], axis=1)


def self_hidden(length, size):
    keys = lax.broadcasted_iota(jnp.int32, (size, size), 0)
    queries = lax.broadcasted_iota(jnp.int32, (size, size), 1)
    return jnp.where((keys <= queries) & (keys < length), 0.0, MASKED)


def cross_hidden(length, core, size, half):
    out = []
    for part in (core, 1 - core):
        pos = lax.broadcasted_iota(jnp.int32, (half, size), 0) + part * half
        out.append(twice(jnp.where(pos < length, 0.0, MASKED)))
    return out


def table_lines(table):
    lanes = lax.broadcasted_iota(jnp.int32, (1, 128), 1)
    lines = []
    for head in range(table.shape[0]):
        line = jnp.zeros((1, 128), F32)
        for b in range(NB):
            line = jnp.where(lanes == b, table[head, b], line)
        lines.append(line)
    return lines


def pair_bias(lines, index, pair, hidden):
    cols = []
    for head in (2 * pair, 2 * pair + 1):
        line = jnp.broadcast_to(lines[head], index.shape)
        cols.append(jnp.take_along_axis(line, index, axis=1, mode="promise_in_bounds") + hidden)
    return jnp.concatenate(cols, axis=1)


def self_forward(lens, table, x, gain, wq, wk, wv, wo, buckets, h_o, q_o, k_o, v_o, o_o, lse_o, part_o):
    docs, size = buckets.shape[0], buckets.shape[1]
    xf = x[...].astype(F32)
    h = (xf * inverse_rms(xf) * row_of(gain)).astype(BF16)
    h_o[...] = h
    q_o[...] = dot(h, wq[...]).astype(BF16)
    k_o[...] = dot(h, wk[...]).astype(BF16)
    v_o[...] = dot(h, wv[...]).astype(BF16)
    lines = table_lines(table)
    pairs = wq.shape[1] // PAIR
    for d in range(docs):
        rows = slice(d * size, (d + 1) * size)
        hidden = self_hidden(lens[d], size)
        index = buckets[d].T
        for p in range(pairs):
            cols = slice(p * PAIR, (p + 1) * PAIR)
            q2 = stack_pair(q_o[rows, cols], SCALE)
            bias = pair_bias(lines, index, p, hidden)
            out, lse = attend(q2, [k_o[rows, cols]], [v_o[rows, cols]], [bias])
            o_o[rows, cols] = join_pair(out).astype(BF16)
            at = d * pairs + p
            lse_o[at : at + 1, :] = lse
    part_o[...] = dot(o_o[...], wo[...]).astype(BF16)


def plus_parts(own, oth):
    return own[...].astype(F32) + oth[...].astype(F32)


def project_kv(e, wk, wv, kv_o):
    n = wk.shape[1]
    kv_o[0, :, :n] = dot(e[0], wk[...]).astype(BF16)
    kv_o[0, :, n:] = dot(e[0], wv[...]).astype(BF16)


def cross_forward(meta, lens, x, p_own, p_oth, gain, wq, wo, kv_own, kv_oth, x1_o, h_o, q_o, o_o, lse_o, part_o):
    docs, half, n = kv_own.shape[0], kv_own.shape[1], wq.shape[1]
    size = x.shape[0] // docs
    x1 = x[...].astype(F32) + plus_parts(p_own, p_oth)
    x1_o[...] = x1
    h = (x1 * inverse_rms(x1) * row_of(gain)).astype(BF16)
    h_o[...] = h
    q = dot(h, wq[...]).astype(BF16)
    q_o[...] = q
    for d in range(docs):
        rows = slice(d * size, (d + 1) * size)
        hidden = cross_hidden(lens[d], meta[2], size, half)
        out = []
        for p in range(n // PAIR):
            cols = slice(p * PAIR, (p + 1) * PAIR)
            vals = slice(n + p * PAIR, n + (p + 1) * PAIR)
            turned, lse = attend(
                stack_pair(q[rows, cols], SCALE),
                [kv_own[d, :, cols], kv_oth[d, :, cols]],
                [kv_own[d, :, vals], kv_oth[d, :, vals]],
                hidden,
            )
            out.append(join_pair(turned).astype(BF16))
            lse_o[d, p : p + 1, :] = lse
        o = jnp.concatenate(out, axis=1)
        o_o[rows, :] = o
        part_o[rows, :] = dot(o, wo[...]).astype(BF16)


GELU_C = 0.7978845608028654
GELU_A = 0.044715


def grid_slot(i):
    return jnp.where(i < 2, 2 * i + 1, 2 * (i - 2))


def ffn_act_grad(meta, dy, wout, dz_o):
    dz_o[0] = dot_nt(dy[...], wout[...])


def ffn_forward(meta, x1, p_own, p_oth, gain, win, dz, x2_o, z_send, z_keep, du_send, du_keep, part_o):
    x2 = x1[...] + plus_parts(p_own, p_oth)
    x2_o[...] = x2
    h = (x2 * inverse_rms(x2) * row_of(gain)).astype(BF16)
    half = h.shape[1] // 2
    du_send[2] = h[:, :half]
    du_send[3] = h[:, half:]
    block = win.shape[1] // 4
    total = 0.0
    for s in (1, 3, 0, 2):
        w = win[:, pl.ds(pl.multiple_of((meta[0] ^ s) * block, 128), block)]
        u = dot(h, w)
        u2 = u * u
        t = jnp.tanh(GELU_C * (u + GELU_A * (u * u2)))
        g = 0.5 * (1.0 + t)
        slope = g + (0.5 * GELU_C) * u * (1.0 - t * t) * (1.0 + 3.0 * GELU_A * u2)
        z = (u * g).astype(BF16)
        du = (dz[s] * slope).astype(BF16)
        z_slot = meta[0] ^ s ^ meta[3]

        @pl.when((z_slot & 1) == 1)
        def _(z=z, z_slot=z_slot):
            z_send[z_slot >> 1] = z

        @pl.when((z_slot & 1) == 0)
        def _(z=z, z_slot=z_slot):
            z_keep[z_slot >> 1] = z

        (du_send if s % 2 else du_keep)[s // 2] = du
        total = total + dot_nt(du, w)
    part_o[...] = total.astype(BF16)


def ffn_out_grads(meta, keep, got, dy, dy_got, keep_o, send_o):
    half = dy.shape[1] // 2
    for j, out in enumerate((keep_o, send_o)):
        w = (dot_tn(keep[j], dy[...]) + dot_tn(got[j], dy_got[...])).astype(BF16)
        r = w.shape[0] // 4
        for az in range(4):
            for k in range(2):
                out[meta[1] ^ az, k * r : (k + 1) * r] = w[az * r : (az + 1) * r, k * half : (k + 1) * half]


def ffn_in_grads(meta, keep, send, got, keep_o, send_o):
    for j, out in enumerate((keep_o, send_o)):
        for k in range(2):
            w = (dot_tn(send[2 + k], keep[j]) + dot_tn(got[2 + k], got[j])).astype(BF16)
            r = w.shape[0] // 2
            for az in range(2):
                out[meta[1] ^ (2 * k + az)] = w[az * r : (az + 1) * r]


def ffn_branch(meta, send, keep, wout, part_o, total):
    i = pl.program_id(0)
    branch = dot(jnp.where(i < 2, send[0], keep[0]), wout[...])

    @pl.when(i == 0)
    def _():
        total[...] = branch

    @pl.when((i > 0) & (i < 3))
    def _():
        total[...] += branch

    @pl.when(i == 3)
    def _():
        part_o[...] = (total[...] + branch).astype(BF16)


def finish_output(x2, p_own, p_oth, y_o):
    y_o[...] = (x2[...] + (p_own[...].astype(F32) + p_oth[...].astype(F32))).astype(BF16)


def cross_backward(meta, lens, x2, p_own, p_oth, gain, dy, wo, wq, q, lse, kv_own, kv_oth, gain_o, dx2_o, dc_o, dq_o, part_o, dkv_own, dkv_oth, dy_o):
    docs, half, n = kv_own.shape[0], kv_own.shape[1], q.shape[1]
    size = x2.shape[0] // docs
    dv, gain_grad = rms_backward(x2[...], row_of(gain), plus_parts(p_own, p_oth))
    gain_o[...] = gain_grad
    dy_o[...] = dy[...]
    dx2 = dy[...].astype(F32) + dv
    dx2_o[...] = dx2
    dc = dx2.astype(BF16)
    dc_o[...] = dc
    do = dot_nt(dc, wo[...]).astype(BF16)
    for d in range(docs):
        rows = slice(d * size, (d + 1) * size)
        hidden = cross_hidden(lens[d], meta[2], size, half)
        out = []
        for p in range(n // PAIR):
            cols = slice(p * PAIR, (p + 1) * PAIR)
            vals = slice(n + p * PAIR, n + (p + 1) * PAIR)
            dq, _, dk, dv = attend_back(
                stack_pair(q[rows, cols], SCALE),
                stack_pair(do[rows, cols]),
                lse[d, p : p + 1, :],
                [kv_own[d, :, cols], kv_oth[d, :, cols]],
                [kv_own[d, :, vals], kv_oth[d, :, vals]],
                hidden,
            )
            out.append((join_pair(dq) * SCALE).astype(BF16))
            dkv_own[d, :, cols], dkv_oth[d, :, cols] = dk
            dkv_own[d, :, vals], dkv_oth[d, :, vals] = dv
        dq = jnp.concatenate(out, axis=1)
        dq_o[rows, :] = dq
        part_o[rows, :] = dot_nt(dq, wq[...]).astype(BF16)


def store_tensors(tensors, zq, scratch):
    for t, quarters in enumerate(tensors):
        for az, quarter in enumerate(quarters):
            scratch[t, zq ^ az] = quarter.astype(BF16)


def tall(a):
    r = a.shape[0] // 4
    return [a[z * r : (z + 1) * r] for z in range(4)]


def wide(a):
    r, c = a.shape[0] // 2, a.shape[1] // 2
    return [a[(z % 2) * r : (z % 2 + 1) * r, (z // 2) * c : (z // 2 + 1) * c] for z in range(4)]


def send_blocks(quad, scratch, keep, send, sem):
    copies = []
    for s in range(4):
        ref = keep if s % 2 == 0 else send
        copies.append(pltpu.make_async_copy(scratch.at[quad ^ s], ref.at[s // 2], sem.at[s]))
    for c in copies:
        c.start()
    for c in copies:
        c.wait()


def cross_grads(meta, h, dq, e_own, e_oth, dkv_own, dkv_oth, dc, o, keep, send, scratch, sem):
    n = dq.shape[1]
    kv = dot_tn(e_own[...], dkv_own[...]) + dot_tn(e_oth[...], dkv_oth[...])
    gq = dot_tn(h[...], dq[...])
    go = dot_tn(o[...], dc[...])
    store_tensors([tall(gq), tall(kv[:, :n]), tall(kv[:, n:]), wide(go)], meta[1], scratch)
    send_blocks(meta[0], scratch, keep, send, sem)


def self_backward(lens, table, x1, dx2, p_own, p_oth, gain, wo, q, k, v, lse, buckets, gain_o, dx1_o, da_o, dqkv_o, ds_o):
    docs, size = buckets.shape[0], buckets.shape[1]
    n = q.shape[1]
    dv, gain_grad = rms_backward(x1[...], row_of(gain), plus_parts(p_own, p_oth))
    gain_o[...] = gain_grad
    dx1 = dx2[...] + dv
    dx1_o[...] = dx1
    da = dx1.astype(BF16)
    da_o[...] = da
    do = dot_nt(da, wo[...]).astype(BF16)
    lines = table_lines(table)
    pairs = n // PAIR
    for d in range(docs):
        rows = slice(d * size, (d + 1) * size)
        hidden = self_hidden(lens[d], size)
        index = buckets[d].T
        for p in range(pairs):
            cols = slice(p * PAIR, (p + 1) * PAIR)
            at = d * pairs + p
            dq, ds, dk, dvv = attend_back(
                stack_pair(q[rows, cols], SCALE),
                stack_pair(do[rows, cols]),
                lse[at : at + 1, :],
                [k[rows, cols]],
                [v[rows, cols]],
                [pair_bias(lines, index, p, hidden)],
            )
            dqkv_o[rows, cols] = (join_pair(dq) * SCALE).astype(BF16)
            dqkv_o[rows, n + p * PAIR : n + (p + 1) * PAIR] = dk[0]
            dqkv_o[rows, 2 * n + p * PAIR : 2 * n + (p + 1) * PAIR] = dvv[0]
            ds_o[p, d] = ds[0]


def self_input(dqkv, wq, wk, wv, part_o):
    n = wq.shape[1]
    part_o[...] = (
        dot_nt(dqkv[:, :n], wq[...])
        + dot_nt(dqkv[:, n : 2 * n], wk[...])
        + dot_nt(dqkv[:, 2 * n :], wv[...])
    ).astype(BF16)


def self_grads(meta, h, dqkv, da, o, keep, send, scratch, sem):
    n = o.shape[1]
    g = dot_tn(h[...], dqkv[...])
    go = dot_tn(o[...], da[...])
    store_tensors([tall(g[:, t * n : (t + 1) * n]) for t in range(3)] + [wide(go)], meta[1], scratch)
    send_blocks(meta[0], scratch, keep, send, sem)


def finish_input(x, p_own, p_oth, gain, dx1, gain_o, dx_o):
    dv, gain_grad = rms_backward(
        x[...].astype(F32), row_of(gain), p_own[...].astype(F32) + p_oth[...].astype(F32)
    )
    gain_o[...] = gain_grad
    dx_o[...] = dx1[...] + dv


def small_grads(buckets, ds, gain1, gain2, gain3, out):
    docs, size = buckets.shape[0], buckets.shape[1]
    pairs = ds.shape[0]
    half = out.shape[1]
    lanes = lax.broadcasted_iota(jnp.int32, (8, 128), 1)
    subs = lax.broadcasted_iota(jnp.int32, (8, 128), 0)
    out[...] = jnp.zeros(out.shape, F32)
    for j, gain in enumerate((gain1, gain2, gain3)):
        for k in range(2):
            out[2 * j + k : 2 * j + k + 1, :] = gain[:, k * half : (k + 1) * half]
    table = jnp.zeros((8, 128), F32)
    index = [twice(buckets[d].T) for d in range(docs)]
    for p in range(pairs):
        for b in range(NB):
            line = fold(
                jnp.add,
                [
                    jnp.sum(jnp.where(index[d] == b, ds[p, d].astype(F32), 0.0), axis=0, keepdims=True)
                    for d in range(docs)
                ],
            )
            for j in range(2):
                total = jnp.sum(line[:, j * size : (j + 1) * size], axis=1, keepdims=True)
                table = jnp.where((subs == 2 * p + j) & (lanes == b), total, table)
    out[8:16, :128] = table


def enc_part(dkv, wk, wv, out):
    n = wk.shape[1]
    out[0] = (dot_nt(dkv[0, :, :n], wk[...]) + dot_nt(dkv[0, :, n:], wv[...])).astype(BF16)


def finish_enc(dkv, wk, wv, got, out):
    n = wk.shape[1]
    own = dot_nt(dkv[0, :, :n], wk[...]) + dot_nt(dkv[0, :, n:], wv[...])
    out[0] = (own + got[0].astype(F32)).astype(BF16)


def add_quads(keep, got, keep_o, send_o):
    keep_o[...] = keep[0] + got[0]
    send_o[...] = keep[1] + got[1]


EXTRA = 16


def add_quads(keep, got, keep_o, send_o):
    keep_o[...] = keep[0] + got[0]
    send_o[...] = keep[1] + got[1]


def add_pieces(keep, got, keep_o, send_o):
    for j in range(2):
        keep_o[j] = keep[2 * j] + got[2 * j]
        send_o[j] = keep[2 * j + 1] + got[2 * j + 1]


def add_pair(keep, got, keep_o, send_o):
    keep_o[...] = keep[0] + got[0]
    send_o[...] = keep[1] + got[1]


def add_shard(keep, got, out):
    out[...] = keep[...] + got[...]


def put_two(a, b, out):
    out[0] = a[...]
    out[1] = b[...]


def join_pieces(meta, own, got, out):
    r = own.shape[1]
    for j in range(2):
        out[pl.ds(pl.multiple_of((meta[1] ^ (2 * j)) * r, r), r), :] = own[j]
        out[pl.ds(pl.multiple_of((meta[1] ^ (2 * j + 1)) * r, r), r), :] = got[j]


def put_blocks(a, b, out):
    r = a.shape[0]
    out[:r] = a[...]
    out[r:] = b[...]


def plus_small(own, got):
    return (own[...].astype(BF16).astype(F32) + got.astype(F32)).astype(BF16)


def self_pieces(keep, got, small, keep_o, send_o):
    r = keep.shape[1]
    for j in range(2):
        keep_o[j] = keep[2 * j] + got[2 * j]
        send_o[j * r : (j + 1) * r] = keep[2 * j + 1] + got[2 * j + 1]
    send_o[2 * r :] = small[...].astype(BF16)


def self_pair(keep, got, small, keep_o, send_o, small_o):
    r = keep.shape[1]
    total = plus_small(small, got[2 * r :])
    small_o[...] = total
    keep_o[...] = keep[0] + got[:r]
    send_o[:r] = keep[1] + got[r : 2 * r]
    send_o[r:] = total


def self_shard(keep, got, small, out, small_o):
    r = keep.shape[0]
    out[...] = keep[...] + got[:r]
    small_o[...] = plus_small(small, got[r:])


def self_join(meta, own, got, small, out):
    join_pieces(meta, own, got, out)
    out[4 * own.shape[1] :] = small[...]


def self_blocks(a, b, small, out):
    r = a.shape[0] - EXTRA
    out[:r] = a[:r]
    out[r : 2 * r] = b[:r]
    out[2 * r :] = plus_small(small, b[r:])


def write_small(own, got, gain1_o, gain2_o, gain3_o, table_o):
    at = got.shape[0] - EXTRA
    total = own[at:, :].astype(F32) + got[at:, :].astype(F32)
    for j, gain in enumerate((gain1_o, gain2_o, gain3_o)):
        gain[...] = jnp.concatenate([total[2 * j : 2 * j + 1], total[2 * j + 1 : 2 * j + 2]], axis=1).reshape(gain.shape)
    heads, buckets = table_o.shape
    table_o[...] = total[8 : 8 + heads, :buckets]


def write_ffn_out(slots, meta, both, *refs):
    out, done, scratch, sem = refs[-4:]
    done[...] = jnp.zeros(done.shape, F32)
    r, c = scratch.shape[1] // 4, scratch.shape[2] // 2
    copies = []
    for i, s in enumerate(slots):
        for z in range(4):
            for j in range(2):
                at = (8 * i + 2 * z + j) * r
                scratch[i, z * r : (z + 1) * r, j * c : (j + 1) * c] = both[at : at + r].astype(F32)
        copies.append(pltpu.make_async_copy(scratch.at[i], out.at[meta[0] ^ s], sem.at[i]))
        copies[-1].start()
    for copy in copies:
        copy.wait()


def write_ffn_in(slots, meta, both, *refs):
    out, done, scratch, sem = refs[-4:]
    done[...] = jnp.zeros(done.shape, F32)
    r, c = scratch.shape[1:]
    copies = []
    for i, s in enumerate(slots):
        scratch[i] = both[i * r : (i + 1) * r].astype(F32)
        cols = pl.ds(pl.multiple_of((meta[0] ^ s) * c, 128), c)
        copies.append(pltpu.make_async_copy(scratch.at[i], out.at[:, cols], sem.at[i]))
        copies[-1].start()
    for copy in copies:
        copy.wait()


def write_attention(slots, meta, both, *refs):
    q_o, k_o, v_o, o_o, done, scratch, sem = refs[-7:]
    done[...] = jnp.zeros(done.shape, F32)
    rows, c = scratch.shape[1:]
    r = rows // 4

    def copy_of(i, t, z):
        src = scratch.at[i, pl.ds(z * r, r)]
        if t < 3:
            return pltpu.make_async_copy(src, (q_o, k_o, v_o)[t].at[pl.ds(z * r, r)], sem.at[i, z])
        to = o_o.at[pl.ds((z % 2) * r, r), pl.ds((z // 2) * c, c)]
        return pltpu.make_async_copy(src, to, sem.at[i, z])

    def each(act):
        for i, s in enumerate(slots):
            for z in range(4):
                act(i, s, z)

    def start(i, s, z):
        at = i * rows + z * r
        scratch[i, z * r : (z + 1) * r] = both[at : at + r].astype(F32)
        for t in range(4):
            pl.when((meta[0] ^ s) == t)(lambda: copy_of(i, t, z).start())

    def wait(i, s, z):
        for t in range(4):
            pl.when((meta[0] ^ s) == t)(lambda: copy_of(i, t, z).wait())

    each(start)
    each(wait)


class Sum:
    def __init__(self, name, dp, masks, meta, keep=None, send=None):
        self.name, self.dp, self.masks, self.meta = name, dp, masks, meta
        self.keep, self.send, self.small = keep, send, None

    def move(self, a, mask, what):
        pairs = [(2 * i + c, 2 * (i ^ mask[c]) + c) for i in range(self.dp) for c in range(2)]
        with jax.named_scope(f"{self.name}_{what}"):
            return lax.ppermute(a, ("top", "mid", "xy", "seq"), pairs)

    def exchange(self, a, k, what):
        self.got = self.move(a, self.masks[k], what)

    def call(self, body, outs, ins, after, **kw):
        name = f"{self.name}_{body.__name__}" if hasattr(body, "__name__") else f"{self.name}_write"
        return kernel(body, name, outs, ins, [after], **{"limit": SUM_LIMIT, **kw})

    def step_a(self):
        self.exchange(self.send, 0, "sum_a")

    def step_b(self, after):
        z, r, c = self.keep.shape[1:]
        self.keep, send = self.call(add_quads, [((z, r, c), BF16)] * 2, [self.keep, self.got], after)
        self.exchange(send, 1, "sum_b")
        return self.keep

    def step_c(self, after, small=None):
        z, r, c = self.keep.shape
        ins, half = [self.keep, self.got], ((2, r, c), BF16)
        self.small = small
        if small is None:
            self.keep, send = self.call(add_pieces, [half] * 2, ins, after)
        else:
            self.keep, send = self.call(self_pieces, [half, ((2 * r + EXTRA, c), BF16)], [*ins, small], after)
        self.exchange(send, 2, "sum_c")
        return self.keep

    def step_d(self, after):
        z, r, c = self.keep.shape
        ins, one = [self.keep, self.got], ((r, c), BF16)
        if self.small is None:
            self.keep, send = self.call(add_pair, [one] * 2, ins, after)
        else:
            self.keep, send, self.small = self.call(
                self_pair,
                [one, ((r + EXTRA, c), BF16), (self.small.shape, BF16)],
                [*ins, self.small],
                after,
            )
        self.exchange(send, 3, "sum_d")
        return self.keep

    def step_e(self, after):
        ins, one = [self.keep, self.got], (self.keep.shape, BF16)
        if self.small is None:
            self.shard = self.call(add_shard, [one], ins, after)[0]
        else:
            self.shard, self.small = self.call(
                self_shard, [one, (self.small.shape, BF16)], [*ins, self.small], after
            )
        step = 16
        while step < self.dp:
            rest = (step, step)
            self.shard = self.shard + self.move(self.shard, rest, "sum_rest")
            if self.small is not None:
                self.small = self.small + self.move(self.small, rest, "sum_rest")
            step *= 2
        self.exchange(self.shard, 3, "gather_d")
        return self.shard

    def hand_small(self, other):
        other.small, self.small = self.small, None

    def step_f(self, after):
        shape = (2,) + self.shard.shape
        self.two = self.call(put_two, [(shape, BF16)], [self.shard, self.got], after)[0]
        self.exchange(self.two, 2, "gather_c")
        return self.two

    def step_g(self, after):
        r, c = self.shard.shape
        ins = [self.meta, self.two, self.got]
        if self.small is None:
            self.block = self.call(join_pieces, [((4 * r, c), BF16)], ins, after, smem=1)[0]
        else:
            self.block = self.call(self_join, [((4 * r + EXTRA, c), BF16)], [*ins, self.small], after, smem=1)[0]
        self.exchange(self.block, 1, "gather_b")
        return self.block

    def step_h(self, after):
        r, c = self.block.shape
        ins = [self.block, self.got]
        if self.small is None:
            self.near = self.call(put_blocks, [((2 * r, c), BF16)], ins, after)[0]
        else:
            self.near = self.call(self_blocks, [((2 * r - EXTRA, c), BF16)], [*ins, self.small], after)[0]
        self.exchange(self.near, 0, "gather_a")
        return self.near

    def write(self, slots, both, into, after):
        body, outs, scratch = self.target
        into = list(into)
        *self.out, done = self.call(
            functools.partial(body, slots),
            [(o, F32) for o in outs] + [((8, 128), F32)],
            [self.meta, both, *into],
            after,
            smem=1,
            in_specs=[VMEM] + [ANY] * len(into),
            out_specs=[ANY] * len(outs) + [VMEM],
            scratch=scratch,
            aliases={2 + i: i for i in range(len(into))},
            limit=30,
            us=0.1,
        )
        return done

    def write1(self, after):
        return self.write((0, 2), self.near, (), after)

    def write2(self, after):
        return self.write((1, 3), self.got, self.out, after)


def shards(
    dec_input,
    enc_states,
    dec_lengths,
    enc_lengths,
    rel_buckets,
    out_grad,
    gain_self,
    gain_cross,
    gain_ffn,
    rel_table,
    self_query,
    self_key,
    self_value,
    self_out,
    cross_query,
    cross_key,
    cross_value,
    cross_out,
    ffn_in,
    ffn_out,
    *,
    dp,
):
    docs, size, width = dec_input.shape
    half = enc_states.shape[1]
    rows = docs * size
    n = self_query.shape[1]
    hidden = ffn_in.shape[1]
    block = hidden // 4
    pairs = n // PAIR
    index, core = lax.axis_index(("top", "mid", "xy")), lax.axis_index("seq")
    bits = [(index >> k) & 1 for k in range(4)]
    one, two = jnp.where(core == 0, bits[0], bits[1]), jnp.where(core == 0, bits[1], bits[0])
    near, far, up, top = (1, 2), (2, 1), (4, 4), (8, 8)
    quad, quad_out = one + 2 * two, bits[2] + 2 * one
    meta = jnp.stack([quad, bits[2] + 2 * bits[3], core, quad_out, two + 2 * bits[3]]).astype(jnp.int32)
    meta_out = meta[3:]

    def swap(a):
        return lax.ppermute(a, "seq", [(0, 1), (1, 0)])

    dec_lengths, enc_lengths, table = pin(dec_lengths, enc_lengths, rel_table.T)
    gain_self, gain_cross, gain_ffn = pin(gain_self, gain_cross, gain_ffn)
    buckets = pin(rel_buckets)[0]
    x = dec_input.reshape(rows, width)
    dy = out_grad.reshape(rows, width)
    fo = Sum("ffn_out", dp, (up, near, far, top), meta_out)
    fi = Sum("ffn_in", dp, (near, far, up, top), meta)
    enc_oth = swap(enc_states)

    tok = (rows, width)
    head = (rows, n)
    kept = "kept"
    h1, q1, k1, v1, o1, lse1, self_part = kernel(
        self_forward,
        "self_forward",
        [(tok, BF16, kept)] + [(head, BF16, kept)] * 4 + [((docs * pairs, 2 * size), F32), (tok, BF16)],
        [dec_lengths, table, *pin(x), gain_self, *pin(self_query, self_key, self_value, self_out), buckets],
        smem=2,
        us=2.7,
    )
    self_part_oth = swap(self_part)
    kv_shape = (docs, half, 2 * n)
    kv_block = step_block((1, half, 2 * n))
    enc_block = step_block((1, half, width))
    w_block = whole((width, n))
    project = dict(grid=(docs,), in_specs=[enc_block, w_block, w_block], out_specs=[kv_block], us=2)
    kv_own, key_near, value_near, query_near, out_near = kernel(
        project_kv,
        "project_own",
        [(kv_shape, BF16)],
        pin(enc_states, cross_key, cross_value),
        [self_part],
        fetch=[cross_key, cross_value, cross_query, cross_out],
        **project,
    )
    kv_oth, ffn_out_near, dy_near = kernel(
        project_kv,
        "project_oth",
        [(kv_shape, BF16)],
        [enc_oth, key_near, value_near],
        [kv_own],
        fetch=[ffn_out, dy],
        **project,
    )
    wide_tok, wide_head, wo_block = whole(tok), whole(head), whole((n, width))
    gain_block = whole((width,))
    lse_shape = (docs, pairs, 2 * size)
    lse_block = step_block((1, pairs, 2 * size))
    head_block = step_block((size, n))
    tok_block = step_block((size, width))
    x1, h2, q2, o2, lse2, cross_part, ffn_in_near = kernel(
        cross_forward,
        "cross_forward",
        [(tok, F32), (tok, BF16, kept), (head, BF16, kept), (head, BF16, kept), (lse_shape, F32), (tok, BF16)],
        [meta, enc_lengths, *pin(x), self_part, self_part_oth, gain_cross, query_near, out_near, kv_own, kv_oth],
        smem=2,
        fetch=[ffn_in],
        us=8,
    )
    cross_part_oth = swap(cross_part)
    group = (2, 4, width // 4, n)
    act = (4, rows, block)
    act_block = pl.BlockSpec((1, rows, block), lambda i, m: (grid_slot(i), 0, 0))
    win_block = pl.BlockSpec((width, block), lambda i, m: (0, m[0] ^ grid_slot(i)))
    wout_block = pl.BlockSpec((block, width), lambda i, m: (m[0] ^ grid_slot(i), 0))
    dz = kernel(
        ffn_act_grad,
        "ffn_act_grad",
        [(act, F32)],
        [meta, dy_near, ffn_out_near],
        [cross_part],
        smem=1,
        grid=(4,),
        in_specs=[wide_tok, wout_block],
        out_specs=[act_block],
        us=2.5,
    )[0]
    pair_act, sent = (2, rows, block), (4, rows, block)
    x2, z_send, z_keep, du_send, du_keep, part = kernel(
        ffn_forward,
        "ffn_forward",
        [(tok, F32), (pair_act, BF16), (pair_act, BF16), (sent, BF16), (pair_act, BF16), (tok, BF16)],
        [meta, x1, cross_part, cross_part_oth, gain_ffn, ffn_in_near, dz],
        smem=1,
        us=8,
    )
    z_got = fo.move(z_send, up, "sum_a")
    du_got = fi.move(du_send, near, "sum_a")
    part_oth = swap(part)
    gain3, dx2, dc, dq2, query_part, dkv_own, dkv_oth, dy_sent = kernel(
        cross_backward,
        "cross_backward",
        [((1, width), F32), (tok, F32), (tok, BF16), (head, BF16), (tok, BF16)] + [(kv_shape, BF16)] * 2 + [(tok, BF16)],
        [meta, enc_lengths, x2, part, part_oth, gain_ffn, dy, cross_out, cross_query, q2, lse2, kv_own, kv_oth],
        smem=2,
        us=10,
    )
    query_part_oth = swap(query_part)
    dy_got = fo.move(dy_sent, up, "tokens")
    piece = group[1:]
    group_scratch = [pltpu.VMEM((4,) + group[1:], BF16), pltpu.SemaphoreType.DMA((4,))]
    enc_rows = (docs * half, width)
    cross = Sum("cross", dp, (near, far, up, top), meta)
    own = Sum("self", dp, (near, far, up, top), meta)

    def run_out_grads(last):
        fo.keep, send = kernel(
            ffn_out_grads, "ffn_out_grads", [(piece, BF16)] * 2, [meta_out, z_keep, z_got, dy, dy_got], [last], smem=1, us=3
        )
        fo.exchange(send, 1, "sum_b")
        return fo.keep

    def run_in_grads(last):
        fi.keep, send = kernel(
            ffn_in_grads, "ffn_in_grads", [(piece, BF16)] * 2, [meta, du_keep, du_send, du_got], [last], smem=1, us=3
        )
        fi.exchange(send, 1, "sum_b")
        return fi.keep

    def run_cross_grads(last):
        cross.keep, cross.send = kernel(
            cross_grads,
            "cross_grads",
            [(group, BF16)] * 2,
            [meta, h2, dq2, enc_states.reshape(enc_rows), enc_oth.reshape(enc_rows)]
            + [dkv_own.reshape(enc_rows), dkv_oth.reshape(enc_rows), dc, o2],
            [last],
            smem=1,
            out_specs=[ANY] * 2,
            scratch=group_scratch,
            us=5,
        )
        cross.step_a()
        return cross.keep

    sems = pltpu.SemaphoreType.DMA
    fo.target = (write_ffn_out, [(4, block, width)], [pltpu.VMEM((2, block, width), F32), sems((2,))])
    fi.target = (write_ffn_in, [ffn_in.shape], [pltpu.VMEM((2, width, block), F32), sems((2,))])
    cross.target = own.target = (
        write_attention,
        [(width, n)] * 3 + [(n, width)],
        [pltpu.VMEM((2, width, n), F32), sems((2, 4))],
    )

    def run_self_backward(last):
        nonlocal gain2, dx1, da, dqkv, ds1
        gain2, dx1, da, dqkv, ds1 = kernel(
            self_backward,
            "self_backward",
            [((1, width), F32), (tok, F32), (tok, BF16), ((rows, 3 * n), BF16), ((pairs, docs, size, 2 * size), BF16)],
            [dec_lengths, table, x1, dx2, query_part, query_part_oth, gain_cross, self_out]
            + [q1, k1, v1, lse1, buckets],
            [last],
            smem=2,
            us=5,
        )
        return ds1

    def run_self_grads(last):
        own.keep, own.send = kernel(
            self_grads,
            "self_grads",
            [(group, BF16)] * 2,
            [meta, h1, dqkv, da, o1],
            [last],
            smem=1,
            out_specs=[ANY] * 2,
            scratch=group_scratch,
            us=2.7,
        )
        own.step_a()
        return own.keep

    def run_self_input(last):
        nonlocal part1, part1_oth
        part1 = kernel(
            self_input, "self_input", [(tok, BF16)], [dqkv, self_query, self_key, self_value], [last], us=0.1
        )[0]
        part1_oth = swap(part1)
        return part1

    def run_enc_part(last):
        nonlocal enc_sent, enc_got
        enc_sent = kernel(
            enc_part,
            "enc_part",
            [((docs, half, width), BF16)],
            [dkv_oth, cross_key, cross_value],
            [last],
            grid=(docs,),
            in_specs=[kv_block, w_block, w_block],
            out_specs=[enc_block],
            us=0.1,
        )[0]
        enc_got = swap(enc_sent)
        return enc_sent

    def run_finish_input(last):
        nonlocal gain1, dx
        gain1, dx = kernel(
            finish_input,
            "finish_input",
            [((1, width), F32), (tok, F32)],
            [x, part1, part1_oth, gain_self, dx1],
            [last],
            us=0.1,
        )
        return dx

    def run_small(last):
        nonlocal small
        small = kernel(
            small_grads,
            "small_grads",
            [((EXTRA, width // 2), F32)],
            [buckets, ds1, gain1, gain2, gain3],
            [last],
            us=0.1,
        )[0]
        return small

    def run_finish_enc(last):
        nonlocal enc_grad
        enc_grad = kernel(
            finish_enc,
            "finish_enc",
            [((docs, half, width), BF16)],
            [dkv_own, cross_key, cross_value, enc_got],
            [last],
            grid=(docs,),
            in_specs=[kv_block, w_block, w_block, enc_block],
            out_specs=[enc_block],
            us=0.1,
        )[0]
        return enc_grad

    def run_branch(last):
        nonlocal branch, branch_oth
        branch = kernel(
            ffn_branch,
            "ffn_branch",
            [(tok, BF16)],
            [meta_out, z_send, z_keep, ffn_out],
            [last],
            smem=1,
            grid=(4,),
            in_specs=[
                pl.BlockSpec((1, rows, block), lambda i, m: (jnp.minimum(i, 1), 0, 0)),
                pl.BlockSpec((1, rows, block), lambda i, m: (jnp.maximum(i - 2, 0), 0, 0)),
                wout_block,
            ],
            out_specs=[wide_tok],
            scratch=[pltpu.VMEM(tok, F32)],
            us=0.1,
        )[0]
        branch_oth = swap(branch)
        return branch

    def run_finish_output(last):
        nonlocal y
        y = kernel(finish_output, "finish_output", [(tok, BF16)], [x2, branch, branch_oth], [last], us=0.1)[0]
        return y

    def run_own_e(last):
        last = own.step_e(last)
        own.hand_small(cross)
        return last

    def run_write_small(last):
        nonlocal totals
        totals = kernel(
            write_small,
            "write_small",
            [((width,), F32, kept)] * 3 + [((n // DH, NB), F32, kept)],
            [cross.near, cross.got],
            [last],
            limit=16,
            us=0.1,
        )
        return totals[-1]

    totals = gain2 = dx1 = da = dqkv = ds1 = part1 = part1_oth = enc_sent = enc_got = None
    gain1 = dx = small = enc_grad = branch = branch_oth = y = None
    steps = (
        (run_in_grads, run_cross_grads, run_self_backward, fi.step_c, run_out_grads, fi.step_d, cross.step_b)
        + (run_branch, fo.step_c, fi.step_e, run_self_grads, cross.step_c, run_self_input, run_finish_output)
        + (fo.step_d, fi.step_f, cross.step_d, own.step_b, run_finish_input, fo.step_e, run_small)
        + (lambda last: own.step_c(last, small), fi.step_g, cross.step_e, fo.step_f, own.step_d, fi.step_h)
        + (cross.step_f, run_own_e, fi.write1, fo.step_g, own.step_f, cross.step_g, fi.write2, run_enc_part)
        + (own.step_g, fo.step_h, cross.step_h, own.step_h, cross.write1, fo.write1, own.write1, run_finish_enc)
        + (fo.write2, run_write_small, cross.write2)
    )
    last = dq2
    for step in steps:
        last = step(last)
    own.write2(last)
    return (
        y.reshape(dec_input.shape),
        dx.reshape(dec_input.shape),
        enc_grad,
        totals[0],
        totals[1],
        totals[2],
        totals[3].T,
        *own.out,
        *cross.out,
        fi.out[0],
        fo.out[0].reshape(ffn_out.shape),
    )


def solution(mesh):
    dp = mesh.shape["dp"]
    split = jax.sharding.Mesh(mesh.devices.reshape(dp // 8, 2, 4, 2), ("top", "mid", "xy", "seq"))
    rows = ("top", "mid", "xy")
    col, row, doc = P(None, "seq"), P("seq", None), P(rows, None, None)
    in_specs = (
        (doc, P(rows, "seq", None), P(rows), P(rows), doc, doc)
        + (P(),) * 3
        + (col,) * 4
        + (row,)
        + (col,) * 3
        + (row, col, row)
    )
    out_specs = (
        (doc, doc, P(rows, "seq", None))
        + (P(),) * 3
        + (col,) * 4
        + (row,)
        + (col,) * 3
        + (row, col, row)
    )
    return jax.shard_map(
        functools.partial(shards, dp=dp),
        mesh=split,
        in_specs=in_specs,
        out_specs=out_specs,
        check_vma=False,
    )
```

```python
import functools

import jax
import jax.numpy as jnp
from jax import lax
from jax.experimental import pallas as pl
from jax.experimental.pallas import tpu as pltpu
from jax.sharding import PartitionSpec as P

DH = 64
NB = 32
PAIR = 2 * DH
SCALE = DH**-0.5
EPSILON = 1e-06
MASKED = -1e30
F32 = jnp.float32
BF16 = jnp.bfloat16
MIB = 1024 * 1024
SUM_LIMIT = 16


def dot(a, b):
    return lax.dot_general(a, b, (((1,), (0,)), ((), ())), preferred_element_type=F32)


def dot_nt(a, b):
    return lax.dot_general(a, b, (((1,), (1,)), ((), ())), preferred_element_type=F32)


def dot_tn(a, b):
    return lax.dot_general(a, b, (((0,), (0,)), ((), ())), preferred_element_type=F32)


VMEM = pl.BlockSpec(memory_space=pltpu.VMEM)
SMEM = pl.BlockSpec(memory_space=pltpu.SMEM)
ANY = pl.BlockSpec(memory_space=pl.ANY)


def kernel(body, name, outs, ins, after=(), smem=0, in_specs=None, out_specs=None, scratch=(), grid=None, limit=30, aliases=None, us=0.5, fetch=()):
    n_in, n_out, n_after, n_fetch = len(ins), len(outs), len(after), len(fetch)

    def wrapped(*refs):
        at = n_in + n_after
        sources, at = refs[at : at + n_fetch], at + n_fetch
        results, at = refs[at : at + n_out], at + n_out
        targets, at = refs[at : at + n_fetch], at + n_fetch
        rest, sems = (refs[at:-1], refs[-1]) if n_fetch else (refs[at:], None)
        copies = [pltpu.make_async_copy(src, to, sems.at[i]) for i, (src, to) in enumerate(zip(sources, targets))]

        def begin():
            for copy in copies:
                copy.start()

        def end():
            for copy in copies:
                copy.wait()

        if copies and grid is not None:
            pl.when(pl.program_id(0) == 0)(begin)
        else:
            begin()
        body(*refs[:n_in], *results, *rest)
        if copies and grid is not None:
            pl.when(pl.program_id(0) == grid[0] - 1)(end)
        else:
            end()

    in_specs = list(in_specs) if in_specs is not None else [VMEM] * (n_in - smem)
    out_specs = list(out_specs) if out_specs is not None else [VMEM] * len(outs)
    in_specs += [ANY] * (n_after + n_fetch)
    out_specs += [ANY] * n_fetch
    scratch = list(scratch) + ([pltpu.SemaphoreType.DMA((n_fetch,))] if n_fetch else [])
    params = pltpu.CompilerParams(vmem_limit_bytes=limit * MIB)
    cost = pl.CostEstimate(flops=int(us * 10e9), bytes_accessed=0, transcendentals=0)
    shapes = [pltpu.HBM(o[0], o[1]) if len(o) > 2 else jax.ShapeDtypeStruct(*o) for o in outs]
    shapes += [pltpu.VMEM(a.shape, a.dtype) for a in fetch]
    if grid is None:
        how = dict(in_specs=[SMEM] * smem + in_specs, out_specs=out_specs, scratch_shapes=scratch)
    else:
        how = dict(
            grid_spec=pltpu.PrefetchScalarGridSpec(
                num_scalar_prefetch=smem, grid=grid, in_specs=in_specs, out_specs=out_specs, scratch_shapes=scratch
            )
        )
    call = pl.pallas_call(
        wrapped,
        name=name,
        out_shape=shapes,
        compiler_params=params,
        cost_estimate=cost,
        input_output_aliases=aliases or {},
        **how,
    )
    return call(*ins, *after, *pin(*fetch))


def pin(*arrays):
    return [pltpu.with_memory_space_constraint(a, pltpu.HBM) for a in arrays]


def whole(shape):
    return pl.BlockSpec(shape, lambda *_: (0,) * len(shape))


def step_block(shape):
    return pl.BlockSpec(shape, lambda i, *_: (i,) + (0,) * (len(shape) - 1))


def inverse_rms(values):
    return lax.rsqrt(jnp.mean(values * values, axis=-1, keepdims=True) + EPSILON)


def row_of(gain):
    return gain[...].reshape(1, gain.shape[0])


def rms_backward(values, gain, grad):
    inverse = inverse_rms(values)
    scaled = grad * gain
    inner = jnp.mean(scaled * values, axis=-1, keepdims=True)
    grad_in = inverse * scaled - values * (inverse * inverse * inverse * inner)
    return grad_in, jnp.sum(grad * values * inverse, axis=0, keepdims=True)


def stack_pair(pair, scale=1.0):
    lanes = lax.broadcasted_iota(jnp.int32, (1, PAIR), 1)
    low = jnp.where(lanes < DH, scale, 0.0).astype(BF16)
    high = jnp.where(lanes < DH, 0.0, scale).astype(BF16)
    return jnp.concatenate([pair * low, pair * high], axis=0)


def join_pair(turned):
    n = turned.shape[1] // 2
    return jnp.concatenate([turned[:DH, :n], turned[DH:, n:]], axis=0).T


def fold(op, parts):
    return functools.reduce(op, parts)


def attend(q2, keys, values, biases):
    scores = [dot_nt(k, q2) + b for k, b in zip(keys, biases)]
    top = fold(jnp.maximum, [jnp.max(s, axis=0, keepdims=True) for s in scores])
    exps = [jnp.exp(s - top) for s in scores]
    total = fold(jnp.add, [jnp.sum(e, axis=0, keepdims=True) for e in exps])
    inv = 1.0 / total
    out = fold(jnp.add, [dot_tn(v, (e * inv).astype(BF16)) for e, v in zip(exps, values)])
    return out, top + jnp.log(total)


def attend_back(q2, do2, lse, keys, values, biases):
    probs = [jnp.exp(dot_nt(k, q2) + b - lse) for k, b in zip(keys, biases)]
    dv = [dot(p.astype(BF16), do2).astype(BF16) for p in probs]
    dp = [dot_nt(v, do2) for v in values]
    row = fold(jnp.add, [jnp.sum(p * g, axis=0, keepdims=True) for p, g in zip(probs, dp)])
    ds = [(p * (g - row)).astype(BF16) for p, g in zip(probs, dp)]
    dq = fold(jnp.add, [dot_tn(k, s) for s, k in zip(ds, keys)])
    dk = [dot(s, q2).astype(BF16) for s in ds]
    return dq, ds, dk, dv


def twice(a):
    return jnp.concatenate([a, a], axis=1)


def self_hidden(length, size):
    keys = lax.broadcasted_iota(jnp.int32, (size, size), 0)
    queries = lax.broadcasted_iota(jnp.int32, (size, size), 1)
    return jnp.where((keys <= queries) & (keys < length), 0.0, MASKED)


def cross_hidden(length, core, size, half):
    out = []
    for part in (core, 1 - core):
        pos = lax.broadcasted_iota(jnp.int32, (half, size), 0) + part * half
        out.append(twice(jnp.where(pos < length, 0.0, MASKED)))
    return out


def table_lines(table):
    lanes = lax.broadcasted_iota(jnp.int32, (1, 128), 1)
    lines = []
    for head in range(table.shape[0]):
        line = jnp.zeros((1, 128), F32)
        for b in range(NB):
            line = jnp.where(lanes == b, table[head, b], line)
        lines.append(line)
    return lines


def pair_bias(lines, index, pair, hidden):
    cols = []
    for head in (2 * pair, 2 * pair + 1):
        line = jnp.broadcast_to(lines[head], index.shape)
        cols.append(jnp.take_along_axis(line, index, axis=1, mode="promise_in_bounds") + hidden)
    return jnp.concatenate(cols, axis=1)


def self_forward(lens, table, x, gain, wq, wk, wv, wo, buckets, h_o, q_o, k_o, v_o, o_o, lse_o, part_o):
    docs, size = buckets.shape[0], buckets.shape[1]
    xf = x[...].astype(F32)
    h = (xf * inverse_rms(xf) * row_of(gain)).astype(BF16)
    h_o[...] = h
    q_o[...] = dot(h, wq[...]).astype(BF16)
    k_o[...] = dot(h, wk[...]).astype(BF16)
    v_o[...] = dot(h, wv[...]).astype(BF16)
    lines = table_lines(table)
    pairs = wq.shape[1] // PAIR
    for d in range(docs):
        rows = slice(d * size, (d + 1) * size)
        hidden = self_hidden(lens[d], size)
        index = buckets[d].T
        for p in range(pairs):
            cols = slice(p * PAIR, (p + 1) * PAIR)
            q2 = stack_pair(q_o[rows, cols], SCALE)
            bias = pair_bias(lines, index, p, hidden)
            out, lse = attend(q2, [k_o[rows, cols]], [v_o[rows, cols]], [bias])
            o_o[rows, cols] = join_pair(out).astype(BF16)
            at = d * pairs + p
            lse_o[at : at + 1, :] = lse
    part_o[...] = dot(o_o[...], wo[...]).astype(BF16)


def plus_parts(own, oth):
    return own[...].astype(F32) + oth[...].astype(F32)


def project_kv(e, wk, wv, kv_o):
    n = wk.shape[1]
    kv_o[0, :, :n] = dot(e[0], wk[...]).astype(BF16)
    kv_o[0, :, n:] = dot(e[0], wv[...]).astype(BF16)


def cross_forward(meta, lens, x, p_own, p_oth, gain, wq, wo, kv_own, kv_oth, x1_o, h_o, q_o, o_o, lse_o, part_o):
    docs, half, n = kv_own.shape[0], kv_own.shape[1], wq.shape[1]
    size = x.shape[0] // docs
    x1 = x[...].astype(F32) + plus_parts(p_own, p_oth)
    x1_o[...] = x1
    h = (x1 * inverse_rms(x1) * row_of(gain)).astype(BF16)
    h_o[...] = h
    q = dot(h, wq[...]).astype(BF16)
    q_o[...] = q
    pairs = range(n // PAIR)
    cols = [slice(p * PAIR, (p + 1) * PAIR) for p in pairs]
    vals = [slice(n + p * PAIR, n + (p + 1) * PAIR) for p in pairs]
    for d in range(docs):
        rows = slice(d * size, (d + 1) * size)
        hidden = cross_hidden(lens[d], meta[2], size, half)
        q2 = [stack_pair(q[rows, c], SCALE) for c in cols]
        scores = [[dot_nt(kv[d, :, c], q2[p]) + m for kv, m in zip((kv_own, kv_oth), hidden)] for p, c in enumerate(cols)]
        tops = [fold(jnp.maximum, [jnp.max(s, axis=0, keepdims=True) for s in scores[p]]) for p in pairs]
        exps = [[jnp.exp(s - tops[p]) for s in scores[p]] for p in pairs]
        totals = [fold(jnp.add, [jnp.sum(e, axis=0, keepdims=True) for e in exps[p]]) for p in pairs]
        out = []
        for p in pairs:
            inv = 1.0 / totals[p]
            turned = fold(
                jnp.add,
                [dot_tn(kv[d, :, vals[p]], (e * inv).astype(BF16)) for kv, e in zip((kv_own, kv_oth), exps[p])],
            )
            out.append(join_pair(turned).astype(BF16))
            lse_o[d, p : p + 1, :] = tops[p] + jnp.log(totals[p])
        o = jnp.concatenate(out, axis=1)
        o_o[rows, :] = o
        part_o[rows, :] = dot(o, wo[...]).astype(BF16)


GELU_C = 0.7978845608028654
GELU_A = 0.044715


def grid_slot(i):
    return jnp.where(i < 2, 2 * i + 1, 2 * (i - 2))


def ffn_act_grad(meta, dy, wout, dz_o):
    dz_o[0] = dot_nt(dy[...], wout[...])


def ffn_forward(meta, x1, p_own, p_oth, gain, win, dz, x2_o, z_send, z_keep, du_send, du_keep, part_o):
    x2 = x1[...] + plus_parts(p_own, p_oth)
    x2_o[...] = x2
    h = (x2 * inverse_rms(x2) * row_of(gain)).astype(BF16)
    half = h.shape[1] // 2
    du_send[2] = h[:, :half]
    du_send[3] = h[:, half:]
    block = win.shape[1] // 4
    total = 0.0
    for s in (1, 3, 0, 2):
        w = win[:, pl.ds(pl.multiple_of((meta[0] ^ s) * block, 128), block)]
        u = dot(h, w)
        u2 = u * u
        t = jnp.tanh(GELU_C * (u + GELU_A * (u * u2)))
        g = 0.5 * (1.0 + t)
        slope = g + (0.5 * GELU_C) * u * (1.0 - t * t) * (1.0 + 3.0 * GELU_A * u2)
        z = (u * g).astype(BF16)
        du = (dz[s] * slope).astype(BF16)
        z_slot = meta[0] ^ s ^ meta[3]

        @pl.when((z_slot & 1) == 1)
        def _(z=z, z_slot=z_slot):
            z_send[z_slot >> 1] = z

        @pl.when((z_slot & 1) == 0)
        def _(z=z, z_slot=z_slot):
            z_keep[z_slot >> 1] = z

        (du_send if s % 2 else du_keep)[s // 2] = du
        total = total + dot_nt(du, w)
    part_o[...] = total.astype(BF16)


def ffn_out_grads(meta, keep, got, dy, dy_got, keep_o, send_o):
    half = dy.shape[1] // 2
    for j, out in enumerate((keep_o, send_o)):
        w = (dot_tn(keep[j], dy[...]) + dot_tn(got[j], dy_got[...])).astype(BF16)
        r = w.shape[0] // 4
        for az in range(4):
            for k in range(2):
                out[meta[1] ^ az, k * r : (k + 1) * r] = w[az * r : (az + 1) * r, k * half : (k + 1) * half]


def ffn_in_grads(meta, keep, send, got, keep_o, send_o):
    for j, out in enumerate((keep_o, send_o)):
        for k in range(2):
            w = (dot_tn(send[2 + k], keep[j]) + dot_tn(got[2 + k], got[j])).astype(BF16)
            r = w.shape[0] // 2
            for az in range(2):
                out[meta[1] ^ (2 * k + az)] = w[az * r : (az + 1) * r]


def ffn_branch(meta, send, keep, wout, part_o, total):
    i = pl.program_id(0)
    branch = dot(jnp.where(i < 2, send[0], keep[0]), wout[...])

    @pl.when(i == 0)
    def _():
        total[...] = branch

    @pl.when((i > 0) & (i < 3))
    def _():
        total[...] += branch

    @pl.when(i == 3)
    def _():
        part_o[...] = (total[...] + branch).astype(BF16)


def finish_output(x2, p_own, p_oth, y_o):
    y_o[...] = (x2[...] + (p_own[...].astype(F32) + p_oth[...].astype(F32))).astype(BF16)


def cross_backward(meta, lens, x2, p_own, p_oth, gain, dy, wo, wq, q, lse, kv_own, kv_oth, gain_o, dx2_o, dc_o, dq_o, part_o, dkv_own, dkv_oth, dy_o):
    docs, half, n = kv_own.shape[0], kv_own.shape[1], q.shape[1]
    size = x2.shape[0] // docs
    dv, gain_grad = rms_backward(x2[...], row_of(gain), plus_parts(p_own, p_oth))
    gain_o[...] = gain_grad
    dy_o[...] = dy[...]
    dx2 = dy[...].astype(F32) + dv
    dx2_o[...] = dx2
    dc = dx2.astype(BF16)
    dc_o[...] = dc
    do = dot_nt(dc, wo[...]).astype(BF16)
    pairs = range(n // PAIR)
    cols = [slice(p * PAIR, (p + 1) * PAIR) for p in pairs]
    vals = [slice(n + p * PAIR, n + (p + 1) * PAIR) for p in pairs]
    both = ((kv_own, dkv_own), (kv_oth, dkv_oth))
    for d in range(docs):
        rows = slice(d * size, (d + 1) * size)
        hidden = cross_hidden(lens[d], meta[2], size, half)
        q2 = [stack_pair(q[rows, c], SCALE) for c in cols]
        do2 = [stack_pair(do[rows, c]) for c in cols]
        probs = [
            [jnp.exp(dot_nt(kv[d, :, cols[p]], q2[p]) + m - lse[d, p : p + 1, :]) for (kv, _), m in zip(both, hidden)]
            for p in pairs
        ]
        dp = [[dot_nt(kv[d, :, vals[p]], do2[p]) for kv, _ in both] for p in pairs]
        row = [fold(jnp.add, [jnp.sum(a * g, axis=0, keepdims=True) for a, g in zip(probs[p], dp[p])]) for p in pairs]
        ds = [[(a * (g - row[p])).astype(BF16) for a, g in zip(probs[p], dp[p])] for p in pairs]
        out = []
        for p in pairs:
            for (_, to), a, s in zip(both, probs[p], ds[p]):
                to[d, :, vals[p]] = dot(a.astype(BF16), do2[p]).astype(BF16)
                to[d, :, cols[p]] = dot(s, q2[p]).astype(BF16)
            dq = fold(jnp.add, [dot_tn(kv[d, :, cols[p]], s) for (kv, _), s in zip(both, ds[p])])
            out.append((join_pair(dq) * SCALE).astype(BF16))
        dq = jnp.concatenate(out, axis=1)
        dq_o[rows, :] = dq
        part_o[rows, :] = dot_nt(dq, wq[...]).astype(BF16)


def store_tensors(tensors, zq, scratch):
    for t, quarters in enumerate(tensors):
        for az, quarter in enumerate(quarters):
            scratch[t, zq ^ az] = quarter.astype(BF16)


def tall(a):
    r = a.shape[0] // 4
    return [a[z * r : (z + 1) * r] for z in range(4)]


def wide(a):
    r, c = a.shape[0] // 2, a.shape[1] // 2
    return [a[(z % 2) * r : (z % 2 + 1) * r, (z // 2) * c : (z // 2 + 1) * c] for z in range(4)]


def send_blocks(quad, scratch, keep, send, sem):
    copies = []
    for s in range(4):
        ref = keep if s % 2 == 0 else send
        copies.append(pltpu.make_async_copy(scratch.at[quad ^ s], ref.at[s // 2], sem.at[s]))
    for c in copies:
        c.start()
    for c in copies:
        c.wait()


def cross_grads(meta, h, dq, e_own, e_oth, dkv_own, dkv_oth, dc, o, keep, send, scratch, sem):
    n = dq.shape[1]
    kv = dot_tn(e_own[...], dkv_own[...]) + dot_tn(e_oth[...], dkv_oth[...])
    gq = dot_tn(h[...], dq[...])
    go = dot_tn(o[...], dc[...])
    store_tensors([tall(gq), tall(kv[:, :n]), tall(kv[:, n:]), wide(go)], meta[1], scratch)
    send_blocks(meta[0], scratch, keep, send, sem)


def self_backward(lens, table, x1, dx2, p_own, p_oth, gain, wo, q, k, v, lse, buckets, gain_o, dx1_o, da_o, dqkv_o, ds_o):
    docs, size = buckets.shape[0], buckets.shape[1]
    n = q.shape[1]
    dv, gain_grad = rms_backward(x1[...], row_of(gain), plus_parts(p_own, p_oth))
    gain_o[...] = gain_grad
    dx1 = dx2[...] + dv
    dx1_o[...] = dx1
    da = dx1.astype(BF16)
    da_o[...] = da
    do = dot_nt(da, wo[...]).astype(BF16)
    lines = table_lines(table)
    pairs = n // PAIR
    for d in range(docs):
        rows = slice(d * size, (d + 1) * size)
        hidden = self_hidden(lens[d], size)
        index = buckets[d].T
        for p in range(pairs):
            cols = slice(p * PAIR, (p + 1) * PAIR)
            at = d * pairs + p
            dq, ds, dk, dvv = attend_back(
                stack_pair(q[rows, cols], SCALE),
                stack_pair(do[rows, cols]),
                lse[at : at + 1, :],
                [k[rows, cols]],
                [v[rows, cols]],
                [pair_bias(lines, index, p, hidden)],
            )
            dqkv_o[rows, cols] = (join_pair(dq) * SCALE).astype(BF16)
            dqkv_o[rows, n + p * PAIR : n + (p + 1) * PAIR] = dk[0]
            dqkv_o[rows, 2 * n + p * PAIR : 2 * n + (p + 1) * PAIR] = dvv[0]
            ds_o[p, d] = ds[0]


def self_input(dqkv, wq, wk, wv, part_o):
    n = wq.shape[1]
    part_o[...] = (
        dot_nt(dqkv[:, :n], wq[...])
        + dot_nt(dqkv[:, n : 2 * n], wk[...])
        + dot_nt(dqkv[:, 2 * n :], wv[...])
    ).astype(BF16)


def self_grads(meta, h, dqkv, da, o, keep, send, scratch, sem):
    n = o.shape[1]
    g = dot_tn(h[...], dqkv[...])
    go = dot_tn(o[...], da[...])
    store_tensors([tall(g[:, t * n : (t + 1) * n]) for t in range(3)] + [wide(go)], meta[1], scratch)
    send_blocks(meta[0], scratch, keep, send, sem)


def finish_input(x, p_own, p_oth, gain, dx1, gain_o, dx_o):
    dv, gain_grad = rms_backward(
        x[...].astype(F32), row_of(gain), p_own[...].astype(F32) + p_oth[...].astype(F32)
    )
    gain_o[...] = gain_grad
    dx_o[...] = dx1[...] + dv


def small_grads(buckets, ds, gain1, gain2, gain3, out):
    docs, size = buckets.shape[0], buckets.shape[1]
    pairs = ds.shape[0]
    half = out.shape[1]
    lanes = lax.broadcasted_iota(jnp.int32, (8, 128), 1)
    subs = lax.broadcasted_iota(jnp.int32, (8, 128), 0)
    out[...] = jnp.zeros(out.shape, F32)
    for j, gain in enumerate((gain1, gain2, gain3)):
        for k in range(2):
            out[2 * j + k : 2 * j + k + 1, :] = gain[:, k * half : (k + 1) * half]
    table = jnp.zeros((8, 128), F32)
    index = [twice(buckets[d].T) for d in range(docs)]
    for p in range(pairs):
        for b in range(NB):
            line = fold(
                jnp.add,
                [
                    jnp.sum(jnp.where(index[d] == b, ds[p, d].astype(F32), 0.0), axis=0, keepdims=True)
                    for d in range(docs)
                ],
            )
            for j in range(2):
                total = jnp.sum(line[:, j * size : (j + 1) * size], axis=1, keepdims=True)
                table = jnp.where((subs == 2 * p + j) & (lanes == b), total, table)
    out[8:16, :128] = table


def enc_part(dkv, wk, wv, out):
    n = wk.shape[1]
    out[0] = (dot_nt(dkv[0, :, :n], wk[...]) + dot_nt(dkv[0, :, n:], wv[...])).astype(BF16)


def finish_enc(dkv, wk, wv, got, out):
    n = wk.shape[1]
    own = dot_nt(dkv[0, :, :n], wk[...]) + dot_nt(dkv[0, :, n:], wv[...])
    out[0] = (own + got[0].astype(F32)).astype(BF16)


def add_quads(keep, got, keep_o, send_o):
    keep_o[...] = keep[0] + got[0]
    send_o[...] = keep[1] + got[1]


EXTRA = 16


def add_quads(keep, got, keep_o, send_o):
    keep_o[...] = keep[0] + got[0]
    send_o[...] = keep[1] + got[1]


def add_pieces(keep, got, keep_o, send_o):
    for j in range(2):
        keep_o[j] = keep[2 * j] + got[2 * j]
        send_o[j] = keep[2 * j + 1] + got[2 * j + 1]


def add_pair(keep, got, keep_o, send_o):
    keep_o[...] = keep[0] + got[0]
    send_o[...] = keep[1] + got[1]


def add_shard(keep, got, out):
    out[...] = keep[...] + got[...]


def put_two(a, b, out):
    out[0] = a[...]
    out[1] = b[...]


def join_pieces(meta, own, got, out):
    r = own.shape[1]
    for j in range(2):
        out[pl.ds(pl.multiple_of((meta[1] ^ (2 * j)) * r, r), r), :] = own[j]
        out[pl.ds(pl.multiple_of((meta[1] ^ (2 * j + 1)) * r, r), r), :] = got[j]


def put_blocks(a, b, out):
    r = a.shape[0]
    out[:r] = a[...]
    out[r:] = b[...]


def plus_small(own, got):
    return (own[...].astype(BF16).astype(F32) + got.astype(F32)).astype(BF16)


def self_pieces(keep, got, small, keep_o, send_o):
    r = keep.shape[1]
    for j in range(2):
        keep_o[j] = keep[2 * j] + got[2 * j]
        send_o[j * r : (j + 1) * r] = keep[2 * j + 1] + got[2 * j + 1]
    send_o[2 * r :] = small[...].astype(BF16)


def self_pair(keep, got, small, keep_o, send_o, small_o):
    r = keep.shape[1]
    total = plus_small(small, got[2 * r :])
    small_o[...] = total
    keep_o[...] = keep[0] + got[:r]
    send_o[:r] = keep[1] + got[r : 2 * r]
    send_o[r:] = total


def self_shard(keep, got, small, out, small_o):
    r = keep.shape[0]
    out[...] = keep[...] + got[:r]
    small_o[...] = plus_small(small, got[r:])


def self_join(meta, own, got, small, out):
    join_pieces(meta, own, got, out)
    out[4 * own.shape[1] :] = small[...]


def self_blocks(a, b, small, out):
    r = a.shape[0] - EXTRA
    out[:r] = a[:r]
    out[r : 2 * r] = b[:r]
    out[2 * r :] = plus_small(small, b[r:])


def write_small(own, got, gain1_o, gain2_o, gain3_o, table_o):
    at = got.shape[0] - EXTRA
    total = own[at:, :].astype(F32) + got[at:, :].astype(F32)
    for j, gain in enumerate((gain1_o, gain2_o, gain3_o)):
        gain[...] = jnp.concatenate([total[2 * j : 2 * j + 1], total[2 * j + 1 : 2 * j + 2]], axis=1).reshape(gain.shape)
    heads, buckets = table_o.shape
    table_o[...] = total[8 : 8 + heads, :buckets]


def write_ffn_out(slots, meta, both, *refs):
    out, done, scratch, sem = refs[-4:]
    done[...] = jnp.zeros(done.shape, F32)
    r, c = scratch.shape[1] // 4, scratch.shape[2] // 2
    copies = []
    for i, s in enumerate(slots):
        for z in range(4):
            for j in range(2):
                at = (8 * i + 2 * z + j) * r
                scratch[i, z * r : (z + 1) * r, j * c : (j + 1) * c] = both[at : at + r].astype(F32)
        copies.append(pltpu.make_async_copy(scratch.at[i], out.at[meta[0] ^ s], sem.at[i]))
        copies[-1].start()
    for copy in copies:
        copy.wait()


def write_ffn_in(slots, meta, both, *refs):
    out, done, scratch, sem = refs[-4:]
    done[...] = jnp.zeros(done.shape, F32)
    r, c = scratch.shape[1:]
    copies = []
    for i, s in enumerate(slots):
        scratch[i] = both[i * r : (i + 1) * r].astype(F32)
        cols = pl.ds(pl.multiple_of((meta[0] ^ s) * c, 128), c)
        copies.append(pltpu.make_async_copy(scratch.at[i], out.at[:, cols], sem.at[i]))
        copies[-1].start()
    for copy in copies:
        copy.wait()


def write_attention(slots, meta, both, *refs):
    q_o, k_o, v_o, o_o, done, scratch, sem = refs[-7:]
    done[...] = jnp.zeros(done.shape, F32)
    rows, c = scratch.shape[1:]
    r = rows // 4

    def copy_of(i, t, z):
        src = scratch.at[i, pl.ds(z * r, r)]
        if t < 3:
            return pltpu.make_async_copy(src, (q_o, k_o, v_o)[t].at[pl.ds(z * r, r)], sem.at[i, z])
        to = o_o.at[pl.ds((z % 2) * r, r), pl.ds((z // 2) * c, c)]
        return pltpu.make_async_copy(src, to, sem.at[i, z])

    def each(act):
        for i, s in enumerate(slots):
            for z in range(4):
                act(i, s, z)

    def start(i, s, z):
        at = i * rows + z * r
        scratch[i, z * r : (z + 1) * r] = both[at : at + r].astype(F32)
        for t in range(4):
            pl.when((meta[0] ^ s) == t)(lambda: copy_of(i, t, z).start())

    def wait(i, s, z):
        for t in range(4):
            pl.when((meta[0] ^ s) == t)(lambda: copy_of(i, t, z).wait())

    each(start)
    each(wait)


class Sum:
    def __init__(self, name, dp, masks, meta, keep=None, send=None):
        self.name, self.dp, self.masks, self.meta = name, dp, masks, meta
        self.keep, self.send, self.small = keep, send, None

    def move(self, a, mask, what):
        pairs = [(2 * i + c, 2 * (i ^ mask[c]) + c) for i in range(self.dp) for c in range(2)]
        with jax.named_scope(f"{self.name}_{what}"):
            return lax.ppermute(a, ("top", "mid", "xy", "seq"), pairs)

    def exchange(self, a, k, what):
        self.got = self.move(a, self.masks[k], what)

    def call(self, body, outs, ins, after, **kw):
        name = f"{self.name}_{body.__name__}" if hasattr(body, "__name__") else f"{self.name}_write"
        return kernel(body, name, outs, ins, [after], **{"limit": SUM_LIMIT, **kw})

    def step_a(self):
        self.exchange(self.send, 0, "sum_a")

    def step_b(self, after):
        z, r, c = self.keep.shape[1:]
        self.keep, send = self.call(add_quads, [((z, r, c), BF16)] * 2, [self.keep, self.got], after)
        self.exchange(send, 1, "sum_b")
        return self.keep

    def step_c(self, after, small=None):
        z, r, c = self.keep.shape
        ins, half = [self.keep, self.got], ((2, r, c), BF16)
        self.small = small
        if small is None:
            self.keep, send = self.call(add_pieces, [half] * 2, ins, after)
        else:
            self.keep, send = self.call(self_pieces, [half, ((2 * r + EXTRA, c), BF16)], [*ins, small], after)
        self.exchange(send, 2, "sum_c")
        return self.keep

    def step_d(self, after):
        z, r, c = self.keep.shape
        ins, one = [self.keep, self.got], ((r, c), BF16)
        if self.small is None:
            self.keep, send = self.call(add_pair, [one] * 2, ins, after)
        else:
            self.keep, send, self.small = self.call(
                self_pair,
                [one, ((r + EXTRA, c), BF16), (self.small.shape, BF16)],
                [*ins, self.small],
                after,
            )
        self.exchange(send, 3, "sum_d")
        return self.keep

    def step_e(self, after):
        ins, one = [self.keep, self.got], (self.keep.shape, BF16)
        if self.small is None:
            self.shard = self.call(add_shard, [one], ins, after)[0]
        else:
            self.shard, self.small = self.call(
                self_shard, [one, (self.small.shape, BF16)], [*ins, self.small], after
            )
        step = 16
        while step < self.dp:
            rest = (step, step)
            self.shard = self.shard + self.move(self.shard, rest, "sum_rest")
            if self.small is not None:
                self.small = self.small + self.move(self.small, rest, "sum_rest")
            step *= 2
        self.exchange(self.shard, 3, "gather_d")
        return self.shard

    def hand_small(self, other):
        other.small, self.small = self.small, None

    def step_f(self, after):
        shape = (2,) + self.shard.shape
        self.two = self.call(put_two, [(shape, BF16)], [self.shard, self.got], after)[0]
        self.exchange(self.two, 2, "gather_c")
        return self.two

    def step_g(self, after):
        r, c = self.shard.shape
        ins = [self.meta, self.two, self.got]
        if self.small is None:
            self.block = self.call(join_pieces, [((4 * r, c), BF16)], ins, after, smem=1)[0]
        else:
            self.block = self.call(self_join, [((4 * r + EXTRA, c), BF16)], [*ins, self.small], after, smem=1)[0]
        self.exchange(self.block, 1, "gather_b")
        return self.block

    def step_h(self, after):
        r, c = self.block.shape
        ins = [self.block, self.got]
        if self.small is None:
            self.near = self.call(put_blocks, [((2 * r, c), BF16)], ins, after)[0]
        else:
            self.near = self.call(self_blocks, [((2 * r - EXTRA, c), BF16)], [*ins, self.small], after)[0]
        self.exchange(self.near, 0, "gather_a")
        return self.near

    def write(self, slots, both, into, after):
        body, outs, scratch = self.target
        into = list(into)
        *self.out, done = self.call(
            functools.partial(body, slots),
            [(o, F32) for o in outs] + [((8, 128), F32)],
            [self.meta, both, *into],
            after,
            smem=1,
            in_specs=[VMEM] + [ANY] * len(into),
            out_specs=[ANY] * len(outs) + [VMEM],
            scratch=scratch,
            aliases={2 + i: i for i in range(len(into))},
            limit=30,
            us=0.1,
        )
        return done

    def write1(self, after):
        return self.write((0, 2), self.near, (), after)

    def write2(self, after):
        return self.write((1, 3), self.got, self.out, after)


def shards(
    dec_input,
    enc_states,
    dec_lengths,
    enc_lengths,
    rel_buckets,
    out_grad,
    gain_self,
    gain_cross,
    gain_ffn,
    rel_table,
    self_query,
    self_key,
    self_value,
    self_out,
    cross_query,
    cross_key,
    cross_value,
    cross_out,
    ffn_in,
    ffn_out,
    *,
    dp,
):
    docs, size, width = dec_input.shape
    half = enc_states.shape[1]
    rows = docs * size
    n = self_query.shape[1]
    hidden = ffn_in.shape[1]
    block = hidden // 4
    pairs = n // PAIR
    index, core = lax.axis_index(("top", "mid", "xy")), lax.axis_index("seq")
    bits = [(index >> k) & 1 for k in range(4)]
    one, two = jnp.where(core == 0, bits[0], bits[1]), jnp.where(core == 0, bits[1], bits[0])
    near, far, up, top = (1, 2), (2, 1), (4, 4), (8, 8)
    quad, quad_out = one + 2 * two, bits[2] + 2 * one
    meta = jnp.stack([quad, bits[2] + 2 * bits[3], core, quad_out, two + 2 * bits[3]]).astype(jnp.int32)
    meta_out = meta[3:]

    def swap(a):
        return lax.ppermute(a, "seq", [(0, 1), (1, 0)])

    dec_lengths, enc_lengths, table = pin(dec_lengths, enc_lengths, rel_table.T)
    gain_self, gain_cross, gain_ffn = pin(gain_self, gain_cross, gain_ffn)
    buckets = pin(rel_buckets)[0]
    x = dec_input.reshape(rows, width)
    dy = out_grad.reshape(rows, width)
    fo = Sum("ffn_out", dp, (up, near, far, top), meta_out)
    fi = Sum("ffn_in", dp, (near, far, up, top), meta)
    enc_oth = swap(enc_states)

    tok = (rows, width)
    head = (rows, n)
    kept = "kept"
    h1, q1, k1, v1, o1, lse1, self_part = kernel(
        self_forward,
        "self_forward",
        [(tok, BF16, kept)] + [(head, BF16, kept)] * 4 + [((docs * pairs, 2 * size), F32), (tok, BF16)],
        [dec_lengths, table, *pin(x), gain_self, *pin(self_query, self_key, self_value, self_out), buckets],
        smem=2,
        us=2.7,
    )
    self_part_oth = swap(self_part)
    kv_shape = (docs, half, 2 * n)
    kv_block = step_block((1, half, 2 * n))
    enc_block = step_block((1, half, width))
    w_block = whole((width, n))
    project = dict(grid=(docs,), in_specs=[enc_block, w_block, w_block], out_specs=[kv_block], us=2)
    kv_own, key_near, value_near, query_near, out_near = kernel(
        project_kv,
        "project_own",
        [(kv_shape, BF16)],
        pin(enc_states, cross_key, cross_value),
        [self_part],
        fetch=[cross_key, cross_value, cross_query, cross_out],
        **project,
    )
    kv_oth, ffn_out_near, dy_near = kernel(
        project_kv,
        "project_oth",
        [(kv_shape, BF16)],
        [enc_oth, key_near, value_near],
        [kv_own],
        fetch=[ffn_out, dy],
        **project,
    )
    wide_tok, wide_head, wo_block = whole(tok), whole(head), whole((n, width))
    gain_block = whole((width,))
    lse_shape = (docs, pairs, 2 * size)
    lse_block = step_block((1, pairs, 2 * size))
    head_block = step_block((size, n))
    tok_block = step_block((size, width))
    x1, h2, q2, o2, lse2, cross_part, ffn_in_near = kernel(
        cross_forward,
        "cross_forward",
        [(tok, F32), (tok, BF16, kept), (head, BF16, kept), (head, BF16, kept), (lse_shape, F32), (tok, BF16)],
        [meta, enc_lengths, *pin(x), self_part, self_part_oth, gain_cross, query_near, out_near, kv_own, kv_oth],
        smem=2,
        fetch=[ffn_in],
        us=8,
    )
    cross_part_oth = swap(cross_part)
    group = (2, 4, width // 4, n)
    act = (4, rows, block)
    act_block = pl.BlockSpec((1, rows, block), lambda i, m: (grid_slot(i), 0, 0))
    win_block = pl.BlockSpec((width, block), lambda i, m: (0, m[0] ^ grid_slot(i)))
    wout_block = pl.BlockSpec((block, width), lambda i, m: (m[0] ^ grid_slot(i), 0))
    dz = kernel(
        ffn_act_grad,
        "ffn_act_grad",
        [(act, F32)],
        [meta, dy_near, ffn_out_near],
        [cross_part],
        smem=1,
        grid=(4,),
        in_specs=[wide_tok, wout_block],
        out_specs=[act_block],
        us=2.5,
    )[0]
    pair_act, sent = (2, rows, block), (4, rows, block)
    x2, z_send, z_keep, du_send, du_keep, part = kernel(
        ffn_forward,
        "ffn_forward",
        [(tok, F32), (pair_act, BF16), (pair_act, BF16), (sent, BF16), (pair_act, BF16), (tok, BF16)],
        [meta, x1, cross_part, cross_part_oth, gain_ffn, ffn_in_near, dz],
        smem=1,
        us=8,
    )
    z_got = fo.move(z_send, up, "sum_a")
    du_got = fi.move(du_send, near, "sum_a")
    part_oth = swap(part)
    gain3, dx2, dc, dq2, query_part, dkv_own, dkv_oth, dy_sent = kernel(
        cross_backward,
        "cross_backward",
        [((1, width), F32), (tok, F32), (tok, BF16), (head, BF16), (tok, BF16)] + [(kv_shape, BF16)] * 2 + [(tok, BF16)],
        [meta, enc_lengths, x2, part, part_oth, gain_ffn, dy, cross_out, cross_query, q2, lse2, kv_own, kv_oth],
        smem=2,
        us=10,
    )
    query_part_oth = swap(query_part)
    dy_got = fo.move(dy_sent, up, "tokens")
    piece = group[1:]
    group_scratch = [pltpu.VMEM((4,) + group[1:], BF16), pltpu.SemaphoreType.DMA((4,))]
    enc_rows = (docs * half, width)
    cross = Sum("cross", dp, (near, far, up, top), meta)
    own = Sum("self", dp, (near, far, up, top), meta)

    def run_out_grads(last):
        fo.keep, send = kernel(
            ffn_out_grads, "ffn_out_grads", [(piece, BF16)] * 2, [meta_out, z_keep, z_got, dy, dy_got], [last], smem=1, us=3
        )
        fo.exchange(send, 1, "sum_b")
        return fo.keep

    def run_in_grads(last):
        fi.keep, send = kernel(
            ffn_in_grads, "ffn_in_grads", [(piece, BF16)] * 2, [meta, du_keep, du_send, du_got], [last], smem=1, us=3
        )
        fi.exchange(send, 1, "sum_b")
        return fi.keep

    def run_cross_grads(last):
        cross.keep, cross.send = kernel(
            cross_grads,
            "cross_grads",
            [(group, BF16)] * 2,
            [meta, h2, dq2, enc_states.reshape(enc_rows), enc_oth.reshape(enc_rows)]
            + [dkv_own.reshape(enc_rows), dkv_oth.reshape(enc_rows), dc, o2],
            [last],
            smem=1,
            out_specs=[ANY] * 2,
            scratch=group_scratch,
            us=5,
        )
        cross.step_a()
        return cross.keep

    sems = pltpu.SemaphoreType.DMA
    fo.target = (write_ffn_out, [(4, block, width)], [pltpu.VMEM((2, block, width), F32), sems((2,))])
    fi.target = (write_ffn_in, [ffn_in.shape], [pltpu.VMEM((2, width, block), F32), sems((2,))])
    cross.target = own.target = (
        write_attention,
        [(width, n)] * 3 + [(n, width)],
        [pltpu.VMEM((2, width, n), F32), sems((2, 4))],
    )

    def run_self_backward(last):
        nonlocal gain2, dx1, da, dqkv, ds1
        gain2, dx1, da, dqkv, ds1 = kernel(
            self_backward,
            "self_backward",
            [((1, width), F32), (tok, F32), (tok, BF16), ((rows, 3 * n), BF16), ((pairs, docs, size, 2 * size), BF16)],
            [dec_lengths, table, x1, dx2, query_part, query_part_oth, gain_cross, self_out]
            + [q1, k1, v1, lse1, buckets],
            [last],
            smem=2,
            us=5,
        )
        return ds1

    def run_self_grads(last):
        own.keep, own.send = kernel(
            self_grads,
            "self_grads",
            [(group, BF16)] * 2,
            [meta, h1, dqkv, da, o1],
            [last],
            smem=1,
            out_specs=[ANY] * 2,
            scratch=group_scratch,
            us=2.7,
        )
        own.step_a()
        return own.keep

    def run_self_input(last):
        nonlocal part1, part1_oth
        part1 = kernel(
            self_input, "self_input", [(tok, BF16)], [dqkv, self_query, self_key, self_value], [last], us=0.1
        )[0]
        part1_oth = swap(part1)
        return part1

    def run_enc_part(last):
        nonlocal enc_sent, enc_got
        enc_sent = kernel(
            enc_part,
            "enc_part",
            [((docs, half, width), BF16)],
            [dkv_oth, cross_key, cross_value],
            [last],
            grid=(docs,),
            in_specs=[kv_block, w_block, w_block],
            out_specs=[enc_block],
            us=0.1,
        )[0]
        enc_got = swap(enc_sent)
        return enc_sent

    def run_finish_input(last):
        nonlocal gain1, dx
        gain1, dx = kernel(
            finish_input,
            "finish_input",
            [((1, width), F32), (tok, F32)],
            [x, part1, part1_oth, gain_self, dx1],
            [last],
            us=0.1,
        )
        return dx

    def run_small(last):
        nonlocal small
        small = kernel(
            small_grads,
            "small_grads",
            [((EXTRA, width // 2), F32)],
            [buckets, ds1, gain1, gain2, gain3],
            [last],
            us=0.1,
        )[0]
        return small

    def run_finish_enc(last):
        nonlocal enc_grad
        enc_grad = kernel(
            finish_enc,
            "finish_enc",
            [((docs, half, width), BF16)],
            [dkv_own, cross_key, cross_value, enc_got],
            [last],
            grid=(docs,),
            in_specs=[kv_block, w_block, w_block, enc_block],
            out_specs=[enc_block],
            us=0.1,
        )[0]
        return enc_grad

    def run_branch(last):
        nonlocal branch, branch_oth
        branch = kernel(
            ffn_branch,
            "ffn_branch",
            [(tok, BF16)],
            [meta_out, z_send, z_keep, ffn_out],
            [last],
            smem=1,
            grid=(4,),
            in_specs=[
                pl.BlockSpec((1, rows, block), lambda i, m: (jnp.minimum(i, 1), 0, 0)),
                pl.BlockSpec((1, rows, block), lambda i, m: (jnp.maximum(i - 2, 0), 0, 0)),
                wout_block,
            ],
            out_specs=[wide_tok],
            scratch=[pltpu.VMEM(tok, F32)],
            us=0.1,
        )[0]
        branch_oth = swap(branch)
        return branch

    def run_finish_output(last):
        nonlocal y
        y = kernel(finish_output, "finish_output", [(tok, BF16)], [x2, branch, branch_oth], [last], us=0.1)[0]
        return y

    def run_own_e(last):
        last = own.step_e(last)
        own.hand_small(cross)
        return last

    def run_write_small(last):
        nonlocal totals
        totals = kernel(
            write_small,
            "write_small",
            [((width,), F32, kept)] * 3 + [((n // DH, NB), F32, kept)],
            [cross.near, cross.got],
            [last],
            limit=16,
            us=0.1,
        )
        return totals[-1]

    totals = gain2 = dx1 = da = dqkv = ds1 = part1 = part1_oth = enc_sent = enc_got = None
    gain1 = dx = small = enc_grad = branch = branch_oth = y = None
    steps = (
        (run_in_grads, run_cross_grads, run_self_backward, fi.step_c, run_out_grads, fi.step_d, cross.step_b)
        + (run_branch, fo.step_c, fi.step_e, run_self_grads, cross.step_c, run_self_input, run_finish_output)
        + (fo.step_d, fi.step_f, cross.step_d, own.step_b, run_finish_input, fo.step_e, run_small)
        + (lambda last: own.step_c(last, small), fi.step_g, cross.step_e, fo.step_f, own.step_d, fi.step_h)
        + (cross.step_f, run_own_e, fi.write1, fo.step_g, own.step_f, cross.step_g, fi.write2, run_enc_part)
        + (own.step_g, fo.step_h, cross.step_h, own.step_h, cross.write1, fo.write1, own.write1, run_finish_enc)
        + (fo.write2, run_write_small, cross.write2)
    )
    last = dq2
    for step in steps:
        last = step(last)
    own.write2(last)
    return (
        y.reshape(dec_input.shape),
        dx.reshape(dec_input.shape),
        enc_grad,
        totals[0],
        totals[1],
        totals[2],
        totals[3].T,
        *own.out,
        *cross.out,
        fi.out[0],
        fo.out[0].reshape(ffn_out.shape),
    )


def solution(mesh):
    dp = mesh.shape["dp"]
    split = jax.sharding.Mesh(mesh.devices.reshape(dp // 8, 2, 4, 2), ("top", "mid", "xy", "seq"))
    rows = ("top", "mid", "xy")
    col, row, doc = P(None, "seq"), P("seq", None), P(rows, None, None)
    in_specs = (
        (doc, P(rows, "seq", None), P(rows), P(rows), doc, doc)
        + (P(),) * 3
        + (col,) * 4
        + (row,)
        + (col,) * 3
        + (row, col, row)
    )
    out_specs = (
        (doc, doc, P(rows, "seq", None))
        + (P(),) * 3
        + (col,) * 4
        + (row,)
        + (col,) * 3
        + (row, col, row)
    )
    return jax.shard_map(
        functools.partial(shards, dp=dp),
        mesh=split,
        in_specs=in_specs,
        out_specs=out_specs,
        check_vma=False,
    )
```

```python
import functools

import jax
import jax.numpy as jnp
from jax import lax
from jax.experimental import pallas as pl
from jax.experimental.pallas import tpu as pltpu
from jax.sharding import PartitionSpec as P

DH = 64
NB = 32
PAIR = 2 * DH
SCALE = DH**-0.5
EPSILON = 1e-06
MASKED = -1e30
F32 = jnp.float32
BF16 = jnp.bfloat16
MIB = 1024 * 1024
SUM_LIMIT = 16


def dot(a, b):
    return lax.dot_general(a, b, (((1,), (0,)), ((), ())), preferred_element_type=F32)


def dot_nt(a, b):
    return lax.dot_general(a, b, (((1,), (1,)), ((), ())), preferred_element_type=F32)


def dot_tn(a, b):
    return lax.dot_general(a, b, (((0,), (0,)), ((), ())), preferred_element_type=F32)


VMEM = pl.BlockSpec(memory_space=pltpu.VMEM)
SMEM = pl.BlockSpec(memory_space=pltpu.SMEM)
ANY = pl.BlockSpec(memory_space=pl.ANY)


def kernel(body, name, outs, ins, after=(), smem=0, in_specs=None, out_specs=None, scratch=(), grid=None, limit=30, aliases=None, us=0.5, fetch=()):
    n_in, n_out, n_after, n_fetch = len(ins), len(outs), len(after), len(fetch)

    def wrapped(*refs):
        at = n_in + n_after
        sources, at = refs[at : at + n_fetch], at + n_fetch
        results, at = refs[at : at + n_out], at + n_out
        targets, at = refs[at : at + n_fetch], at + n_fetch
        rest, sems = (refs[at:-1], refs[-1]) if n_fetch else (refs[at:], None)
        copies = [pltpu.make_async_copy(src, to, sems.at[i]) for i, (src, to) in enumerate(zip(sources, targets))]

        def begin():
            for copy in copies:
                copy.start()

        def end():
            for copy in copies:
                copy.wait()

        if copies and grid is not None:
            pl.when(pl.program_id(0) == 0)(begin)
        else:
            begin()
        body(*refs[:n_in], *results, *rest)
        if copies and grid is not None:
            pl.when(pl.program_id(0) == grid[0] - 1)(end)
        else:
            end()

    in_specs = list(in_specs) if in_specs is not None else [VMEM] * (n_in - smem)
    out_specs = list(out_specs) if out_specs is not None else [VMEM] * len(outs)
    in_specs += [ANY] * (n_after + n_fetch)
    out_specs += [ANY] * n_fetch
    scratch = list(scratch) + ([pltpu.SemaphoreType.DMA((n_fetch,))] if n_fetch else [])
    params = pltpu.CompilerParams(vmem_limit_bytes=limit * MIB)
    cost = pl.CostEstimate(flops=int(us * 10e9), bytes_accessed=0, transcendentals=0)
    shapes = [pltpu.HBM(o[0], o[1]) if len(o) > 2 else jax.ShapeDtypeStruct(*o) for o in outs]
    shapes += [pltpu.VMEM(a.shape, a.dtype) for a in fetch]
    if grid is None:
        how = dict(in_specs=[SMEM] * smem + in_specs, out_specs=out_specs, scratch_shapes=scratch)
    else:
        how = dict(
            grid_spec=pltpu.PrefetchScalarGridSpec(
                num_scalar_prefetch=smem, grid=grid, in_specs=in_specs, out_specs=out_specs, scratch_shapes=scratch
            )
        )
    call = pl.pallas_call(
        wrapped,
        name=name,
        out_shape=shapes,
        compiler_params=params,
        cost_estimate=cost,
        input_output_aliases=aliases or {},
        **how,
    )
    return call(*ins, *after, *pin(*fetch))


def pin(*arrays):
    return [pltpu.with_memory_space_constraint(a, pltpu.HBM) for a in arrays]


def whole(shape):
    return pl.BlockSpec(shape, lambda *_: (0,) * len(shape))


def step_block(shape):
    return pl.BlockSpec(shape, lambda i, *_: (i,) + (0,) * (len(shape) - 1))


def inverse_rms(values):
    return lax.rsqrt(jnp.mean(values * values, axis=-1, keepdims=True) + EPSILON)


def row_of(gain):
    return gain[...].reshape(1, gain.shape[0])


def rms_backward(values, gain, grad):
    inverse = inverse_rms(values)
    scaled = grad * gain
    inner = jnp.mean(scaled * values, axis=-1, keepdims=True)
    grad_in = inverse * scaled - values * (inverse * inverse * inverse * inner)
    return grad_in, jnp.sum(grad * values * inverse, axis=0, keepdims=True)


def stack_pair(pair, scale=1.0):
    lanes = lax.broadcasted_iota(jnp.int32, (1, PAIR), 1)
    low = jnp.where(lanes < DH, scale, 0.0).astype(BF16)
    high = jnp.where(lanes < DH, 0.0, scale).astype(BF16)
    return jnp.concatenate([pair * low, pair * high], axis=0)


def join_pair(turned):
    n = turned.shape[1] // 2
    return jnp.concatenate([turned[:DH, :n], turned[DH:, n:]], axis=0).T


def fold(op, parts):
    return functools.reduce(op, parts)


def attend(q2, keys, values, biases):
    scores = [dot_nt(k, q2) + b for k, b in zip(keys, biases)]
    top = fold(jnp.maximum, [jnp.max(s, axis=0, keepdims=True) for s in scores])
    exps = [jnp.exp(s - top) for s in scores]
    total = fold(jnp.add, [jnp.sum(e, axis=0, keepdims=True) for e in exps])
    inv = 1.0 / total
    out = fold(jnp.add, [dot_tn(v, (e * inv).astype(BF16)) for e, v in zip(exps, values)])
    return out, top + jnp.log(total)


def attend_back(q2, do2, lse, keys, values, biases):
    probs = [jnp.exp(dot_nt(k, q2) + b - lse) for k, b in zip(keys, biases)]
    dv = [dot(p.astype(BF16), do2).astype(BF16) for p in probs]
    dp = [dot_nt(v, do2) for v in values]
    row = fold(jnp.add, [jnp.sum(p * g, axis=0, keepdims=True) for p, g in zip(probs, dp)])
    ds = [(p * (g - row)).astype(BF16) for p, g in zip(probs, dp)]
    dq = fold(jnp.add, [dot_tn(k, s) for s, k in zip(ds, keys)])
    dk = [dot(s, q2).astype(BF16) for s in ds]
    return dq, ds, dk, dv


def twice(a):
    return jnp.concatenate([a, a], axis=1)


def self_hidden(length, size):
    keys = lax.broadcasted_iota(jnp.int32, (size, size), 0)
    queries = lax.broadcasted_iota(jnp.int32, (size, size), 1)
    return jnp.where((keys <= queries) & (keys < length), 0.0, MASKED)


def cross_hidden(length, core, size, half):
    out = []
    for part in (core, 1 - core):
        pos = lax.broadcasted_iota(jnp.int32, (half, size), 0) + part * half
        out.append(twice(jnp.where(pos < length, 0.0, MASKED)))
    return out


def table_lines(table):
    lanes = lax.broadcasted_iota(jnp.int32, (1, 128), 1)
    lines = []
    for head in range(table.shape[0]):
        line = jnp.zeros((1, 128), F32)
        for b in range(NB):
            line = jnp.where(lanes == b, table[head, b], line)
        lines.append(line)
    return lines


def pair_bias(lines, index, pair, hidden):
    cols = []
    for head in (2 * pair, 2 * pair + 1):
        line = jnp.broadcast_to(lines[head], index.shape)
        cols.append(jnp.take_along_axis(line, index, axis=1, mode="promise_in_bounds") + hidden)
    return jnp.concatenate(cols, axis=1)


def self_forward(lens, table, x, gain, wq, wk, wv, wo, buckets, h_o, q_o, k_o, v_o, o_o, lse_o, part_o):
    docs, size = buckets.shape[0], buckets.shape[1]
    xf = x[...].astype(F32)
    h = (xf * inverse_rms(xf) * row_of(gain)).astype(BF16)
    h_o[...] = h
    q_o[...] = dot(h, wq[...]).astype(BF16)
    k_o[...] = dot(h, wk[...]).astype(BF16)
    v_o[...] = dot(h, wv[...]).astype(BF16)
    lines = table_lines(table)
    pairs = wq.shape[1] // PAIR
    for d in range(docs):
        rows = slice(d * size, (d + 1) * size)
        hidden = self_hidden(lens[d], size)
        index = buckets[d].T
        for p in range(pairs):
            cols = slice(p * PAIR, (p + 1) * PAIR)
            q2 = stack_pair(q_o[rows, cols], SCALE)
            bias = pair_bias(lines, index, p, hidden)
            out, lse = attend(q2, [k_o[rows, cols]], [v_o[rows, cols]], [bias])
            o_o[rows, cols] = join_pair(out).astype(BF16)
            at = d * pairs + p
            lse_o[at : at + 1, :] = lse
    part_o[...] = dot(o_o[...], wo[...]).astype(BF16)


def plus_parts(own, oth):
    return own[...].astype(F32) + oth[...].astype(F32)


def project_kv(e, wk, wv, kv_o):
    n = wk.shape[1]
    kv_o[0, :, :n] = dot(e[0], wk[...]).astype(BF16)
    kv_o[0, :, n:] = dot(e[0], wv[...]).astype(BF16)


def cross_forward(meta, lens, x, p_own, p_oth, gain, wq, wo, kv_own, kv_oth, x1_o, h_o, q_o, o_o, lse_o, part_o):
    docs, half, n = kv_own.shape[0], kv_own.shape[1], wq.shape[1]
    size = x.shape[0] // docs
    x1 = x[...].astype(F32) + plus_parts(p_own, p_oth)
    x1_o[...] = x1
    h = (x1 * inverse_rms(x1) * row_of(gain)).astype(BF16)
    h_o[...] = h
    q = dot(h, wq[...]).astype(BF16)
    q_o[...] = q
    pairs = range(n // PAIR)
    cols = [slice(p * PAIR, (p + 1) * PAIR) for p in pairs]
    vals = [slice(n + p * PAIR, n + (p + 1) * PAIR) for p in pairs]
    for d in range(docs):
        rows = slice(d * size, (d + 1) * size)
        hidden = cross_hidden(lens[d], meta[2], size, half)
        q2 = [stack_pair(q[rows, c], SCALE) for c in cols]
        scores = [[dot_nt(kv[d, :, c], q2[p]) + m for kv, m in zip((kv_own, kv_oth), hidden)] for p, c in enumerate(cols)]
        tops = [fold(jnp.maximum, [jnp.max(s, axis=0, keepdims=True) for s in scores[p]]) for p in pairs]
        exps = [[jnp.exp(s - tops[p]) for s in scores[p]] for p in pairs]
        totals = [fold(jnp.add, [jnp.sum(e, axis=0, keepdims=True) for e in exps[p]]) for p in pairs]
        out = []
        for p in pairs:
            inv = 1.0 / totals[p]
            turned = fold(
                jnp.add,
                [dot_tn(kv[d, :, vals[p]], (e * inv).astype(BF16)) for kv, e in zip((kv_own, kv_oth), exps[p])],
            )
            out.append(join_pair(turned).astype(BF16))
            lse_o[d, p : p + 1, :] = tops[p] + jnp.log(totals[p])
        o = jnp.concatenate(out, axis=1)
        o_o[rows, :] = o
        part_o[rows, :] = dot(o, wo[...]).astype(BF16)


GELU_C = 0.7978845608028654
GELU_A = 0.044715


def grid_slot(i):
    return jnp.where(i < 2, 2 * i + 1, 2 * (i - 2))


def ffn_act_grad(meta, dy, wout, dz_o):
    dz_o[0] = dot_nt(dy[...], wout[...])


def ffn_forward(meta, x1, p_own, p_oth, gain, win, dz, x2_o, z_send, z_keep, du_send, du_keep, part_o):
    x2 = x1[...] + plus_parts(p_own, p_oth)
    x2_o[...] = x2
    h = (x2 * inverse_rms(x2) * row_of(gain)).astype(BF16)
    half = h.shape[1] // 2
    du_send[2] = h[:, :half]
    du_send[3] = h[:, half:]
    block = win.shape[1] // 4
    order = (1, 3, 0, 2)
    ws = [win[:, pl.ds(pl.multiple_of((meta[0] ^ s) * block, 128), block)] for s in order]
    us = [dot(h, w) for w in ws]
    dus = []
    for s, u in zip(order, us):
        u2 = u * u
        t = jnp.tanh(GELU_C * (u + GELU_A * (u * u2)))
        g = 0.5 * (1.0 + t)
        slope = g + (0.5 * GELU_C) * u * (1.0 - t * t) * (1.0 + 3.0 * GELU_A * u2)
        z = (u * g).astype(BF16)
        dus.append((dz[s] * slope).astype(BF16))
        z_slot = meta[0] ^ s ^ meta[3]

        @pl.when((z_slot & 1) == 1)
        def _(z=z, z_slot=z_slot):
            z_send[z_slot >> 1] = z

        @pl.when((z_slot & 1) == 0)
        def _(z=z, z_slot=z_slot):
            z_keep[z_slot >> 1] = z

        (du_send if s % 2 else du_keep)[s // 2] = dus[-1]
    total = fold(jnp.add, [dot_nt(du, w) for du, w in zip(dus, ws)])
    part_o[...] = total.astype(BF16)


def ffn_out_grads(meta, keep, got, dy, dy_got, keep_o, send_o):
    half = dy.shape[1] // 2
    for j, out in enumerate((keep_o, send_o)):
        w = (dot_tn(keep[j], dy[...]) + dot_tn(got[j], dy_got[...])).astype(BF16)
        r = w.shape[0] // 4
        for az in range(4):
            for k in range(2):
                out[meta[1] ^ az, k * r : (k + 1) * r] = w[az * r : (az + 1) * r, k * half : (k + 1) * half]


def ffn_in_grads(meta, keep, send, got, keep_o, send_o):
    for j, out in enumerate((keep_o, send_o)):
        for k in range(2):
            w = (dot_tn(send[2 + k], keep[j]) + dot_tn(got[2 + k], got[j])).astype(BF16)
            r = w.shape[0] // 2
            for az in range(2):
                out[meta[1] ^ (2 * k + az)] = w[az * r : (az + 1) * r]


def ffn_branch(meta, send, keep, wout, part_o, total):
    i = pl.program_id(0)
    branch = dot(jnp.where(i < 2, send[0], keep[0]), wout[...])

    @pl.when(i == 0)
    def _():
        total[...] = branch

    @pl.when((i > 0) & (i < 3))
    def _():
        total[...] += branch

    @pl.when(i == 3)
    def _():
        part_o[...] = (total[...] + branch).astype(BF16)


def finish_output(x2, p_own, p_oth, y_o):
    y_o[...] = (x2[...] + (p_own[...].astype(F32) + p_oth[...].astype(F32))).astype(BF16)


def cross_backward(meta, lens, x2, p_own, p_oth, gain, dy, wo, wq, q, lse, kv_own, kv_oth, gain_o, dx2_o, dc_o, dq_o, part_o, dkv_own, dkv_oth, dy_o):
    docs, half, n = kv_own.shape[0], kv_own.shape[1], q.shape[1]
    size = x2.shape[0] // docs
    dv, gain_grad = rms_backward(x2[...], row_of(gain), plus_parts(p_own, p_oth))
    gain_o[...] = gain_grad
    dy_o[...] = dy[...]
    dx2 = dy[...].astype(F32) + dv
    dx2_o[...] = dx2
    dc = dx2.astype(BF16)
    dc_o[...] = dc
    do = dot_nt(dc, wo[...]).astype(BF16)
    pairs = range(n // PAIR)
    cols = [slice(p * PAIR, (p + 1) * PAIR) for p in pairs]
    vals = [slice(n + p * PAIR, n + (p + 1) * PAIR) for p in pairs]
    both = ((kv_own, dkv_own), (kv_oth, dkv_oth))
    for d in range(docs):
        rows = slice(d * size, (d + 1) * size)
        hidden = cross_hidden(lens[d], meta[2], size, half)
        q2 = [stack_pair(q[rows, c], SCALE) for c in cols]
        do2 = [stack_pair(do[rows, c]) for c in cols]
        probs = [
            [jnp.exp(dot_nt(kv[d, :, cols[p]], q2[p]) + m - lse[d, p : p + 1, :]) for (kv, _), m in zip(both, hidden)]
            for p in pairs
        ]
        dp = [[dot_nt(kv[d, :, vals[p]], do2[p]) for kv, _ in both] for p in pairs]
        row = [fold(jnp.add, [jnp.sum(a * g, axis=0, keepdims=True) for a, g in zip(probs[p], dp[p])]) for p in pairs]
        ds = [[(a * (g - row[p])).astype(BF16) for a, g in zip(probs[p], dp[p])] for p in pairs]
        out = []
        for p in pairs:
            for (_, to), a, s in zip(both, probs[p], ds[p]):
                to[d, :, vals[p]] = dot(a.astype(BF16), do2[p]).astype(BF16)
                to[d, :, cols[p]] = dot(s, q2[p]).astype(BF16)
            dq = fold(jnp.add, [dot_tn(kv[d, :, cols[p]], s) for (kv, _), s in zip(both, ds[p])])
            out.append((join_pair(dq) * SCALE).astype(BF16))
        dq = jnp.concatenate(out, axis=1)
        dq_o[rows, :] = dq
        part_o[rows, :] = dot_nt(dq, wq[...]).astype(BF16)


def store_tensors(tensors, zq, scratch):
    for t, quarters in enumerate(tensors):
        for az, quarter in enumerate(quarters):
            scratch[t, zq ^ az] = quarter.astype(BF16)


def tall(a):
    r = a.shape[0] // 4
    return [a[z * r : (z + 1) * r] for z in range(4)]


def wide(a):
    r, c = a.shape[0] // 2, a.shape[1] // 2
    return [a[(z % 2) * r : (z % 2 + 1) * r, (z // 2) * c : (z // 2 + 1) * c] for z in range(4)]


def send_blocks(quad, scratch, keep, send, sem):
    copies = []
    for s in range(4):
        ref = keep if s % 2 == 0 else send
        copies.append(pltpu.make_async_copy(scratch.at[quad ^ s], ref.at[s // 2], sem.at[s]))
    for c in copies:
        c.start()
    for c in copies:
        c.wait()


def cross_grads(meta, h, dq, e_own, e_oth, dkv_own, dkv_oth, dc, o, keep, send, scratch, sem):
    n = dq.shape[1]
    kv = dot_tn(e_own[...], dkv_own[...]) + dot_tn(e_oth[...], dkv_oth[...])
    gq = dot_tn(h[...], dq[...])
    go = dot_tn(o[...], dc[...])
    store_tensors([tall(gq), tall(kv[:, :n]), tall(kv[:, n:]), wide(go)], meta[1], scratch)
    send_blocks(meta[0], scratch, keep, send, sem)


def self_backward(lens, table, x1, dx2, p_own, p_oth, gain, wo, q, k, v, lse, buckets, gain_o, dx1_o, da_o, dqkv_o, ds_o):
    docs, size = buckets.shape[0], buckets.shape[1]
    n = q.shape[1]
    dv, gain_grad = rms_backward(x1[...], row_of(gain), plus_parts(p_own, p_oth))
    gain_o[...] = gain_grad
    dx1 = dx2[...] + dv
    dx1_o[...] = dx1
    da = dx1.astype(BF16)
    da_o[...] = da
    do = dot_nt(da, wo[...]).astype(BF16)
    lines = table_lines(table)
    pairs = n // PAIR
    for d in range(docs):
        rows = slice(d * size, (d + 1) * size)
        hidden = self_hidden(lens[d], size)
        index = buckets[d].T
        for p in range(pairs):
            cols = slice(p * PAIR, (p + 1) * PAIR)
            at = d * pairs + p
            dq, ds, dk, dvv = attend_back(
                stack_pair(q[rows, cols], SCALE),
                stack_pair(do[rows, cols]),
                lse[at : at + 1, :],
                [k[rows, cols]],
                [v[rows, cols]],
                [pair_bias(lines, index, p, hidden)],
            )
            dqkv_o[rows, cols] = (join_pair(dq) * SCALE).astype(BF16)
            dqkv_o[rows, n + p * PAIR : n + (p + 1) * PAIR] = dk[0]
            dqkv_o[rows, 2 * n + p * PAIR : 2 * n + (p + 1) * PAIR] = dvv[0]
            ds_o[p, d] = ds[0]


def self_input(dqkv, wq, wk, wv, part_o):
    n = wq.shape[1]
    part_o[...] = (
        dot_nt(dqkv[:, :n], wq[...])
        + dot_nt(dqkv[:, n : 2 * n], wk[...])
        + dot_nt(dqkv[:, 2 * n :], wv[...])
    ).astype(BF16)


def self_grads(meta, h, dqkv, da, o, keep, send, scratch, sem):
    n = o.shape[1]
    g = dot_tn(h[...], dqkv[...])
    go = dot_tn(o[...], da[...])
    store_tensors([tall(g[:, t * n : (t + 1) * n]) for t in range(3)] + [wide(go)], meta[1], scratch)
    send_blocks(meta[0], scratch, keep, send, sem)


def finish_input(x, p_own, p_oth, gain, dx1, gain_o, dx_o):
    dv, gain_grad = rms_backward(
        x[...].astype(F32), row_of(gain), p_own[...].astype(F32) + p_oth[...].astype(F32)
    )
    gain_o[...] = gain_grad
    dx_o[...] = dx1[...] + dv


def small_grads(buckets, ds, gain1, gain2, gain3, out):
    docs, size = buckets.shape[0], buckets.shape[1]
    pairs = ds.shape[0]
    half = out.shape[1]
    lanes = lax.broadcasted_iota(jnp.int32, (8, 128), 1)
    subs = lax.broadcasted_iota(jnp.int32, (8, 128), 0)
    out[...] = jnp.zeros(out.shape, F32)
    for j, gain in enumerate((gain1, gain2, gain3)):
        for k in range(2):
            out[2 * j + k : 2 * j + k + 1, :] = gain[:, k * half : (k + 1) * half]
    table = jnp.zeros((8, 128), F32)
    index = [twice(buckets[d].T) for d in range(docs)]
    for p in range(pairs):
        for b in range(NB):
            line = fold(
                jnp.add,
                [
                    jnp.sum(jnp.where(index[d] == b, ds[p, d].astype(F32), 0.0), axis=0, keepdims=True)
                    for d in range(docs)
                ],
            )
            for j in range(2):
                total = jnp.sum(line[:, j * size : (j + 1) * size], axis=1, keepdims=True)
                table = jnp.where((subs == 2 * p + j) & (lanes == b), total, table)
    out[8:16, :128] = table


def enc_part(dkv, wk, wv, out):
    n = wk.shape[1]
    out[0] = (dot_nt(dkv[0, :, :n], wk[...]) + dot_nt(dkv[0, :, n:], wv[...])).astype(BF16)


def finish_enc(dkv, wk, wv, got, out):
    n = wk.shape[1]
    own = dot_nt(dkv[0, :, :n], wk[...]) + dot_nt(dkv[0, :, n:], wv[...])
    out[0] = (own + got[0].astype(F32)).astype(BF16)


def add_quads(keep, got, keep_o, send_o):
    keep_o[...] = keep[0] + got[0]
    send_o[...] = keep[1] + got[1]


EXTRA = 16


def add_quads(keep, got, keep_o, send_o):
    keep_o[...] = keep[0] + got[0]
    send_o[...] = keep[1] + got[1]


def add_pieces(keep, got, keep_o, send_o):
    for j in range(2):
        keep_o[j] = keep[2 * j] + got[2 * j]
        send_o[j] = keep[2 * j + 1] + got[2 * j + 1]


def add_pair(keep, got, keep_o, send_o):
    keep_o[...] = keep[0] + got[0]
    send_o[...] = keep[1] + got[1]


def add_shard(keep, got, out):
    out[...] = keep[...] + got[...]


def put_two(a, b, out):
    out[0] = a[...]
    out[1] = b[...]


def join_pieces(meta, own, got, out):
    r = own.shape[1]
    for j in range(2):
        out[pl.ds(pl.multiple_of((meta[1] ^ (2 * j)) * r, r), r), :] = own[j]
        out[pl.ds(pl.multiple_of((meta[1] ^ (2 * j + 1)) * r, r), r), :] = got[j]


def put_blocks(a, b, out):
    r = a.shape[0]
    out[:r] = a[...]
    out[r:] = b[...]


def plus_small(own, got):
    return (own[...].astype(BF16).astype(F32) + got.astype(F32)).astype(BF16)


def self_pieces(keep, got, small, keep_o, send_o):
    r = keep.shape[1]
    for j in range(2):
        keep_o[j] = keep[2 * j] + got[2 * j]
        send_o[j * r : (j + 1) * r] = keep[2 * j + 1] + got[2 * j + 1]
    send_o[2 * r :] = small[...].astype(BF16)


def self_pair(keep, got, small, keep_o, send_o, small_o):
    r = keep.shape[1]
    total = plus_small(small, got[2 * r :])
    small_o[...] = total
    keep_o[...] = keep[0] + got[:r]
    send_o[:r] = keep[1] + got[r : 2 * r]
    send_o[r:] = total


def self_shard(keep, got, small, out, small_o):
    r = keep.shape[0]
    out[...] = keep[...] + got[:r]
    small_o[...] = plus_small(small, got[r:])


def self_join(meta, own, got, small, out):
    join_pieces(meta, own, got, out)
    out[4 * own.shape[1] :] = small[...]


def self_blocks(a, b, small, out):
    r = a.shape[0] - EXTRA
    out[:r] = a[:r]
    out[r : 2 * r] = b[:r]
    out[2 * r :] = plus_small(small, b[r:])


def write_small(own, got, gain1_o, gain2_o, gain3_o, table_o):
    at = got.shape[0] - EXTRA
    total = own[at:, :].astype(F32) + got[at:, :].astype(F32)
    for j, gain in enumerate((gain1_o, gain2_o, gain3_o)):
        gain[...] = jnp.concatenate([total[2 * j : 2 * j + 1], total[2 * j + 1 : 2 * j + 2]], axis=1).reshape(gain.shape)
    heads, buckets = table_o.shape
    table_o[...] = total[8 : 8 + heads, :buckets]


def write_ffn_out(slots, meta, both, *refs):
    out, done, scratch, sem = refs[-4:]
    done[...] = jnp.zeros(done.shape, F32)
    r, c = scratch.shape[1] // 4, scratch.shape[2] // 2
    copies = []
    for i, s in enumerate(slots):
        for z in range(4):
            for j in range(2):
                at = (8 * i + 2 * z + j) * r
                scratch[i, z * r : (z + 1) * r, j * c : (j + 1) * c] = both[at : at + r].astype(F32)
        copies.append(pltpu.make_async_copy(scratch.at[i], out.at[meta[0] ^ s], sem.at[i]))
        copies[-1].start()
    for copy in copies:
        copy.wait()


def write_ffn_in(slots, meta, both, *refs):
    out, done, scratch, sem = refs[-4:]
    done[...] = jnp.zeros(done.shape, F32)
    r, c = scratch.shape[1:]
    copies = []
    for i, s in enumerate(slots):
        scratch[i] = both[i * r : (i + 1) * r].astype(F32)
        cols = pl.ds(pl.multiple_of((meta[0] ^ s) * c, 128), c)
        copies.append(pltpu.make_async_copy(scratch.at[i], out.at[:, cols], sem.at[i]))
        copies[-1].start()
    for copy in copies:
        copy.wait()


def write_attention(slots, meta, both, *refs):
    q_o, k_o, v_o, o_o, done, scratch, sem = refs[-7:]
    done[...] = jnp.zeros(done.shape, F32)
    rows, c = scratch.shape[1:]
    r = rows // 4

    def copy_of(i, t, z):
        src = scratch.at[i, pl.ds(z * r, r)]
        if t < 3:
            return pltpu.make_async_copy(src, (q_o, k_o, v_o)[t].at[pl.ds(z * r, r)], sem.at[i, z])
        to = o_o.at[pl.ds((z % 2) * r, r), pl.ds((z // 2) * c, c)]
        return pltpu.make_async_copy(src, to, sem.at[i, z])

    def each(act):
        for i, s in enumerate(slots):
            for z in range(4):
                act(i, s, z)

    def start(i, s, z):
        at = i * rows + z * r
        scratch[i, z * r : (z + 1) * r] = both[at : at + r].astype(F32)
        for t in range(4):
            pl.when((meta[0] ^ s) == t)(lambda: copy_of(i, t, z).start())

    def wait(i, s, z):
        for t in range(4):
            pl.when((meta[0] ^ s) == t)(lambda: copy_of(i, t, z).wait())

    each(start)
    each(wait)


class Sum:
    def __init__(self, name, dp, masks, meta, keep=None, send=None):
        self.name, self.dp, self.masks, self.meta = name, dp, masks, meta
        self.keep, self.send, self.small = keep, send, None

    def move(self, a, mask, what):
        pairs = [(2 * i + c, 2 * (i ^ mask[c]) + c) for i in range(self.dp) for c in range(2)]
        with jax.named_scope(f"{self.name}_{what}"):
            return lax.ppermute(a, ("top", "mid", "xy", "seq"), pairs)

    def exchange(self, a, k, what):
        self.got = self.move(a, self.masks[k], what)

    def call(self, body, outs, ins, after, **kw):
        name = f"{self.name}_{body.__name__}" if hasattr(body, "__name__") else f"{self.name}_write"
        return kernel(body, name, outs, ins, [after], **{"limit": SUM_LIMIT, **kw})

    def step_a(self):
        self.exchange(self.send, 0, "sum_a")

    def step_b(self, after):
        z, r, c = self.keep.shape[1:]
        self.keep, send = self.call(add_quads, [((z, r, c), BF16)] * 2, [self.keep, self.got], after)
        self.exchange(send, 1, "sum_b")
        return self.keep

    def step_c(self, after, small=None):
        z, r, c = self.keep.shape
        ins, half = [self.keep, self.got], ((2, r, c), BF16)
        self.small = small
        if small is None:
            self.keep, send = self.call(add_pieces, [half] * 2, ins, after)
        else:
            self.keep, send = self.call(self_pieces, [half, ((2 * r + EXTRA, c), BF16)], [*ins, small], after)
        self.exchange(send, 2, "sum_c")
        return self.keep

    def step_d(self, after):
        z, r, c = self.keep.shape
        ins, one = [self.keep, self.got], ((r, c), BF16)
        if self.small is None:
            self.keep, send = self.call(add_pair, [one] * 2, ins, after)
        else:
            self.keep, send, self.small = self.call(
                self_pair,
                [one, ((r + EXTRA, c), BF16), (self.small.shape, BF16)],
                [*ins, self.small],
                after,
            )
        self.exchange(send, 3, "sum_d")
        return self.keep

    def step_e(self, after):
        ins, one = [self.keep, self.got], (self.keep.shape, BF16)
        if self.small is None:
            self.shard = self.call(add_shard, [one], ins, after)[0]
        else:
            self.shard, self.small = self.call(
                self_shard, [one, (self.small.shape, BF16)], [*ins, self.small], after
            )
        step = 16
        while step < self.dp:
            rest = (step, step)
            self.shard = self.shard + self.move(self.shard, rest, "sum_rest")
            if self.small is not None:
                self.small = self.small + self.move(self.small, rest, "sum_rest")
            step *= 2
        self.exchange(self.shard, 3, "gather_d")
        return self.shard

    def hand_small(self, other):
        other.small, self.small = self.small, None

    def step_f(self, after):
        shape = (2,) + self.shard.shape
        self.two = self.call(put_two, [(shape, BF16)], [self.shard, self.got], after)[0]
        self.exchange(self.two, 2, "gather_c")
        return self.two

    def step_g(self, after):
        r, c = self.shard.shape
        ins = [self.meta, self.two, self.got]
        if self.small is None:
            self.block = self.call(join_pieces, [((4 * r, c), BF16)], ins, after, smem=1)[0]
        else:
            self.block = self.call(self_join, [((4 * r + EXTRA, c), BF16)], [*ins, self.small], after, smem=1)[0]
        self.exchange(self.block, 1, "gather_b")
        return self.block

    def step_h(self, after):
        r, c = self.block.shape
        ins = [self.block, self.got]
        if self.small is None:
            self.near = self.call(put_blocks, [((2 * r, c), BF16)], ins, after)[0]
        else:
            self.near = self.call(self_blocks, [((2 * r - EXTRA, c), BF16)], [*ins, self.small], after)[0]
        self.exchange(self.near, 0, "gather_a")
        return self.near

    def write(self, slots, both, into, after):
        body, outs, scratch = self.target
        into = list(into)
        *self.out, done = self.call(
            functools.partial(body, slots),
            [(o, F32) for o in outs] + [((8, 128), F32)],
            [self.meta, both, *into],
            after,
            smem=1,
            in_specs=[VMEM] + [ANY] * len(into),
            out_specs=[ANY] * len(outs) + [VMEM],
            scratch=scratch,
            aliases={2 + i: i for i in range(len(into))},
            limit=30,
            us=0.1,
        )
        return done

    def write1(self, after):
        return self.write((0, 2), self.near, (), after)

    def write2(self, after):
        return self.write((1, 3), self.got, self.out, after)


def shards(
    dec_input,
    enc_states,
    dec_lengths,
    enc_lengths,
    rel_buckets,
    out_grad,
    gain_self,
    gain_cross,
    gain_ffn,
    rel_table,
    self_query,
    self_key,
    self_value,
    self_out,
    cross_query,
    cross_key,
    cross_value,
    cross_out,
    ffn_in,
    ffn_out,
    *,
    dp,
):
    docs, size, width = dec_input.shape
    half = enc_states.shape[1]
    rows = docs * size
    n = self_query.shape[1]
    hidden = ffn_in.shape[1]
    block = hidden // 4
    pairs = n // PAIR
    index, core = lax.axis_index(("top", "mid", "xy")), lax.axis_index("seq")
    bits = [(index >> k) & 1 for k in range(4)]
    one, two = jnp.where(core == 0, bits[0], bits[1]), jnp.where(core == 0, bits[1], bits[0])
    near, far, up, top = (1, 2), (2, 1), (4, 4), (8, 8)
    quad, quad_out = one + 2 * two, bits[2] + 2 * one
    meta = jnp.stack([quad, bits[2] + 2 * bits[3], core, quad_out, two + 2 * bits[3]]).astype(jnp.int32)
    meta_out = meta[3:]

    def swap(a):
        return lax.ppermute(a, "seq", [(0, 1), (1, 0)])

    dec_lengths, enc_lengths, table = pin(dec_lengths, enc_lengths, rel_table.T)
    gain_self, gain_cross, gain_ffn = pin(gain_self, gain_cross, gain_ffn)
    buckets = pin(rel_buckets)[0]
    x = dec_input.reshape(rows, width)
    dy = out_grad.reshape(rows, width)
    fo = Sum("ffn_out", dp, (up, near, far, top), meta_out)
    fi = Sum("ffn_in", dp, (near, far, up, top), meta)
    enc_oth = swap(enc_states)

    tok = (rows, width)
    head = (rows, n)
    kept = "kept"
    h1, q1, k1, v1, o1, lse1, self_part = kernel(
        self_forward,
        "self_forward",
        [(tok, BF16, kept)] + [(head, BF16, kept)] * 4 + [((docs * pairs, 2 * size), F32), (tok, BF16)],
        [dec_lengths, table, *pin(x), gain_self, *pin(self_query, self_key, self_value, self_out), buckets],
        smem=2,
        us=2.7,
    )
    self_part_oth = swap(self_part)
    kv_shape = (docs, half, 2 * n)
    kv_block = step_block((1, half, 2 * n))
    enc_block = step_block((1, half, width))
    w_block = whole((width, n))
    project = dict(grid=(docs,), in_specs=[enc_block, w_block, w_block], out_specs=[kv_block], us=2)
    kv_own, key_near, value_near, query_near, out_near = kernel(
        project_kv,
        "project_own",
        [(kv_shape, BF16)],
        pin(enc_states, cross_key, cross_value),
        [self_part],
        fetch=[cross_key, cross_value, cross_query, cross_out],
        **project,
    )
    kv_oth, ffn_out_near, dy_near = kernel(
        project_kv,
        "project_oth",
        [(kv_shape, BF16)],
        [enc_oth, key_near, value_near],
        [kv_own],
        fetch=[ffn_out, dy],
        **project,
    )
    wide_tok, wide_head, wo_block = whole(tok), whole(head), whole((n, width))
    gain_block = whole((width,))
    lse_shape = (docs, pairs, 2 * size)
    lse_block = step_block((1, pairs, 2 * size))
    head_block = step_block((size, n))
    tok_block = step_block((size, width))
    x1, h2, q2, o2, lse2, cross_part, ffn_in_near = kernel(
        cross_forward,
        "cross_forward",
        [(tok, F32), (tok, BF16, kept), (head, BF16, kept), (head, BF16, kept), (lse_shape, F32), (tok, BF16)],
        [meta, enc_lengths, *pin(x), self_part, self_part_oth, gain_cross, query_near, out_near, kv_own, kv_oth],
        smem=2,
        fetch=[ffn_in],
        us=8,
    )
    cross_part_oth = swap(cross_part)
    group = (2, 4, width // 4, n)
    act = (4, rows, block)
    act_block = pl.BlockSpec((1, rows, block), lambda i, m: (grid_slot(i), 0, 0))
    win_block = pl.BlockSpec((width, block), lambda i, m: (0, m[0] ^ grid_slot(i)))
    wout_block = pl.BlockSpec((block, width), lambda i, m: (m[0] ^ grid_slot(i), 0))
    dz = kernel(
        ffn_act_grad,
        "ffn_act_grad",
        [(act, F32)],
        [meta, dy_near, ffn_out_near],
        [cross_part],
        smem=1,
        grid=(4,),
        in_specs=[wide_tok, wout_block],
        out_specs=[act_block],
        us=2.5,
    )[0]
    pair_act, sent = (2, rows, block), (4, rows, block)
    x2, z_send, z_keep, du_send, du_keep, part = kernel(
        ffn_forward,
        "ffn_forward",
        [(tok, F32), (pair_act, BF16), (pair_act, BF16), (sent, BF16), (pair_act, BF16), (tok, BF16)],
        [meta, x1, cross_part, cross_part_oth, gain_ffn, ffn_in_near, dz],
        smem=1,
        us=8,
    )
    z_got = fo.move(z_send, up, "sum_a")
    du_got = fi.move(du_send, near, "sum_a")
    part_oth = swap(part)
    gain3, dx2, dc, dq2, query_part, dkv_own, dkv_oth, dy_sent = kernel(
        cross_backward,
        "cross_backward",
        [((1, width), F32), (tok, F32), (tok, BF16), (head, BF16), (tok, BF16)] + [(kv_shape, BF16)] * 2 + [(tok, BF16)],
        [meta, enc_lengths, x2, part, part_oth, gain_ffn, dy, cross_out, cross_query, q2, lse2, kv_own, kv_oth],
        smem=2,
        us=10,
    )
    query_part_oth = swap(query_part)
    dy_got = fo.move(dy_sent, up, "tokens")
    piece = group[1:]
    group_scratch = [pltpu.VMEM((4,) + group[1:], BF16), pltpu.SemaphoreType.DMA((4,))]
    enc_rows = (docs * half, width)
    cross = Sum("cross", dp, (near, far, up, top), meta)
    own = Sum("self", dp, (near, far, up, top), meta)

    def run_out_grads(last):
        fo.keep, send = kernel(
            ffn_out_grads, "ffn_out_grads", [(piece, BF16)] * 2, [meta_out, z_keep, z_got, dy, dy_got], [last], smem=1, us=3
        )
        fo.exchange(send, 1, "sum_b")
        return fo.keep

    def run_in_grads(last):
        fi.keep, send = kernel(
            ffn_in_grads, "ffn_in_grads", [(piece, BF16)] * 2, [meta, du_keep, du_send, du_got], [last], smem=1, us=3
        )
        fi.exchange(send, 1, "sum_b")
        return fi.keep

    def run_cross_grads(last):
        cross.keep, cross.send = kernel(
            cross_grads,
            "cross_grads",
            [(group, BF16)] * 2,
            [meta, h2, dq2, enc_states.reshape(enc_rows), enc_oth.reshape(enc_rows)]
            + [dkv_own.reshape(enc_rows), dkv_oth.reshape(enc_rows), dc, o2],
            [last],
            smem=1,
            out_specs=[ANY] * 2,
            scratch=group_scratch,
            us=5,
        )
        cross.step_a()
        return cross.keep

    sems = pltpu.SemaphoreType.DMA
    fo.target = (write_ffn_out, [(4, block, width)], [pltpu.VMEM((2, block, width), F32), sems((2,))])
    fi.target = (write_ffn_in, [ffn_in.shape], [pltpu.VMEM((2, width, block), F32), sems((2,))])
    cross.target = own.target = (
        write_attention,
        [(width, n)] * 3 + [(n, width)],
        [pltpu.VMEM((2, width, n), F32), sems((2, 4))],
    )

    def run_self_backward(last):
        nonlocal gain2, dx1, da, dqkv, ds1
        gain2, dx1, da, dqkv, ds1 = kernel(
            self_backward,
            "self_backward",
            [((1, width), F32), (tok, F32), (tok, BF16), ((rows, 3 * n), BF16), ((pairs, docs, size, 2 * size), BF16)],
            [dec_lengths, table, x1, dx2, query_part, query_part_oth, gain_cross, self_out]
            + [q1, k1, v1, lse1, buckets],
            [last],
            smem=2,
            us=5,
        )
        return ds1

    def run_self_grads(last):
        own.keep, own.send = kernel(
            self_grads,
            "self_grads",
            [(group, BF16)] * 2,
            [meta, h1, dqkv, da, o1],
            [last],
            smem=1,
            out_specs=[ANY] * 2,
            scratch=group_scratch,
            us=2.7,
        )
        own.step_a()
        return own.keep

    def run_self_input(last):
        nonlocal part1, part1_oth
        part1 = kernel(
            self_input, "self_input", [(tok, BF16)], [dqkv, self_query, self_key, self_value], [last], us=0.1
        )[0]
        part1_oth = swap(part1)
        return part1

    def run_enc_part(last):
        nonlocal enc_sent, enc_got
        enc_sent = kernel(
            enc_part,
            "enc_part",
            [((docs, half, width), BF16)],
            [dkv_oth, cross_key, cross_value],
            [last],
            grid=(docs,),
            in_specs=[kv_block, w_block, w_block],
            out_specs=[enc_block],
            us=0.1,
        )[0]
        enc_got = swap(enc_sent)
        return enc_sent

    def run_finish_input(last):
        nonlocal gain1, dx
        gain1, dx = kernel(
            finish_input,
            "finish_input",
            [((1, width), F32), (tok, F32)],
            [x, part1, part1_oth, gain_self, dx1],
            [last],
            us=0.1,
        )
        return dx

    def run_small(last):
        nonlocal small
        small = kernel(
            small_grads,
            "small_grads",
            [((EXTRA, width // 2), F32)],
            [buckets, ds1, gain1, gain2, gain3],
            [last],
            us=0.1,
        )[0]
        return small

    def run_finish_enc(last):
        nonlocal enc_grad
        enc_grad = kernel(
            finish_enc,
            "finish_enc",
            [((docs, half, width), BF16)],
            [dkv_own, cross_key, cross_value, enc_got],
            [last],
            grid=(docs,),
            in_specs=[kv_block, w_block, w_block, enc_block],
            out_specs=[enc_block],
            us=0.1,
        )[0]
        return enc_grad

    def run_branch(last):
        nonlocal branch, branch_oth
        branch = kernel(
            ffn_branch,
            "ffn_branch",
            [(tok, BF16)],
            [meta_out, z_send, z_keep, ffn_out],
            [last],
            smem=1,
            grid=(4,),
            in_specs=[
                pl.BlockSpec((1, rows, block), lambda i, m: (jnp.minimum(i, 1), 0, 0)),
                pl.BlockSpec((1, rows, block), lambda i, m: (jnp.maximum(i - 2, 0), 0, 0)),
                wout_block,
            ],
            out_specs=[wide_tok],
            scratch=[pltpu.VMEM(tok, F32)],
            us=0.1,
        )[0]
        branch_oth = swap(branch)
        return branch

    def run_finish_output(last):
        nonlocal y
        y = kernel(finish_output, "finish_output", [(tok, BF16)], [x2, branch, branch_oth], [last], us=0.1)[0]
        return y

    def run_own_e(last):
        last = own.step_e(last)
        own.hand_small(cross)
        return last

    def run_write_small(last):
        nonlocal totals
        totals = kernel(
            write_small,
            "write_small",
            [((width,), F32, kept)] * 3 + [((n // DH, NB), F32, kept)],
            [cross.near, cross.got],
            [last],
            limit=16,
            us=0.1,
        )
        return totals[-1]

    totals = gain2 = dx1 = da = dqkv = ds1 = part1 = part1_oth = enc_sent = enc_got = None
    gain1 = dx = small = enc_grad = branch = branch_oth = y = None
    steps = (
        (run_in_grads, run_cross_grads, run_self_backward, fi.step_c, run_out_grads, fi.step_d, cross.step_b)
        + (run_branch, fo.step_c, fi.step_e, run_self_grads, cross.step_c, run_self_input, run_finish_output)
        + (fo.step_d, fi.step_f, cross.step_d, own.step_b, run_finish_input, fo.step_e, run_small)
        + (lambda last: own.step_c(last, small), fi.step_g, cross.step_e, fo.step_f, own.step_d, fi.step_h)
        + (cross.step_f, run_own_e, fi.write1, fo.step_g, own.step_f, cross.step_g, fi.write2, run_enc_part)
        + (own.step_g, fo.step_h, cross.step_h, own.step_h, cross.write1, fo.write1, own.write1, run_finish_enc)
        + (fo.write2, run_write_small, cross.write2)
    )
    last = dq2
    for step in steps:
        last = step(last)
    own.write2(last)
    return (
        y.reshape(dec_input.shape),
        dx.reshape(dec_input.shape),
        enc_grad,
        totals[0],
        totals[1],
        totals[2],
        totals[3].T,
        *own.out,
        *cross.out,
        fi.out[0],
        fo.out[0].reshape(ffn_out.shape),
    )


def solution(mesh):
    dp = mesh.shape["dp"]
    split = jax.sharding.Mesh(mesh.devices.reshape(dp // 8, 2, 4, 2), ("top", "mid", "xy", "seq"))
    rows = ("top", "mid", "xy")
    col, row, doc = P(None, "seq"), P("seq", None), P(rows, None, None)
    in_specs = (
        (doc, P(rows, "seq", None), P(rows), P(rows), doc, doc)
        + (P(),) * 3
        + (col,) * 4
        + (row,)
        + (col,) * 3
        + (row, col, row)
    )
    out_specs = (
        (doc, doc, P(rows, "seq", None))
        + (P(),) * 3
        + (col,) * 4
        + (row,)
        + (col,) * 3
        + (row, col, row)
    )
    return jax.shard_map(
        functools.partial(shards, dp=dp),
        mesh=split,
        in_specs=in_specs,
        out_specs=out_specs,
        check_vma=False,
    )
```
